32 devices in a mesh: dp: 4 (over x, core), ctx: 8 (over z, y).
Axes of the slice: x: 2, y: 2, z: 4, core: 2. Of those that a mesh axis runs over, the one named last changes fastest.
Arguments:
- queries: bfloat16 [4, 256, 2048], P('dp', 'ctx'), may hold values from -8 to 8
- keys: bfloat16 [4, 256, 512], P('dp', 'ctx'), may hold values from -8 to 8
- values: bfloat16 [4, 256, 512], P('dp', 'ctx'), may hold values from -6 to 6
- out_grad: bfloat16 [4, 256, 2048], P('dp', 'ctx'), may hold values from -6 to 6
- routed_inputs: bfloat16 [4, 256, 4096], P('dp', 'ctx'), may hold values from -6 to 6
- router_weight: float32 [4096], replicated, may hold values from -0.09375 to 0.09375
- positions: int32 [4, 256], P('dp', 'ctx'), may hold values from 0 to 2047, as said below
Outputs:
- query_grad: bfloat16 [4, 256, 2048], P('dp', 'ctx')
- key_grad: bfloat16 [4, 256, 512], P('dp', 'ctx')
- value_grad: bfloat16 [4, 256, 512], P('dp', 'ctx')
- router_grad: float32 [4096], replicated
The draws below stay inside these ranges and needn't reach their ends.
Inputs may be any that keep to these rules, and one draw needn't show every extreme that they name: `positions`: within each sequence strictly increasing, the first 0 and the last 2047.
All inputs are finite; a program needn't handle non-finite values.
Results may differ from the reference program's by a relative error of at most 0.039.
Values may be sent and summed in bfloat16 or wider, within the bound.
No kernel may reach another device: no remote copies, remote signals or barrier semaphores. Data moves between devices by JAX's collectives and lax.ppermute only.
A program may use at most 128 MiB of HBM per device.

```python
import math
import jax
import jax.numpy as jnp
from jax import lax

D = 4096
HQ = 16
KVH = 4
HD = 128
SEQS = 4
SEL = 256
CTX = 2048


def draw_queries(key, part):
    key = jax.random.fold_in(key, 1)
    full_shape = (SEQS, SEL, HQ * HD)
    result = jnp.clip(jax.random.normal(key, full_shape, jnp.float32), -6.0, 6.0)
    return result.astype(jnp.bfloat16)


def draw_keys(key, part):
    key = jax.random.fold_in(key, 2)
    full_shape = (SEQS, SEL, KVH * HD)
    result = jnp.clip(jax.random.normal(key, full_shape, jnp.float32), -6.0, 6.0)
    return result.astype(jnp.bfloat16)


def draw_positions(key, part):
    key = jax.random.fold_in(key, 3)
    sequences = []
    for sequence in range(SEQS):
        picked = jax.random.permutation(jax.random.fold_in(key, sequence), CTX - 2)[:SEL - 2] + 1
        complete = jnp.concatenate([jnp.zeros((1,), jnp.int32), picked.astype(jnp.int32), jnp.full((1,), CTX - 1, jnp.int32)])
        sequences.append(jnp.sort(complete))
    return jnp.stack(sequences)


def shard_levels(own_key, shape, cuts, low, top_value):
    gain = 1.0
    for axis_at, parts in cuts:
        steps = jax.random.uniform(jax.random.fold_in(jax.random.fold_in(own_key, 6), axis_at), (parts,), jnp.float32, low / len(cuts), top_value / len(cuts))
        gain = gain * jnp.repeat(jnp.exp(steps), shape[axis_at] // parts).reshape((-1,) + (1,) * (len(shape) - 1 - axis_at))
    return gain


def bell_draw(key, extent, width, reach, cuts=(), held_as=jnp.bfloat16):
    values = width * jax.random.normal(key, extent, jnp.float32)
    if cuts:
        values = values * shard_levels(key, extent, cuts, -0.22, 0.18)
    return jnp.clip(values, -reach, reach).astype(held_as)


def setup_inputs(seed: int = 0) -> dict:
    streams_of = jax.random.split(jax.random.key(seed), 8)
    queries = draw_queries(jax.random.fold_in(streams_of[7], 71), 0)
    keys = draw_keys(jax.random.fold_in(streams_of[7], 71), 0)
    values = bell_draw(streams_of[2], (SEQS, SEL, KVH * HD), 1.0, 6.0, ((0, 4), (1, 8)))
    out_grad = bell_draw(streams_of[3], (SEQS, SEL, HQ * HD), 1.0, 6.0, ((0, 4), (1, 8)))
    routed_inputs = bell_draw(streams_of[4], (SEQS, SEL, D), 1.0, 6.0, ((0, 4), (1, 8)))
    router_weight = bell_draw(streams_of[5], (D,), D ** -0.5, 0.09375, (), jnp.float32)
    positions = draw_positions(jax.random.fold_in(streams_of[7], 71), 0)
    return {"queries": queries, "keys": keys, "values": values, "out_grad": out_grad, "routed_inputs": routed_inputs, "router_weight": router_weight, "positions": positions}


ROPE_BASE = 500000.0

def rope_tables(pair_count):
    frequency = [ROPE_BASE ** (-number / pair_count) for number in range(pair_count)]
    coarse = [256.0 * factor % (2.0 * math.pi) for factor in frequency]
    return (jnp.asarray(frequency, jnp.float32), jnp.asarray(coarse, jnp.float32))

def rotation(positions, head_dim):
    frequency, coarse = rope_tables(head_dim // 2)
    upper_part = (positions // 256).astype(jnp.float32)
    lower_part = (positions % 256).astype(jnp.float32)
    angles = upper_part[:, None] * coarse[None, :] + lower_part[:, None] * frequency[None, :]
    return (jnp.cos(angles)[:, None, :], jnp.sin(angles)[:, None, :])

def turn_forward(vectors, cosine, sine):
    width_half = vectors.shape[-1] // 2
    first_half = vectors[..., :width_half]
    second_half = vectors[..., width_half:]
    return jnp.concatenate([first_half * cosine - second_half * sine, second_half * cosine + first_half * sine], axis=-1)

def turn_back(vectors, cosine, sine):
    width_half = vectors.shape[-1] // 2
    first_half = vectors[..., :width_half]
    second_half = vectors[..., width_half:]
    return jnp.concatenate([first_half * cosine + second_half * sine, second_half * cosine - first_half * sine], axis=-1)

def one_sequence(queries, keys, values, out_grad, inputs, router_weight, positions):
    group_size = HQ // KVH
    score_scale = 1.0 / math.sqrt(HD)
    cosine, sine = rotation(positions, HD)
    query_rot = turn_forward(queries.astype(jnp.float32).reshape(SEL, HQ, HD), cosine, sine).astype(jnp.bfloat16)
    key_rot = turn_forward(keys.astype(jnp.float32).reshape(SEL, KVH, HD), cosine, sine).astype(jnp.bfloat16)
    key_wide = key_rot.astype(jnp.float32)
    value_wide = values.reshape(SEL, KVH, HD).astype(jnp.float32)
    logits = jnp.dot(inputs.astype(jnp.float32), router_weight, precision=lax.Precision.HIGHEST)
    gate = jax.nn.sigmoid(logits)
    upstream = out_grad.astype(jnp.float32).reshape(SEL, KVH, group_size, HD)
    scaled_grad = (gate[:, None, None, None] * upstream).astype(jnp.bfloat16)
    rows_block = min(512, SEL)
    blocks = SEL // rows_block

    def split(array):
        return array.reshape((blocks, rows_block) + array.shape[1:])

    def step(carry, pieces):
        key_acc, value_acc = carry
        query_tile, scaled_tile, upstream_tile, place_tile, gate_tile = pieces
        query_wide = query_tile.astype(jnp.float32)
        scaled_wide = scaled_tile.astype(jnp.float32)
        scores = jnp.einsum('tkgd,ukd->kgtu', query_wide, key_wide) * score_scale
        allowed = place_tile[:, None] >= positions[None, :]
        scores = jnp.where(allowed[None, None], scores, -jnp.inf)
        top = lax.optimization_barrier(jnp.max(scores, axis=-1, keepdims=True))
        lse = top + jnp.log(lax.optimization_barrier(jnp.sum(jnp.exp(scores - top), axis=-1, keepdims=True)))
        weights = jnp.exp(scores - lse)
        probs = lax.optimization_barrier(weights.astype(jnp.bfloat16)).astype(jnp.float32)
        attn = jnp.einsum('kgtu,ukd->tkgd', probs, value_wide)
        router_term = lax.optimization_barrier(jnp.sum(upstream_tile * attn, axis=(1, 2, 3)))
        logit_grad = gate_tile * (1.0 - gate_tile) * router_term
        delta = jnp.transpose(lax.optimization_barrier(jnp.sum(scaled_wide * attn, axis=-1)), (1, 2, 0))
        prob_grad = jnp.einsum('tkgd,ukd->kgtu', scaled_wide, value_wide)
        score_grad = (weights * (prob_grad - delta[..., None]) * score_scale).astype(jnp.bfloat16)
        score_wide = lax.optimization_barrier(score_grad).astype(jnp.float32)
        query_acc = jnp.einsum('kgtu,ukd->tkgd', score_wide, key_wide)
        key_acc = key_acc + jnp.einsum('kgtu,tkgd->ukd', score_wide, query_wide)
        value_acc = value_acc + jnp.einsum('kgtu,tkgd->ukd', probs, scaled_wide)
        return ((key_acc, value_acc), (query_acc, logit_grad))
    start_state = (jnp.zeros((SEL, KVH, HD), jnp.float32), jnp.zeros((SEL, KVH, HD), jnp.float32))
    pieces = (split(query_rot.reshape(SEL, KVH, group_size, HD)), split(scaled_grad), split(upstream), split(positions), split(gate))
    (key_acc, value_acc), (query_acc, logit_grad) = lax.scan(step, start_state, pieces)
    query_acc = query_acc.reshape(SEL, HQ, HD)
    logit_grad = logit_grad.reshape(SEL)
    query_grad = turn_back(query_acc, cosine, sine).astype(jnp.bfloat16).reshape(SEL, HQ * HD)
    key_grad = turn_back(key_acc, cosine, sine).astype(jnp.bfloat16).reshape(SEL, KVH * HD)
    value_grad = value_acc.astype(jnp.bfloat16).reshape(SEL, KVH * HD)
    router_part = jnp.dot(logit_grad, inputs.astype(jnp.float32), precision=lax.Precision.HIGHEST)
    return (query_grad, key_grad, value_grad, router_part)

def reference(queries, keys, values, out_grad, routed_inputs, router_weight, positions):
    query_list = []
    key_list = []
    value_list = []
    router_total = jnp.zeros((D,), jnp.float32)
    for sequence in range(SEQS):
        query_grad, key_grad, value_grad, router_part = one_sequence(queries[sequence], keys[sequence], values[sequence], out_grad[sequence], routed_inputs[sequence], router_weight, positions[sequence])
        query_list.append(query_grad)
        key_list.append(key_grad)
        value_list.append(value_grad)
        router_total = router_total + router_part
    router_grad = router_total / math.sqrt(SEQS * SEL)
    return (jnp.stack(query_list), jnp.stack(key_list), jnp.stack(value_list), router_grad)
```

```python
import functools
import math

import jax
import jax.numpy as jnp
import numpy as np
from jax import lax
from jax.experimental import pallas as pl
from jax.experimental.pallas import tpu as pltpu
from jax.sharding import PartitionSpec as P

HQ = 16
KVH = 4
HD = 128
GROUP = HQ // KVH
ROPE_BASE = 500000.0
NEG_LARGE = -1e30
VMEM_LIMIT = 32 * 1024 * 1024
SCORES_COST = 20 * 10**9
TERMS_COST = 20 * 10**9
RIDE_COST = 20 * 10**9


def rope_table():
    half = HD // 2
    frequency = [ROPE_BASE ** (-number / half) for number in range(half)]
    coarse = [256.0 * factor % (2.0 * math.pi) for factor in frequency]
    return np.asarray([coarse + coarse, frequency + frequency], np.float32)


def turn(vectors, cosine, sine):
    return vectors * cosine + pltpu.roll(vectors, HD // 2, 1) * sine


def head(number):
    return slice(number * HD, (number + 1) * HD)


def rows_of(number, depth):
    return slice(number * depth, (number + 1) * depth)


def diagonal(slots, lanes):
    row = lax.broadcasted_iota(jnp.int32, (slots, lanes), 0)
    lane = lax.broadcasted_iota(jnp.int32, (slots, lanes), 1)
    return lax.rem(lane, slots) == row


def prepare_kernel(*refs):
    place_hbm, table_hbm, key_hbm, value_hbm, query_hbm, upstream_hbm = refs[:6]
    pair_ref, query_out, trig_ref = refs[6:9]
    place_ref, table_ref, key_ref, value_ref, query_ref, upstream_ref, semaphores = refs[9:]
    slots = key_ref.shape[0]
    copies = [
        pltpu.make_async_copy(source, target, semaphores.at[at])
        for at, (source, target) in enumerate(
            [
                (place_hbm, place_ref),
                (table_hbm, table_ref),
                (key_hbm, key_ref),
                (value_hbm, value_ref),
                (query_hbm, query_ref),
                (upstream_hbm, upstream_ref),
            ]
        )
    ]
    for copy in copies:
        copy.start()
    copies[0].wait()
    place = place_ref[...]
    upper = (place >> 8).astype(jnp.float32)
    lower = (place & 255).astype(jnp.float32)
    same = diagonal(slots, slots)
    upper = jnp.sum(jnp.where(same, upper, 0.0), axis=1, keepdims=True)
    lower = jnp.sum(jnp.where(same, lower, 0.0), axis=1, keepdims=True)
    copies[1].wait()
    angles = upper * table_ref[0:1, :] + lower * table_ref[1:2, :]
    cosine = jnp.cos(angles)
    lane = lax.broadcasted_iota(jnp.int32, angles.shape, 1)
    sine = jnp.sin(angles)
    sine = jnp.where(lane < HD // 2, -sine, sine)
    trig_ref[0:slots, :] = cosine
    trig_ref[slots : 2 * slots, :] = sine
    for copy in copies[2:]:
        copy.wait()
    for number in range(KVH):
        wide = key_ref[:, head(number)].astype(jnp.float32)
        pair_ref[rows_of(number, slots), :] = turn(wide, cosine, sine).astype(jnp.bfloat16)
        pair_ref[rows_of(KVH + number, slots), :] = value_ref[:, head(number)]
    for number in range(HQ):
        wide = query_ref[:, head(number)].astype(jnp.float32)
        query_out[rows_of(number, slots), :] = turn(wide, cosine, sine).astype(jnp.bfloat16)
        query_out[rows_of(HQ + number, slots), :] = upstream_ref[:, head(number)]


def gate_kernel(weight_hbm, input_hbm, gate_ref, input_ref, weight_ref, semaphores):
    copies = [
        pltpu.make_async_copy(weight_hbm, weight_ref, semaphores.at[0]),
        pltpu.make_async_copy(input_hbm, input_ref, semaphores.at[1]),
    ]
    for copy in copies:
        copy.start()
    for copy in copies:
        copy.wait()
    slots = input_ref.shape[0]
    blocks = weight_ref.shape[0]
    total = jnp.zeros((slots, HD), jnp.float32)
    for number in range(blocks):
        total += input_ref[:, head(number)].astype(jnp.float32) * weight_ref[number : number + 1, :]
    gate = jax.nn.sigmoid(jnp.sum(total, axis=1, keepdims=True))
    same = diagonal(slots, gate_ref.shape[1])
    gate_ref[...] = jnp.broadcast_to(
        jnp.sum(jnp.where(same, gate, 0.0), axis=0, keepdims=True), gate_ref.shape
    )


def tiles(pair_refs, query_refs, number, slots):
    rows = GROUP * slots
    key_tile = jnp.concatenate([ref[rows_of(number, slots), :] for ref in pair_refs], axis=0)
    value_tile = jnp.concatenate(
        [ref[rows_of(KVH + number, slots), :] for ref in pair_refs], axis=0
    )
    query_tile = jnp.concatenate([ref[rows_of(number, rows), :] for ref in query_refs], axis=0)
    upstream_tile = jnp.concatenate(
        [ref[rows_of(KVH + number, rows), :] for ref in query_refs], axis=0
    )
    return key_tile, value_tile, query_tile, upstream_tile


def scores_kernel(slots, *refs):
    gate_ref, own_ref, other_ref = refs[:3]
    pair_refs = refs[3:-3]
    grown_out, grad_out, stats_out = refs[-3:]
    rows = GROUP * slots
    keys_total = len(pair_refs) * slots
    own = lax.axis_index("ctx")
    other = own + 1 - 2 * lax.rem(own, 2)
    row = lax.broadcasted_iota(jnp.int32, (keys_total, 2 * rows), 0)
    lane = lax.broadcasted_iota(jnp.int32, (keys_total, 2 * rows), 1)
    owner = 2 * jnp.bitwise_xor(own // 2, row // slots) + lax.rem(own, 2)
    key_at = owner * slots + lax.rem(row, slots)
    query_at = lax.rem(lane, slots) + jnp.where(lane < rows, own, other) * slots
    bias = jnp.where(key_at <= query_at, 0.0, NEG_LARGE)
    across = (((1,), (1,)), ((), ()))
    for number in range(KVH):
        key_tile, value_tile, query_tile, upstream_tile = tiles(
            pair_refs, (own_ref, other_ref), number, slots
        )
        scores = lax.dot_general(
            key_tile, query_tile, across, preferred_element_type=jnp.float32
        )
        scores = scores * (1.0 / math.sqrt(HD)) + bias
        top = jnp.max(scores, axis=0, keepdims=True)
        grown = jnp.exp(scores - top)
        prob_grad = lax.dot_general(
            value_tile, upstream_tile, across, preferred_element_type=jnp.float32
        )
        grown_out[number] = grown
        grad_out[number] = prob_grad
        stats_out[number : number + 1, :] = top
        stats_out[KVH + number : KVH + number + 1, :] = jnp.sum(grown, axis=0, keepdims=True)
        stats_out[2 * KVH + number : 2 * KVH + number + 1, :] = jnp.sum(
            grown * prob_grad, axis=0, keepdims=True
        )
    stats_out[3 * KVH :, :] = jnp.concatenate(
        [gate_ref[0:KVH, :], jnp.zeros((KVH, rows), jnp.float32)], axis=1
    )


def combine_kernel(own_ref, other_ref, input_ref, input_other_ref, coef_out, router_out):
    slots = input_ref.shape[0]
    rows = GROUP * slots
    mine = own_ref[...]
    swapped = other_ref[...]
    theirs = jnp.concatenate([swapped[:, rows:], swapped[:, :rows]], axis=1)
    top = jnp.maximum(mine[0:KVH], theirs[0:KVH])
    mine_part = jnp.exp(mine[0:KVH] - top)
    their_part = jnp.exp(theirs[0:KVH] - top)
    mass = mine[KVH : 2 * KVH] * mine_part + theirs[KVH : 2 * KVH] * their_part
    inverse = 1.0 / mass
    inner = (
        mine[2 * KVH : 3 * KVH] * mine_part + theirs[2 * KVH : 3 * KVH] * their_part
    ) * inverse
    gate = mine[3 * KVH :] + theirs[3 * KVH :]
    coef_out[0:KVH, :] = mine_part * inverse * gate
    coef_out[KVH : 2 * KVH, :] = inner
    slope = gate[0:1] * (1.0 - gate[0:1]) * jnp.sum(inner, axis=0, keepdims=True)
    same = diagonal(slots, rows)
    own_slope = jnp.sum(jnp.where(same, slope[:, :rows], 0.0), axis=1, keepdims=True)
    other_slope = jnp.sum(jnp.where(same, slope[:, rows:], 0.0), axis=1, keepdims=True)
    for number in range(router_out.shape[0]):
        router_out[number : number + 1, :] = jnp.sum(
            own_slope * input_ref[:, head(number)].astype(jnp.float32)
            + other_slope * input_other_ref[:, head(number)].astype(jnp.float32),
            axis=0,
            keepdims=True,
        )


def terms_kernel(slots, half, *refs):
    coef_ref, grown_ref, grad_ref, own_ref, other_ref = refs[:5]
    pair_refs = refs[5 : 5 + half]
    query_out, query_send, term_own = refs[5 + half : 8 + half]
    term_refs = refs[8 + half :]
    rows = GROUP * slots
    scale = 1.0 / math.sqrt(HD)
    for number in range(KVH):
        key_tile, _, query_tile, upstream_tile = tiles(
            pair_refs, (own_ref, other_ref), number, slots
        )
        gated = grown_ref[number] * coef_ref[number : number + 1, :]
        inner = coef_ref[KVH + number : KVH + number + 1, :]
        score_grad = (gated * (grad_ref[number] - inner) * scale).astype(jnp.bfloat16)
        key_term = jnp.dot(score_grad, query_tile, preferred_element_type=jnp.float32)
        value_term = jnp.dot(
            gated.astype(jnp.bfloat16), upstream_tile, preferred_element_type=jnp.float32
        )
        key_rows, value_rows = rows_of(number, slots), rows_of(KVH + number, slots)
        term_own[key_rows, :] = key_term[0:slots]
        term_own[value_rows, :] = value_term[0:slots]
        for at, ref in enumerate(term_refs, 1):
            ref[key_rows, :] = key_term[rows_of(at, slots)].astype(jnp.bfloat16)
            ref[value_rows, :] = value_term[rows_of(at, slots)].astype(jnp.bfloat16)
        query_term = lax.dot_general(
            score_grad, key_tile, (((0,), (0,)), ((), ())), preferred_element_type=jnp.float32
        )
        query_out[rows_of(number, rows), :] = query_term[0:rows]
        query_send[rows_of(number, rows), :] = query_term[rows:].astype(jnp.bfloat16)


def ride_kernel(groups, *refs):
    router_refs = refs[:groups]
    count = (len(refs) - groups - 1) // 2
    term_refs = refs[groups : groups + count]
    router_out = refs[groups + count]
    router = router_refs[0][...]
    for ref in router_refs[1:]:
        router += ref[...]
    router_out[...] = router
    for term, out in zip(term_refs, refs[groups + count + 1 :]):
        out[0 : term.shape[0], :] = term[...]
        out[term.shape[0] :, :] = router.astype(jnp.bfloat16)


def query_kernel(trig_ref, own_ref, other_ref, query_out, trig_out):
    slots = query_out.shape[0]
    cosine = trig_ref[0:slots, :]
    sine = trig_ref[slots : 2 * slots, :]
    trig_out[...] = trig_ref[...]
    for number in range(HQ):
        part = rows_of(number, slots)
        total = own_ref[part, :] + other_ref[part, :].astype(jnp.float32)
        query_out[:, head(number)] = turn(total, cosine, -sine).astype(jnp.bfloat16)


def final_kernel(router_scale, *refs):
    trig_ref, own_ref, router_ref = refs[:3]
    term_refs = refs[3:-3]
    key_out, value_out, router_out = refs[-3:]
    slots = key_out.shape[0]
    cosine = trig_ref[0:slots, :]
    sine = trig_ref[slots : 2 * slots, :]
    for number in range(2 * KVH):
        part = rows_of(number, slots)
        total = own_ref[part, :]
        for ref in term_refs:
            total += ref[part, :].astype(jnp.float32)
        if number < KVH:
            key_out[:, head(number)] = turn(total, cosine, -sine).astype(jnp.bfloat16)
        else:
            value_out[:, head(number - KVH)] = total.astype(jnp.bfloat16)
    router = router_ref[...]
    for ref in term_refs:
        router += ref[2 * KVH * slots :, :].astype(jnp.float32)
    router_out[...] = router * router_scale


def call(kernel, outs, args, fetched=(), scratch=(), cost=None):
    local = pl.BlockSpec(memory_space=pltpu.VMEM)
    distant = pl.BlockSpec(memory_space=pl.ANY)
    scratch = list(scratch) + [pltpu.SemaphoreType.DMA((len(fetched),))] * bool(fetched)
    return pl.pallas_call(
        kernel,
        out_shape=outs,
        in_specs=[local] * len(args) + [distant] * len(fetched),
        out_specs=[local] * len(outs),
        scratch_shapes=scratch,
        compiler_params=pltpu.CompilerParams(vmem_limit_bytes=VMEM_LIMIT),
        cost_estimate=cost and pl.CostEstimate(cost, 0, 0),
    )(*args, *[pltpu.with_memory_space_constraint(array, pltpu.HBM) for array in fetched])


def exchange(array, axis, step, size):
    return lax.ppermute(array, axis, [(at, at ^ step) for at in range(size)])


def shards(queries, keys, values, out_grad, routed_inputs, router_weight, positions):
    slots = queries.shape[1]
    width = routed_inputs.shape[2]
    count = lax.axis_size("ctx")
    groups = lax.axis_size("dp")
    half = count // 2
    rows = GROUP * slots
    lines = width // HD
    bf16, f32 = jnp.bfloat16, jnp.float32

    def swap(array):
        return exchange(array, "ctx", 1, count)

    near = pltpu.VMEM
    fetched = [positions, jnp.asarray(rope_table()), keys[0], values[0], queries[0], out_grad[0]]
    pair, query, trig = call(
        prepare_kernel,
        [
            near((2 * KVH * slots, HD), bf16),
            near((2 * HQ * slots, HD), bf16),
            near((2 * slots, HD), f32),
        ],
        [],
        fetched,
        [near(array.shape, array.dtype) for array in fetched],
    )
    query_other = swap(query)
    pairs = [pair] + [
        exchange(pair, "ctx", 2 * step, count) for step in range(1, half)
    ]
    gate, inputs = call(
        gate_kernel,
        [near((8, rows), f32), near((slots, width), bf16)],
        [],
        [router_weight.reshape(lines, HD), routed_inputs[0]],
        [near((lines, HD), f32)],
    )
    inputs_other = swap(routed_inputs[0])
    grown, grad, stats = call(
        functools.partial(scores_kernel, slots),
        [
            near((KVH, half * slots, 2 * rows), f32),
            near((KVH, half * slots, 2 * rows), f32),
            near((4 * KVH, 2 * rows), f32),
        ],
        [gate, query, query_other, *pairs],
        cost=SCORES_COST,
    )
    coef, router = call(
        combine_kernel,
        [near((2 * KVH, 2 * rows), f32), near((lines, HD), f32)],
        [stats, swap(stats), inputs, inputs_other],
    )
    routers = [router] + [
        exchange(router, "dp", step, groups) for step in range(1, groups)
    ]
    query_own, query_send, term_own, *terms = call(
        functools.partial(terms_kernel, slots, half),
        [
            near((HQ * slots, HD), f32),
            near((HQ * slots, HD), bf16),
            near((2 * KVH * slots, HD), f32),
        ]
        + [near((2 * KVH * slots, HD), bf16)] * (half - 1),
        [coef, grown, grad, query, query_other, *pairs],
        cost=TERMS_COST,
    )
    query_back = swap(query_send)
    router, *terms = call(
        functools.partial(ride_kernel, groups),
        [near((lines, HD), f32)] + [near((2 * KVH * slots + lines, HD), bf16)] * (half - 1),
        [*routers, *terms],
        cost=RIDE_COST,
    )
    terms = [exchange(term, "ctx", 2 * step, count) for step, term in enumerate(terms, 1)]
    shape = jax.ShapeDtypeStruct
    query_grad, trig = call(
        query_kernel,
        [shape((slots, HQ * HD), bf16), near((2 * slots, HD), f32)],
        [trig, query_own, query_back],
    )
    key_grad, value_grad, router_grad = call(
        functools.partial(final_kernel, 1.0 / math.sqrt(groups * count * slots)),
        [shape((slots, KVH * HD), bf16), shape((slots, KVH * HD), bf16), shape((lines, HD), f32)],
        [trig, term_own, router, *terms],
    )
    return (query_grad[None], key_grad[None], value_grad[None], router_grad.reshape(width))


def solution(mesh):
    in_specs = (
        P("dp", "ctx", None),
        P("dp", "ctx", None),
        P("dp", "ctx", None),
        P("dp", "ctx", None),
        P("dp", "ctx", None),
        P(),
        P("dp", "ctx"),
    )
    out_specs = (P("dp", "ctx", None), P("dp", "ctx", None), P("dp", "ctx", None), P())
    return jax.shard_map(shards, mesh=mesh, in_specs=in_specs, out_specs=out_specs, check_vma=False)
```

```python
import functools
import math

import jax
import jax.numpy as jnp
import numpy as np
from jax import lax
from jax.experimental import pallas as pl
from jax.experimental.pallas import tpu as pltpu
from jax.sharding import PartitionSpec as P

HQ = 16
KVH = 4
HD = 128
GROUP = HQ // KVH
ROPE_BASE = 500000.0
NEG_LARGE = -1e30
VMEM_LIMIT = 32 * 1024 * 1024
SCORES_COST = 20 * 10**9
TERMS_COST = 20 * 10**9
ROUTER_COSTS = (20 * 10**9, 1)
QUERY_COST = 1


def rope_table():
    half = HD // 2
    frequency = [ROPE_BASE ** (-number / half) for number in range(half)]
    coarse = [256.0 * factor % (2.0 * math.pi) for factor in frequency]
    return np.asarray([coarse + coarse, frequency + frequency], np.float32)


def turn(vectors, cosine, sine):
    return vectors * cosine + pltpu.roll(vectors, HD // 2, 1) * sine


def head(number):
    return slice(number * HD, (number + 1) * HD)


def rows_of(number, depth):
    return slice(number * depth, (number + 1) * depth)


def diagonal(slots, lanes):
    row = lax.broadcasted_iota(jnp.int32, (slots, lanes), 0)
    lane = lax.broadcasted_iota(jnp.int32, (slots, lanes), 1)
    return lax.rem(lane, slots) == row


def prepare_kernel(*refs):
    place_hbm, table_hbm, key_hbm, value_hbm, query_hbm, upstream_hbm = refs[:6]
    pair_ref, query_out, trig_ref = refs[6:9]
    place_ref, table_ref, key_ref, value_ref, query_ref, upstream_ref, semaphores = refs[9:]
    slots = key_ref.shape[0]
    copies = [
        pltpu.make_async_copy(source, target, semaphores.at[at])
        for at, (source, target) in enumerate(
            [
                (place_hbm, place_ref),
                (table_hbm, table_ref),
                (key_hbm, key_ref),
                (value_hbm, value_ref),
                (query_hbm, query_ref),
                (upstream_hbm, upstream_ref),
            ]
        )
    ]
    for copy in copies:
        copy.start()
    copies[0].wait()
    place = place_ref[...]
    upper = (place >> 8).astype(jnp.float32)
    lower = (place & 255).astype(jnp.float32)
    same = diagonal(slots, slots)
    upper = jnp.sum(jnp.where(same, upper, 0.0), axis=1, keepdims=True)
    lower = jnp.sum(jnp.where(same, lower, 0.0), axis=1, keepdims=True)
    copies[1].wait()
    angles = upper * table_ref[0:1, :] + lower * table_ref[1:2, :]
    cosine = jnp.cos(angles)
    lane = lax.broadcasted_iota(jnp.int32, angles.shape, 1)
    sine = jnp.sin(angles)
    sine = jnp.where(lane < HD // 2, -sine, sine)
    trig_ref[0:slots, :] = cosine
    trig_ref[slots : 2 * slots, :] = sine
    for copy in copies[2:]:
        copy.wait()
    for number in range(KVH):
        wide = key_ref[:, head(number)].astype(jnp.float32)
        pair_ref[rows_of(number, slots), :] = turn(wide, cosine, sine).astype(jnp.bfloat16)
        pair_ref[rows_of(KVH + number, slots), :] = value_ref[:, head(number)]
    for number in range(HQ):
        wide = query_ref[:, head(number)].astype(jnp.float32)
        query_out[rows_of(number, slots), :] = turn(wide, cosine, sine).astype(jnp.bfloat16)
        query_out[rows_of(HQ + number, slots), :] = upstream_ref[:, head(number)]


def gate_kernel(weight_hbm, input_hbm, gate_ref, input_ref, weight_ref, semaphores):
    copies = [
        pltpu.make_async_copy(weight_hbm, weight_ref, semaphores.at[0]),
        pltpu.make_async_copy(input_hbm, input_ref, semaphores.at[1]),
    ]
    for copy in copies:
        copy.start()
    for copy in copies:
        copy.wait()
    slots = input_ref.shape[0]
    blocks = weight_ref.shape[0]
    total = jnp.zeros((slots, HD), jnp.float32)
    for number in range(blocks):
        total += input_ref[:, head(number)].astype(jnp.float32) * weight_ref[number : number + 1, :]
    gate = jax.nn.sigmoid(jnp.sum(total, axis=1, keepdims=True))
    same = diagonal(slots, gate_ref.shape[1])
    gate_ref[...] = jnp.broadcast_to(
        jnp.sum(jnp.where(same, gate, 0.0), axis=0, keepdims=True), gate_ref.shape
    )


def tiles(pair_refs, query_refs, number, slots):
    rows = GROUP * slots
    key_tile = jnp.concatenate([ref[rows_of(number, slots), :] for ref in pair_refs], axis=0)
    value_tile = jnp.concatenate(
        [ref[rows_of(KVH + number, slots), :] for ref in pair_refs], axis=0
    )
    query_tile = jnp.concatenate([ref[rows_of(number, rows), :] for ref in query_refs], axis=0)
    upstream_tile = jnp.concatenate(
        [ref[rows_of(KVH + number, rows), :] for ref in query_refs], axis=0
    )
    return key_tile, value_tile, query_tile, upstream_tile


def scores_kernel(slots, *refs):
    gate_ref, own_ref, other_ref = refs[:3]
    pair_refs = refs[3:-3]
    grown_out, grad_out, stats_out = refs[-3:]
    rows = GROUP * slots
    keys_total = len(pair_refs) * slots
    own = lax.axis_index("ctx")
    other = own + 1 - 2 * lax.rem(own, 2)
    row = lax.broadcasted_iota(jnp.int32, (keys_total, 2 * rows), 0)
    lane = lax.broadcasted_iota(jnp.int32, (keys_total, 2 * rows), 1)
    owner = 2 * jnp.bitwise_xor(own // 2, row // slots) + lax.rem(own, 2)
    key_at = owner * slots + lax.rem(row, slots)
    query_at = lax.rem(lane, slots) + jnp.where(lane < rows, own, other) * slots
    bias = jnp.where(key_at <= query_at, 0.0, NEG_LARGE)
    across = (((1,), (1,)), ((), ()))
    for number in range(KVH):
        key_tile, value_tile, query_tile, upstream_tile = tiles(
            pair_refs, (own_ref, other_ref), number, slots
        )
        scores = lax.dot_general(
            key_tile, query_tile, across, preferred_element_type=jnp.float32
        )
        scores = scores * (1.0 / math.sqrt(HD)) + bias
        top = jnp.max(scores, axis=0, keepdims=True)
        grown = jnp.exp(scores - top)
        prob_grad = lax.dot_general(
            value_tile, upstream_tile, across, preferred_element_type=jnp.float32
        )
        grown_out[number] = grown
        grad_out[number] = prob_grad
        stats_out[number : number + 1, :] = top
        stats_out[KVH + number : KVH + number + 1, :] = jnp.sum(grown, axis=0, keepdims=True)
        stats_out[2 * KVH + number : 2 * KVH + number + 1, :] = jnp.sum(
            grown * prob_grad, axis=0, keepdims=True
        )
    stats_out[3 * KVH :, :] = jnp.concatenate(
        [gate_ref[0:KVH, :], jnp.zeros((KVH, rows), jnp.float32)], axis=1
    )


def combine_kernel(
    own_ref, other_ref, input_ref, input_other_ref, coef_out, router_out, send_out
):
    slots = input_ref.shape[0]
    rows = GROUP * slots
    mine = own_ref[...]
    swapped = other_ref[...]
    theirs = jnp.concatenate([swapped[:, rows:], swapped[:, :rows]], axis=1)
    top = jnp.maximum(mine[0:KVH], theirs[0:KVH])
    mine_part = jnp.exp(mine[0:KVH] - top)
    their_part = jnp.exp(theirs[0:KVH] - top)
    mass = mine[KVH : 2 * KVH] * mine_part + theirs[KVH : 2 * KVH] * their_part
    inverse = 1.0 / mass
    inner = (
        mine[2 * KVH : 3 * KVH] * mine_part + theirs[2 * KVH : 3 * KVH] * their_part
    ) * inverse
    gate = mine[3 * KVH :] + theirs[3 * KVH :]
    coef_out[0:KVH, :] = mine_part * inverse * gate
    coef_out[KVH : 2 * KVH, :] = inner
    slope = gate[0:1] * (1.0 - gate[0:1]) * jnp.sum(inner, axis=0, keepdims=True)
    same = diagonal(slots, rows)
    own_slope = jnp.sum(jnp.where(same, slope[:, :rows], 0.0), axis=1, keepdims=True)
    other_slope = jnp.sum(jnp.where(same, slope[:, rows:], 0.0), axis=1, keepdims=True)
    for number in range(router_out.shape[0]):
        router_out[number : number + 1, :] = jnp.sum(
            own_slope * input_ref[:, head(number)].astype(jnp.float32)
            + other_slope * input_other_ref[:, head(number)].astype(jnp.float32),
            axis=0,
            keepdims=True,
        )
    send_out[...] = router_out[...].astype(jnp.bfloat16)


def terms_kernel(slots, half, *refs):
    coef_ref, grown_ref, grad_ref, own_ref, other_ref = refs[:5]
    pair_refs = refs[5 : 5 + half]
    query_out, query_send, term_own = refs[5 + half : 8 + half]
    term_refs = refs[8 + half :]
    rows = GROUP * slots
    scale = 1.0 / math.sqrt(HD)
    for number in range(KVH):
        key_tile, _, query_tile, upstream_tile = tiles(
            pair_refs, (own_ref, other_ref), number, slots
        )
        gated = grown_ref[number] * coef_ref[number : number + 1, :]
        inner = coef_ref[KVH + number : KVH + number + 1, :]
        score_grad = (gated * (grad_ref[number] - inner) * scale).astype(jnp.bfloat16)
        key_term = jnp.dot(score_grad, query_tile, preferred_element_type=jnp.float32)
        value_term = jnp.dot(
            gated.astype(jnp.bfloat16), upstream_tile, preferred_element_type=jnp.float32
        )
        key_rows, value_rows = rows_of(number, slots), rows_of(KVH + number, slots)
        term_own[key_rows, :] = key_term[0:slots]
        term_own[value_rows, :] = value_term[0:slots]
        for at, ref in enumerate(term_refs, 1):
            ref[key_rows, :] = key_term[rows_of(at, slots)].astype(jnp.bfloat16)
            ref[value_rows, :] = value_term[rows_of(at, slots)].astype(jnp.bfloat16)
        query_term = lax.dot_general(
            score_grad, key_tile, (((0,), (0,)), ((), ())), preferred_element_type=jnp.float32
        )
        query_out[rows_of(number, rows), :] = query_term[0:rows]
        query_send[rows_of(number, rows), :] = query_term[rows:].astype(jnp.bfloat16)


def router_kernel(*refs):
    total = refs[0][...]
    for ref in refs[1:-1]:
        total += ref[...].astype(jnp.float32)
    refs[-1][...] = total


def query_kernel(trig_ref, own_ref, other_ref, query_out, trig_out):
    slots = query_out.shape[0]
    cosine = trig_ref[0:slots, :]
    sine = trig_ref[slots : 2 * slots, :]
    trig_out[...] = trig_ref[...]
    for number in range(HQ):
        part = rows_of(number, slots)
        total = own_ref[part, :] + other_ref[part, :].astype(jnp.float32)
        query_out[:, head(number)] = turn(total, cosine, -sine).astype(jnp.bfloat16)


def final_kernel(router_scale, *refs):
    trig_ref, own_ref, router_ref, router_other_ref = refs[:4]
    term_refs = refs[4:-3]
    key_out, value_out, router_out = refs[-3:]
    slots = key_out.shape[0]
    cosine = trig_ref[0:slots, :]
    sine = trig_ref[slots : 2 * slots, :]
    for number in range(2 * KVH):
        part = rows_of(number, slots)
        total = own_ref[part, :]
        for ref in term_refs:
            total += ref[part, :].astype(jnp.float32)
        if number < KVH:
            key_out[:, head(number)] = turn(total, cosine, -sine).astype(jnp.bfloat16)
        else:
            value_out[:, head(number - KVH)] = total.astype(jnp.bfloat16)
    router_out[...] = (router_ref[...] + router_other_ref[...]) * router_scale


def call(kernel, outs, args, fetched=(), scratch=(), cost=None):
    local = pl.BlockSpec(memory_space=pltpu.VMEM)
    distant = pl.BlockSpec(memory_space=pl.ANY)
    scratch = list(scratch) + [pltpu.SemaphoreType.DMA((len(fetched),))] * bool(fetched)
    return pl.pallas_call(
        kernel,
        out_shape=outs,
        in_specs=[local] * len(args) + [distant] * len(fetched),
        out_specs=[local] * len(outs),
        scratch_shapes=scratch,
        compiler_params=pltpu.CompilerParams(vmem_limit_bytes=VMEM_LIMIT),
        cost_estimate=cost and pl.CostEstimate(cost, 0, 0),
    )(*args, *[pltpu.with_memory_space_constraint(array, pltpu.HBM) for array in fetched])


def exchange(array, axis, step, size):
    return lax.ppermute(array, axis, [(at, at ^ step) for at in range(size)])


def shards(queries, keys, values, out_grad, routed_inputs, router_weight, positions):
    slots = queries.shape[1]
    width = routed_inputs.shape[2]
    count = lax.axis_size("ctx")
    groups = lax.axis_size("dp")
    half = count // 2
    rows = GROUP * slots
    lines = width // HD
    bf16, f32 = jnp.bfloat16, jnp.float32

    def swap(array):
        return exchange(array, "ctx", 1, count)

    near = pltpu.VMEM
    fetched = [positions, jnp.asarray(rope_table()), keys[0], values[0], queries[0], out_grad[0]]
    pair, query, trig = call(
        prepare_kernel,
        [
            near((2 * KVH * slots, HD), bf16),
            near((2 * HQ * slots, HD), bf16),
            near((2 * slots, HD), f32),
        ],
        [],
        fetched,
        [near(array.shape, array.dtype) for array in fetched],
    )
    query_other = swap(query)
    pairs = [pair] + [
        exchange(pair, "ctx", 2 * step, count) for step in range(1, half)
    ]
    gate, inputs = call(
        gate_kernel,
        [near((8, rows), f32), near((slots, width), bf16)],
        [],
        [router_weight.reshape(lines, HD), routed_inputs[0]],
        [near((lines, HD), f32)],
    )
    inputs_other = swap(routed_inputs[0])
    grown, grad, stats = call(
        functools.partial(scores_kernel, slots),
        [
            near((KVH, half * slots, 2 * rows), f32),
            near((KVH, half * slots, 2 * rows), f32),
            near((4 * KVH, 2 * rows), f32),
        ],
        [gate, query, query_other, *pairs],
        cost=SCORES_COST,
    )
    coef, router, router_send = call(
        combine_kernel,
        [near((2 * KVH, 2 * rows), f32), near((lines, HD), f32), near((lines, HD), bf16)],
        [stats, swap(stats), inputs, inputs_other],
    )
    routers = [router] + [
        exchange(router_send, "ctx", 2 * step, count) for step in reversed(range(1, half))
    ]
    query_own, query_send, term_own, *terms = call(
        functools.partial(terms_kernel, slots, half),
        [
            near((HQ * slots, HD), f32),
            near((HQ * slots, HD), bf16),
            near((2 * KVH * slots, HD), f32),
        ]
        + [near((2 * KVH * slots, HD), bf16)] * (half - 1),
        [coef, grown, grad, query, query_other, *pairs],
        cost=TERMS_COST,
    )
    query_back = swap(query_send)
    terms = [
        exchange(terms[step - 1], "ctx", 2 * step, count) for step in reversed(range(1, half))
    ]
    for bit in range(groups.bit_length() - 1):
        (router,) = call(router_kernel, [near((lines, HD), f32)], routers, cost=ROUTER_COSTS[bit > 0])
        routers = [router, exchange(router, "dp", 1 << bit, groups)]
    shape = jax.ShapeDtypeStruct
    query_grad, trig = call(
        query_kernel,
        [shape((slots, HQ * HD), bf16), near((2 * slots, HD), f32)],
        [trig, query_own, query_back],
        cost=QUERY_COST,
    )
    key_grad, value_grad, router_grad = call(
        functools.partial(final_kernel, 1.0 / math.sqrt(groups * count * slots)),
        [shape((slots, KVH * HD), bf16), shape((slots, KVH * HD), bf16), shape((lines, HD), f32)],
        [trig, term_own, *routers, *terms],
    )
    return (query_grad[None], key_grad[None], value_grad[None], router_grad.reshape(width))


def solution(mesh):
    in_specs = (
        P("dp", "ctx", None),
        P("dp", "ctx", None),
        P("dp", "ctx", None),
        P("dp", "ctx", None),
        P("dp", "ctx", None),
        P(),
        P("dp", "ctx"),
    )
    out_specs = (P("dp", "ctx", None), P("dp", "ctx", None), P("dp", "ctx", None), P())
    return jax.shard_map(shards, mesh=mesh, in_specs=in_specs, out_specs=out_specs, check_vma=False)
```

```python
import functools
import math

import jax
import jax.numpy as jnp
import numpy as np
from jax import lax
from jax.experimental import pallas as pl
from jax.experimental.pallas import tpu as pltpu
from jax.sharding import PartitionSpec as P

HQ = 16
KVH = 4
HD = 128
GROUP = HQ // KVH
ROPE_BASE = 500000.0
NEG_LARGE = -1e30
VMEM_LIMIT = 32 * 1024 * 1024
SCORES_COST = 20 * 10**9
TERMS_COST = 20 * 10**9
RIDE_COST = 20 * 10**9


def rope_table():
    half = HD // 2
    frequency = [ROPE_BASE ** (-number / half) for number in range(half)]
    coarse = [256.0 * factor % (2.0 * math.pi) for factor in frequency]
    return np.asarray([coarse + coarse, frequency + frequency], np.float32)


def turn(vectors, cosine, sine):
    return vectors * cosine + pltpu.roll(vectors, HD // 2, 1) * sine


def head(number):
    return slice(number * HD, (number + 1) * HD)


def rows_of(number, depth):
    return slice(number * depth, (number + 1) * depth)


def diagonal(slots, lanes):
    row = lax.broadcasted_iota(jnp.int32, (slots, lanes), 0)
    lane = lax.broadcasted_iota(jnp.int32, (slots, lanes), 1)
    return lax.rem(lane, slots) == row


def prepare_kernel(*refs):
    place_hbm, table_hbm, key_hbm, value_hbm, query_hbm, upstream_hbm = refs[:6]
    pair_ref, query_out, trig_ref = refs[6:9]
    place_ref, table_ref, key_ref, value_ref, query_ref, upstream_ref, semaphores = refs[9:]
    slots = key_ref.shape[0]
    copies = [
        pltpu.make_async_copy(source, target, semaphores.at[at])
        for at, (source, target) in enumerate(
            [
                (place_hbm, place_ref),
                (table_hbm, table_ref),
                (key_hbm, key_ref),
                (value_hbm, value_ref),
                (query_hbm, query_ref),
                (upstream_hbm, upstream_ref),
            ]
        )
    ]
    for copy in copies:
        copy.start()
    copies[0].wait()
    place = place_ref[...]
    upper = (place >> 8).astype(jnp.float32)
    lower = (place & 255).astype(jnp.float32)
    same = diagonal(slots, slots)
    upper = jnp.sum(jnp.where(same, upper, 0.0), axis=1, keepdims=True)
    lower = jnp.sum(jnp.where(same, lower, 0.0), axis=1, keepdims=True)
    copies[1].wait()
    angles = upper * table_ref[0:1, :] + lower * table_ref[1:2, :]
    low = lax.broadcasted_iota(jnp.int32, angles.shape, 1) < HD // 2
    mixed = jnp.cos(jnp.where(low, angles, angles - 0.5 * math.pi))
    turned = pltpu.roll(mixed, HD // 2, 1)
    cosine = jnp.where(low, mixed, turned)
    sine = jnp.where(low, -turned, mixed)
    trig_ref[0:slots, :] = cosine
    trig_ref[slots : 2 * slots, :] = sine
    for copy in copies[2:]:
        copy.wait()
    for number in range(KVH):
        wide = key_ref[:, head(number)].astype(jnp.float32)
        pair_ref[rows_of(number, slots), :] = turn(wide, cosine, sine).astype(jnp.bfloat16)
        pair_ref[rows_of(KVH + number, slots), :] = value_ref[:, head(number)]
    for number in range(HQ):
        wide = query_ref[:, head(number)].astype(jnp.float32)
        query_out[rows_of(number, slots), :] = turn(wide, cosine, sine).astype(jnp.bfloat16)
        query_out[rows_of(HQ + number, slots), :] = upstream_ref[:, head(number)]


def gate_kernel(weight_hbm, input_hbm, gate_ref, input_ref, weight_ref, semaphores):
    copies = [
        pltpu.make_async_copy(weight_hbm, weight_ref, semaphores.at[0]),
        pltpu.make_async_copy(input_hbm, input_ref, semaphores.at[1]),
    ]
    for copy in copies:
        copy.start()
    for copy in copies:
        copy.wait()
    slots = input_ref.shape[0]
    blocks = weight_ref.shape[0]
    total = jnp.zeros((slots, HD), jnp.float32)
    for number in range(blocks):
        total += input_ref[:, head(number)].astype(jnp.float32) * weight_ref[number : number + 1, :]
    gate = jax.nn.sigmoid(jnp.sum(total, axis=1, keepdims=True))
    same = diagonal(slots, gate_ref.shape[1])
    gate_ref[...] = jnp.broadcast_to(
        jnp.sum(jnp.where(same, gate, 0.0), axis=0, keepdims=True), gate_ref.shape
    )


def tiles(pair_refs, query_refs, number, slots):
    rows = GROUP * slots
    key_tile = jnp.concatenate([ref[rows_of(number, slots), :] for ref in pair_refs], axis=0)
    value_tile = jnp.concatenate(
        [ref[rows_of(KVH + number, slots), :] for ref in pair_refs], axis=0
    )
    query_tile = jnp.concatenate([ref[rows_of(number, rows), :] for ref in query_refs], axis=0)
    upstream_tile = jnp.concatenate(
        [ref[rows_of(KVH + number, rows), :] for ref in query_refs], axis=0
    )
    return key_tile, value_tile, query_tile, upstream_tile


def scores_kernel(slots, *refs):
    gate_ref, own_ref, other_ref = refs[:3]
    pair_refs = refs[3:-3]
    grown_out, grad_out, stats_out = refs[-3:]
    rows = GROUP * slots
    keys_total = len(pair_refs) * slots
    own = lax.axis_index("ctx")
    other = own + 1 - 2 * lax.rem(own, 2)
    row = lax.broadcasted_iota(jnp.int32, (keys_total, 2 * rows), 0)
    lane = lax.broadcasted_iota(jnp.int32, (keys_total, 2 * rows), 1)
    owner = 2 * jnp.bitwise_xor(own // 2, row // slots) + lax.rem(own, 2)
    key_at = owner * slots + lax.rem(row, slots)
    query_at = lax.rem(lane, slots) + jnp.where(lane < rows, own, other) * slots
    bias = jnp.where(key_at <= query_at, 0.0, NEG_LARGE)
    across = (((1,), (1,)), ((), ()))
    for number in range(KVH):
        key_tile, value_tile, query_tile, upstream_tile = tiles(
            pair_refs, (own_ref, other_ref), number, slots
        )
        scores = lax.dot_general(
            key_tile, query_tile, across, preferred_element_type=jnp.float32
        )
        scores = scores * (1.0 / math.sqrt(HD)) + bias
        top = jnp.max(scores, axis=0, keepdims=True)
        grown = jnp.exp(scores - top)
        prob_grad = lax.dot_general(
            value_tile, upstream_tile, across, preferred_element_type=jnp.float32
        )
        grown_out[number] = grown
        grad_out[number] = prob_grad
        stats_out[number : number + 1, :] = top
        stats_out[KVH + number : KVH + number + 1, :] = jnp.sum(grown, axis=0, keepdims=True)
        stats_out[2 * KVH + number : 2 * KVH + number + 1, :] = jnp.sum(
            grown * prob_grad, axis=0, keepdims=True
        )
    stats_out[3 * KVH :, :] = jnp.concatenate(
        [gate_ref[0:KVH, :], jnp.zeros((KVH, rows), jnp.float32)], axis=1
    )


def combine_kernel(own_ref, other_ref, input_ref, input_other_ref, coef_out, router_out):
    slots = input_ref.shape[0]
    rows = GROUP * slots
    mine = own_ref[...]
    swapped = other_ref[...]
    theirs = jnp.concatenate([swapped[:, rows:], swapped[:, :rows]], axis=1)
    top = jnp.maximum(mine[0:KVH], theirs[0:KVH])
    mine_part = jnp.exp(mine[0:KVH] - top)
    their_part = jnp.exp(theirs[0:KVH] - top)
    mass = mine[KVH : 2 * KVH] * mine_part + theirs[KVH : 2 * KVH] * their_part
    inverse = 1.0 / mass
    inner = (
        mine[2 * KVH : 3 * KVH] * mine_part + theirs[2 * KVH : 3 * KVH] * their_part
    ) * inverse
    gate = mine[3 * KVH :] + theirs[3 * KVH :]
    coef_out[0:KVH, :] = mine_part * inverse * gate
    coef_out[KVH : 2 * KVH, :] = inner
    slope = gate[0:1] * (1.0 - gate[0:1]) * jnp.sum(inner, axis=0, keepdims=True)
    same = diagonal(slots, rows)
    own_slope = jnp.sum(jnp.where(same, slope[:, :rows], 0.0), axis=1, keepdims=True)
    other_slope = jnp.sum(jnp.where(same, slope[:, rows:], 0.0), axis=1, keepdims=True)
    for number in range(router_out.shape[0]):
        router_out[number : number + 1, :] = jnp.sum(
            own_slope * input_ref[:, head(number)].astype(jnp.float32)
            + other_slope * input_other_ref[:, head(number)].astype(jnp.float32),
            axis=0,
            keepdims=True,
        )


def terms_kernel(slots, half, *refs):
    coef_ref, grown_ref, grad_ref, own_ref, other_ref = refs[:5]
    pair_refs = refs[5 : 5 + half]
    query_out, query_send, term_own = refs[5 + half : 8 + half]
    term_refs = refs[8 + half :]
    rows = GROUP * slots
    scale = 1.0 / math.sqrt(HD)
    for number in range(KVH):
        key_tile, _, query_tile, upstream_tile = tiles(
            pair_refs, (own_ref, other_ref), number, slots
        )
        gated = grown_ref[number] * coef_ref[number : number + 1, :]
        inner = coef_ref[KVH + number : KVH + number + 1, :]
        score_grad = (gated * (grad_ref[number] - inner) * scale).astype(jnp.bfloat16)
        key_term = jnp.dot(score_grad, query_tile, preferred_element_type=jnp.float32)
        value_term = jnp.dot(
            gated.astype(jnp.bfloat16), upstream_tile, preferred_element_type=jnp.float32
        )
        key_rows, value_rows = rows_of(number, slots), rows_of(KVH + number, slots)
        term_own[key_rows, :] = key_term[0:slots]
        term_own[value_rows, :] = value_term[0:slots]
        for at, ref in enumerate(term_refs, 1):
            ref[key_rows, :] = key_term[rows_of(at, slots)].astype(jnp.bfloat16)
            ref[value_rows, :] = value_term[rows_of(at, slots)].astype(jnp.bfloat16)
        query_term = lax.dot_general(
            score_grad, key_tile, (((0,), (0,)), ((), ())), preferred_element_type=jnp.float32
        )
        query_out[rows_of(number, rows), :] = query_term[0:rows]
        query_send[rows_of(number, rows), :] = query_term[rows:].astype(jnp.bfloat16)


def ride_kernel(groups, *refs):
    router_refs = refs[:groups]
    count = (len(refs) - groups - 1) // 2
    term_refs = refs[groups : groups + count]
    router_out = refs[groups + count]
    router = router_refs[0][...]
    for ref in router_refs[1:]:
        router += ref[...]
    router_out[...] = router
    for term, out in zip(term_refs, refs[groups + count + 1 :]):
        out[0 : term.shape[0], :] = term[...]
        out[term.shape[0] :, :] = router.astype(jnp.bfloat16)


def query_kernel(trig_ref, own_ref, other_ref, query_out, trig_out):
    slots = query_out.shape[0]
    cosine = trig_ref[0:slots, :]
    sine = trig_ref[slots : 2 * slots, :]
    trig_out[...] = trig_ref[...]
    for number in range(HQ):
        part = rows_of(number, slots)
        total = own_ref[part, :] + other_ref[part, :].astype(jnp.float32)
        query_out[:, head(number)] = turn(total, cosine, -sine).astype(jnp.bfloat16)


def final_kernel(router_scale, *refs):
    trig_ref, own_ref, router_ref = refs[:3]
    term_refs = refs[3:-3]
    key_out, value_out, router_out = refs[-3:]
    slots = key_out.shape[0]
    cosine = trig_ref[0:slots, :]
    sine = trig_ref[slots : 2 * slots, :]
    for number in range(2 * KVH):
        part = rows_of(number, slots)
        total = own_ref[part, :]
        for ref in term_refs:
            total += ref[part, :].astype(jnp.float32)
        if number < KVH:
            key_out[:, head(number)] = turn(total, cosine, -sine).astype(jnp.bfloat16)
        else:
            value_out[:, head(number - KVH)] = total.astype(jnp.bfloat16)
    router = router_ref[...]
    for ref in term_refs:
        router += ref[2 * KVH * slots :, :].astype(jnp.float32)
    router_out[...] = router * router_scale


def call(kernel, outs, args, fetched=(), scratch=(), cost=None):
    local = pl.BlockSpec(memory_space=pltpu.VMEM)
    distant = pl.BlockSpec(memory_space=pl.ANY)
    scratch = list(scratch) + [pltpu.SemaphoreType.DMA((len(fetched),))] * bool(fetched)
    return pl.pallas_call(
        kernel,
        out_shape=outs,
        in_specs=[local] * len(args) + [distant] * len(fetched),
        out_specs=[local] * len(outs),
        scratch_shapes=scratch,
        compiler_params=pltpu.CompilerParams(vmem_limit_bytes=VMEM_LIMIT),
        cost_estimate=cost and pl.CostEstimate(cost, 0, 0),
    )(*args, *[pltpu.with_memory_space_constraint(array, pltpu.HBM) for array in fetched])


def exchange(array, axis, step, size):
    return lax.ppermute(array, axis, [(at, at ^ step) for at in range(size)])


def shards(queries, keys, values, out_grad, routed_inputs, router_weight, positions):
    slots = queries.shape[1]
    width = routed_inputs.shape[2]
    count = lax.axis_size("ctx")
    groups = lax.axis_size("dp")
    half = count // 2
    rows = GROUP * slots
    lines = width // HD
    bf16, f32 = jnp.bfloat16, jnp.float32

    def swap(array):
        return exchange(array, "ctx", 1, count)

    near = pltpu.VMEM
    fetched = [positions, jnp.asarray(rope_table()), keys[0], values[0], queries[0], out_grad[0]]
    pair, query, trig = call(
        prepare_kernel,
        [
            near((2 * KVH * slots, HD), bf16),
            near((2 * HQ * slots, HD), bf16),
            near((2 * slots, HD), f32),
        ],
        [],
        fetched,
        [near(array.shape, array.dtype) for array in fetched],
    )
    query_other = swap(query)
    pairs = [pair] + [
        exchange(pair, "ctx", 2 * step, count) for step in range(1, half)
    ]
    gate, inputs = call(
        gate_kernel,
        [near((8, rows), f32), near((slots, width), bf16)],
        [],
        [router_weight.reshape(lines, HD), routed_inputs[0]],
        [near((lines, HD), f32)],
    )
    inputs_other = swap(routed_inputs[0])
    grown, grad, stats = call(
        functools.partial(scores_kernel, slots),
        [
            near((KVH, half * slots, 2 * rows), f32),
            near((KVH, half * slots, 2 * rows), f32),
            near((4 * KVH, 2 * rows), f32),
        ],
        [gate, query, query_other, *pairs],
        cost=SCORES_COST,
    )
    coef, router = call(
        combine_kernel,
        [near((2 * KVH, 2 * rows), f32), near((lines, HD), f32)],
        [stats, swap(stats), inputs, inputs_other],
    )
    routers = [router] + [
        exchange(router, "dp", step, groups) for step in range(1, groups)
    ]
    query_own, query_send, term_own, *terms = call(
        functools.partial(terms_kernel, slots, half),
        [
            near((HQ * slots, HD), f32),
            near((HQ * slots, HD), bf16),
            near((2 * KVH * slots, HD), f32),
        ]
        + [near((2 * KVH * slots, HD), bf16)] * (half - 1),
        [coef, grown, grad, query, query_other, *pairs],
        cost=TERMS_COST,
    )
    query_back = swap(query_send)
    router, *terms = call(
        functools.partial(ride_kernel, groups),
        [near((lines, HD), f32)] + [near((2 * KVH * slots + lines, HD), bf16)] * (half - 1),
        [*routers, *terms],
        cost=RIDE_COST,
    )
    terms = [
        exchange(terms[step - 1], "ctx", 2 * step, count) for step in reversed(range(1, half))
    ]
    shape = jax.ShapeDtypeStruct
    query_grad, trig = call(
        query_kernel,
        [shape((slots, HQ * HD), bf16), near((2 * slots, HD), f32)],
        [trig, query_own, query_back],
    )
    key_grad, value_grad, router_grad = call(
        functools.partial(final_kernel, 1.0 / math.sqrt(groups * count * slots)),
        [shape((slots, KVH * HD), bf16), shape((slots, KVH * HD), bf16), shape((lines, HD), f32)],
        [trig, term_own, router, *terms],
    )
    return (query_grad[None], key_grad[None], value_grad[None], router_grad.reshape(width))


def solution(mesh):
    in_specs = (
        P("dp", "ctx", None),
        P("dp", "ctx", None),
        P("dp", "ctx", None),
        P("dp", "ctx", None),
        P("dp", "ctx", None),
        P(),
        P("dp", "ctx"),
    )
    out_specs = (P("dp", "ctx", None), P("dp", "ctx", None), P("dp", "ctx", None), P())
    return jax.shard_map(shards, mesh=mesh, in_specs=in_specs, out_specs=out_specs, check_vma=False)
```

```python
import functools
import math

import jax
import jax.numpy as jnp
import numpy as np
from jax import lax
from jax.experimental import pallas as pl
from jax.experimental.pallas import tpu as pltpu
from jax.sharding import PartitionSpec as P

HQ = 16
KVH = 4
HD = 128
GROUP = HQ // KVH
ROPE_BASE = 500000.0
NEG_LARGE = -1e30
VMEM_LIMIT = 32 * 1024 * 1024
CHUNKS = 4
SCORES_COST = 20 * 10**9
TERMS_COST = 20 * 10**9
RIDE_COST = 20 * 10**9


def rope_table():
    half = HD // 2
    frequency = [ROPE_BASE ** (-number / half) for number in range(half)]
    coarse = [256.0 * factor % (2.0 * math.pi) for factor in frequency]
    return np.asarray([coarse + coarse, frequency + frequency], np.float32)


def turn(vectors, cosine, sine):
    return vectors * cosine + pltpu.roll(vectors, HD // 2, 1) * sine


def head(number):
    return slice(number * HD, (number + 1) * HD)


def rows_of(number, depth):
    return slice(number * depth, (number + 1) * depth)


def diagonal(slots, lanes):
    row = lax.broadcasted_iota(jnp.int32, (slots, lanes), 0)
    lane = lax.broadcasted_iota(jnp.int32, (slots, lanes), 1)
    return lax.rem(lane, slots) == row


def prepare_kernel(*refs):
    place_hbm, table_hbm, key_hbm, value_hbm, query_hbm, upstream_hbm = refs[:6]
    pair_ref, query_out, trig_ref = refs[6:9]
    place_ref, table_ref, key_ref, value_ref, query_ref, upstream_ref, semaphores = refs[9:]
    slots = key_ref.shape[0]
    chunk = query_ref.shape[1] // CHUNKS
    parts = [slice(at * chunk, (at + 1) * chunk) for at in range(CHUNKS)]
    moves = [(place_hbm, place_ref), (table_hbm, table_ref), (key_hbm, key_ref)]
    moves += [(query_hbm.at[:, part], query_ref.at[:, part]) for part in parts]
    moves += [(value_hbm, value_ref)]
    moves += [(upstream_hbm.at[:, part], upstream_ref.at[:, part]) for part in parts]
    copies = [
        pltpu.make_async_copy(source, target, semaphores.at[at])
        for at, (source, target) in enumerate(moves)
    ]
    for copy in copies:
        copy.start()
    copies[0].wait()
    place = place_ref[...]
    upper = (place >> 8).astype(jnp.float32)
    lower = (place & 255).astype(jnp.float32)
    same = diagonal(slots, slots)
    upper = jnp.sum(jnp.where(same, upper, 0.0), axis=1, keepdims=True)
    lower = jnp.sum(jnp.where(same, lower, 0.0), axis=1, keepdims=True)
    copies[1].wait()
    angles = upper * table_ref[0:1, :] + lower * table_ref[1:2, :]
    low = lax.broadcasted_iota(jnp.int32, angles.shape, 1) < HD // 2
    mixed = jnp.cos(jnp.where(low, angles, angles - 0.5 * math.pi))
    turned = pltpu.roll(mixed, HD // 2, 1)
    cosine = jnp.where(low, mixed, turned)
    sine = jnp.where(low, -turned, mixed)
    trig_ref[0:slots, :] = cosine
    trig_ref[slots : 2 * slots, :] = sine
    copies[2].wait()
    for number in range(KVH):
        wide = key_ref[:, head(number)].astype(jnp.float32)
        pair_ref[rows_of(number, slots), :] = turn(wide, cosine, sine).astype(jnp.bfloat16)
    for number in range(HQ):
        if number % (HQ // CHUNKS) == 0:
            copies[3 + number // (HQ // CHUNKS)].wait()
        wide = query_ref[:, head(number)].astype(jnp.float32)
        query_out[rows_of(number, slots), :] = turn(wide, cosine, sine).astype(jnp.bfloat16)
    for copy in copies[3 + CHUNKS :]:
        copy.wait()
    for number in range(KVH):
        pair_ref[rows_of(KVH + number, slots), :] = value_ref[:, head(number)]
    for number in range(HQ):
        query_out[rows_of(HQ + number, slots), :] = upstream_ref[:, head(number)]


def gate_kernel(weight_hbm, input_hbm, gate_ref, input_ref, weight_ref, semaphores):
    copies = [
        pltpu.make_async_copy(weight_hbm, weight_ref, semaphores.at[0]),
        pltpu.make_async_copy(input_hbm, input_ref, semaphores.at[1]),
    ]
    for copy in copies:
        copy.start()
    for copy in copies:
        copy.wait()
    slots = input_ref.shape[0]
    blocks = weight_ref.shape[0]
    total = jnp.zeros((slots, HD), jnp.float32)
    for number in range(blocks):
        total += input_ref[:, head(number)].astype(jnp.float32) * weight_ref[number : number + 1, :]
    gate = jax.nn.sigmoid(jnp.sum(total, axis=1, keepdims=True))
    same = diagonal(slots, gate_ref.shape[1])
    gate_ref[...] = jnp.broadcast_to(
        jnp.sum(jnp.where(same, gate, 0.0), axis=0, keepdims=True), gate_ref.shape
    )


def tiles(pair_refs, query_refs, number, slots):
    rows = GROUP * slots
    key_tile = jnp.concatenate([ref[rows_of(number, slots), :] for ref in pair_refs], axis=0)
    value_tile = jnp.concatenate(
        [ref[rows_of(KVH + number, slots), :] for ref in pair_refs], axis=0
    )
    query_tile = jnp.concatenate([ref[rows_of(number, rows), :] for ref in query_refs], axis=0)
    upstream_tile = jnp.concatenate(
        [ref[rows_of(KVH + number, rows), :] for ref in query_refs], axis=0
    )
    return key_tile, value_tile, query_tile, upstream_tile


def scores_kernel(slots, *refs):
    gate_ref, own_ref, other_ref = refs[:3]
    pair_refs = refs[3:-3]
    grown_out, grad_out, stats_out = refs[-3:]
    rows = GROUP * slots
    keys_total = len(pair_refs) * slots
    own = lax.axis_index("ctx")
    other = own + 1 - 2 * lax.rem(own, 2)
    row = lax.broadcasted_iota(jnp.int32, (keys_total, 2 * rows), 0)
    lane = lax.broadcasted_iota(jnp.int32, (keys_total, 2 * rows), 1)
    owner = 2 * jnp.bitwise_xor(own // 2, row // slots) + lax.rem(own, 2)
    key_at = owner * slots + lax.rem(row, slots)
    query_at = lax.rem(lane, slots) + jnp.where(lane < rows, own, other) * slots
    bias = jnp.where(key_at <= query_at, 0.0, NEG_LARGE)
    across = (((1,), (1,)), ((), ()))
    for number in range(KVH):
        key_tile, value_tile, query_tile, upstream_tile = tiles(
            pair_refs, (own_ref, other_ref), number, slots
        )
        scores = lax.dot_general(
            key_tile, query_tile, across, preferred_element_type=jnp.float32
        )
        scores = scores * (1.0 / math.sqrt(HD)) + bias
        top = jnp.max(scores, axis=0, keepdims=True)
        grown = jnp.exp(scores - top)
        prob_grad = lax.dot_general(
            value_tile, upstream_tile, across, preferred_element_type=jnp.float32
        )
        grown_out[number] = grown
        grad_out[number] = prob_grad
        stats_out[number : number + 1, :] = top
        stats_out[KVH + number : KVH + number + 1, :] = jnp.sum(grown, axis=0, keepdims=True)
        stats_out[2 * KVH + number : 2 * KVH + number + 1, :] = jnp.sum(
            grown * prob_grad, axis=0, keepdims=True
        )
    stats_out[3 * KVH :, :] = jnp.concatenate(
        [gate_ref[0:KVH, :], jnp.zeros((KVH, rows), jnp.float32)], axis=1
    )


def combine_kernel(own_ref, other_ref, input_ref, input_other_ref, coef_out, router_out):
    slots = input_ref.shape[0]
    rows = GROUP * slots
    mine = own_ref[...]
    swapped = other_ref[...]
    theirs = jnp.concatenate([swapped[:, rows:], swapped[:, :rows]], axis=1)
    top = jnp.maximum(mine[0:KVH], theirs[0:KVH])
    mine_part = jnp.exp(mine[0:KVH] - top)
    their_part = jnp.exp(theirs[0:KVH] - top)
    mass = mine[KVH : 2 * KVH] * mine_part + theirs[KVH : 2 * KVH] * their_part
    inverse = 1.0 / mass
    inner = (
        mine[2 * KVH : 3 * KVH] * mine_part + theirs[2 * KVH : 3 * KVH] * their_part
    ) * inverse
    gate = mine[3 * KVH :] + theirs[3 * KVH :]
    coef_out[0:KVH, :] = mine_part * inverse * gate
    coef_out[KVH : 2 * KVH, :] = inner
    slope = gate[0:1] * (1.0 - gate[0:1]) * jnp.sum(inner, axis=0, keepdims=True)
    same = diagonal(slots, rows)
    own_slope = jnp.sum(jnp.where(same, slope[:, :rows], 0.0), axis=1, keepdims=True)
    other_slope = jnp.sum(jnp.where(same, slope[:, rows:], 0.0), axis=1, keepdims=True)
    for number in range(router_out.shape[0]):
        router_out[number : number + 1, :] = jnp.sum(
            own_slope * input_ref[:, head(number)].astype(jnp.float32)
            + other_slope * input_other_ref[:, head(number)].astype(jnp.float32),
            axis=0,
            keepdims=True,
        )


def terms_kernel(slots, half, *refs):
    coef_ref, grown_ref, grad_ref, own_ref, other_ref = refs[:5]
    pair_refs = refs[5 : 5 + half]
    query_out, query_send, term_own = refs[5 + half : 8 + half]
    term_refs = refs[8 + half :]
    rows = GROUP * slots
    scale = 1.0 / math.sqrt(HD)
    for number in range(KVH):
        key_tile, _, query_tile, upstream_tile = tiles(
            pair_refs, (own_ref, other_ref), number, slots
        )
        gated = grown_ref[number] * coef_ref[number : number + 1, :]
        inner = coef_ref[KVH + number : KVH + number + 1, :]
        score_grad = (gated * (grad_ref[number] - inner) * scale).astype(jnp.bfloat16)
        key_term = jnp.dot(score_grad, query_tile, preferred_element_type=jnp.float32)
        value_term = jnp.dot(
            gated.astype(jnp.bfloat16), upstream_tile, preferred_element_type=jnp.float32
        )
        key_rows, value_rows = rows_of(number, slots), rows_of(KVH + number, slots)
        term_own[key_rows, :] = key_term[0:slots]
        term_own[value_rows, :] = value_term[0:slots]
        for at, ref in enumerate(term_refs, 1):
            ref[key_rows, :] = key_term[rows_of(at, slots)].astype(jnp.bfloat16)
            ref[value_rows, :] = value_term[rows_of(at, slots)].astype(jnp.bfloat16)
        query_term = lax.dot_general(
            score_grad, key_tile, (((0,), (0,)), ((), ())), preferred_element_type=jnp.float32
        )
        query_out[rows_of(number, rows), :] = query_term[0:rows]
        query_send[rows_of(number, rows), :] = query_term[rows:].astype(jnp.bfloat16)


def ride_kernel(groups, *refs):
    router_refs = refs[:groups]
    count = (len(refs) - groups - 1) // 2
    term_refs = refs[groups : groups + count]
    router_out = refs[groups + count]
    router = router_refs[0][...]
    for ref in router_refs[1:]:
        router += ref[...]
    router_out[...] = router
    for term, out in zip(term_refs, refs[groups + count + 1 :]):
        out[0 : term.shape[0], :] = term[...]
        out[term.shape[0] :, :] = router.astype(jnp.bfloat16)


def query_kernel(trig_ref, own_ref, other_ref, query_out, trig_out):
    slots = query_out.shape[0]
    cosine = trig_ref[0:slots, :]
    sine = trig_ref[slots : 2 * slots, :]
    trig_out[...] = trig_ref[...]
    for number in range(HQ):
        part = rows_of(number, slots)
        total = own_ref[part, :] + other_ref[part, :].astype(jnp.float32)
        query_out[:, head(number)] = turn(total, cosine, -sine).astype(jnp.bfloat16)


def final_kernel(router_scale, *refs):
    trig_ref, own_ref, router_ref = refs[:3]
    term_refs = refs[3:-7]
    results = refs[-7:-4]
    key_out, value_out, router_out, semaphores = refs[-4:]
    copies = [
        pltpu.make_async_copy(source, target, semaphores.at[at])
        for at, (source, target) in enumerate(zip((key_out, value_out, router_out), results))
    ]
    slots = key_out.shape[0]
    router = router_ref[...]
    for ref in term_refs:
        router += ref[2 * KVH * slots :, :].astype(jnp.float32)
    router_out[...] = router * router_scale
    copies[2].start()

    def total(number):
        part = rows_of(number, slots)
        result = own_ref[part, :]
        for ref in term_refs:
            result += ref[part, :].astype(jnp.float32)
        return result

    for number in range(KVH):
        value_out[:, head(number)] = total(KVH + number).astype(jnp.bfloat16)
    copies[1].start()
    cosine = trig_ref[0:slots, :]
    sine = trig_ref[slots : 2 * slots, :]
    for number in range(KVH):
        key_out[:, head(number)] = turn(total(number), cosine, -sine).astype(jnp.bfloat16)
    copies[0].start()
    for copy in copies:
        copy.wait()


def call(kernel, outs, args, fetched=(), scratch=(), cost=None, copies=0, kept=0):
    local = pl.BlockSpec(memory_space=pltpu.VMEM)
    distant = pl.BlockSpec(memory_space=pl.ANY)
    scratch = list(scratch) + [pltpu.SemaphoreType.DMA((copies,))] * bool(copies)
    return pl.pallas_call(
        kernel,
        out_shape=outs,
        in_specs=[local] * len(args) + [distant] * len(fetched),
        out_specs=[distant] * kept + [local] * (len(outs) - kept),
        scratch_shapes=scratch,
        compiler_params=pltpu.CompilerParams(vmem_limit_bytes=VMEM_LIMIT),
        cost_estimate=cost and pl.CostEstimate(cost, 0, 0),
    )(*args, *[pltpu.with_memory_space_constraint(array, pltpu.HBM) for array in fetched])


def exchange(array, axis, step, size):
    return lax.ppermute(array, axis, [(at, at ^ step) for at in range(size)])


def shards(queries, keys, values, out_grad, routed_inputs, router_weight, positions):
    slots = queries.shape[1]
    width = routed_inputs.shape[2]
    count = lax.axis_size("ctx")
    groups = lax.axis_size("dp")
    half = count // 2
    rows = GROUP * slots
    lines = width // HD
    bf16, f32 = jnp.bfloat16, jnp.float32

    def swap(array):
        return exchange(array, "ctx", 1, count)

    near = pltpu.VMEM
    fetched = [positions, jnp.asarray(rope_table()), keys[0], values[0], queries[0], out_grad[0]]
    pair, query, trig = call(
        prepare_kernel,
        [
            near((2 * KVH * slots, HD), bf16),
            near((2 * HQ * slots, HD), bf16),
            near((2 * slots, HD), f32),
        ],
        [],
        fetched,
        [near(array.shape, array.dtype) for array in fetched],
        copies=4 + 2 * CHUNKS,
    )
    query_other = swap(query)
    pairs = [pair] + [
        exchange(pair, "ctx", 2 * step, count) for step in range(1, half)
    ]
    gate, inputs = call(
        gate_kernel,
        [near((8, rows), f32), near((slots, width), bf16)],
        [],
        [router_weight.reshape(lines, HD), routed_inputs[0]],
        [near((lines, HD), f32)],
        copies=2,
    )
    inputs_other = swap(routed_inputs[0])
    grown, grad, stats = call(
        functools.partial(scores_kernel, slots),
        [
            near((KVH, half * slots, 2 * rows), f32),
            near((KVH, half * slots, 2 * rows), f32),
            near((4 * KVH, 2 * rows), f32),
        ],
        [gate, query, query_other, *pairs],
        cost=SCORES_COST,
    )
    coef, router = call(
        combine_kernel,
        [near((2 * KVH, 2 * rows), f32), near((lines, HD), f32)],
        [stats, swap(stats), inputs, inputs_other],
    )
    routers = [router] + [
        exchange(router, "dp", step, groups) for step in range(1, groups)
    ]
    query_own, query_send, term_own, *terms = call(
        functools.partial(terms_kernel, slots, half),
        [
            near((HQ * slots, HD), f32),
            near((HQ * slots, HD), bf16),
            near((2 * KVH * slots, HD), f32),
        ]
        + [near((2 * KVH * slots, HD), bf16)] * (half - 1),
        [coef, grown, grad, query, query_other, *pairs],
        cost=TERMS_COST,
    )
    query_back = swap(query_send)
    router, *terms = call(
        functools.partial(ride_kernel, groups),
        [near((lines, HD), f32)] + [near((2 * KVH * slots + lines, HD), bf16)] * (half - 1),
        [*routers, *terms],
        cost=RIDE_COST,
    )
    terms = [
        exchange(terms[step - 1], "ctx", 2 * step, count) for step in reversed(range(1, half))
    ]
    shape = jax.ShapeDtypeStruct
    query_grad, trig = call(
        query_kernel,
        [shape((slots, HQ * HD), bf16), near((2 * slots, HD), f32)],
        [trig, query_own, query_back],
    )
    key_grad, value_grad, router_grad = call(
        functools.partial(final_kernel, 1.0 / math.sqrt(groups * count * slots)),
        [shape((slots, KVH * HD), bf16), shape((slots, KVH * HD), bf16), shape((lines, HD), f32)],
        [trig, term_own, router, *terms],
        scratch=[
            near((slots, KVH * HD), bf16),
            near((slots, KVH * HD), bf16),
            near((lines, HD), f32),
        ],
        copies=3,
        kept=3,
    )
    return (query_grad[None], key_grad[None], value_grad[None], router_grad.reshape(width))


def solution(mesh):
    in_specs = (
        P("dp", "ctx", None),
        P("dp", "ctx", None),
        P("dp", "ctx", None),
        P("dp", "ctx", None),
        P("dp", "ctx", None),
        P(),
        P("dp", "ctx"),
    )
    out_specs = (P("dp", "ctx", None), P("dp", "ctx", None), P("dp", "ctx", None), P())
    return jax.shard_map(shards, mesh=mesh, in_specs=in_specs, out_specs=out_specs, check_vma=False)
```

```python
import functools
import math

import jax
import jax.numpy as jnp
import numpy as np
from jax import lax
from jax.experimental import pallas as pl
from jax.experimental.pallas import tpu as pltpu
from jax.sharding import PartitionSpec as P

HQ = 16
KVH = 4
HD = 128
GROUP = HQ // KVH
ROPE_BASE = 500000.0
NEG_LARGE = -1e30
VMEM_LIMIT = 32 * 1024 * 1024
SCORES_COST = 20 * 10**9
TERMS_COST = 20 * 10**9
RIDE_COST = 10**9
QUERY_COST = 5 * 10**8


def rope_table():
    half = HD // 2
    frequency = [ROPE_BASE ** (-number / half) for number in range(half)]
    coarse = [256.0 * factor % (2.0 * math.pi) for factor in frequency]
    return np.asarray([coarse + coarse, frequency + frequency], np.float32)


def turn(vectors, cosine, sine):
    return vectors * cosine + pltpu.roll(vectors, HD // 2, 1) * sine


def head(number):
    return slice(number * HD, (number + 1) * HD)


def rows_of(number, depth):
    return slice(number * depth, (number + 1) * depth)


def diagonal(slots, lanes):
    row = lax.broadcasted_iota(jnp.int32, (slots, lanes), 0)
    lane = lax.broadcasted_iota(jnp.int32, (slots, lanes), 1)
    return lax.rem(lane, slots) == row


def prepare_kernel(*refs):
    place_hbm, table_hbm, key_hbm, value_hbm, query_hbm, upstream_hbm = refs[:6]
    pair_ref, query_out, trig_ref = refs[6:9]
    place_ref, table_ref, key_ref, value_ref, query_ref, upstream_ref, semaphores = refs[9:]
    slots = key_ref.shape[0]
    copies = [
        pltpu.make_async_copy(source, target, semaphores.at[at])
        for at, (source, target) in enumerate(
            [
                (place_hbm, place_ref),
                (table_hbm, table_ref),
                (key_hbm, key_ref),
                (value_hbm, value_ref),
                (query_hbm, query_ref),
                (upstream_hbm, upstream_ref),
            ]
        )
    ]
    for copy in copies:
        copy.start()
    copies[0].wait()
    place = place_ref[...]
    upper = (place >> 8).astype(jnp.float32)
    lower = (place & 255).astype(jnp.float32)
    same = diagonal(slots, slots)
    upper = jnp.sum(jnp.where(same, upper, 0.0), axis=1, keepdims=True)
    lower = jnp.sum(jnp.where(same, lower, 0.0), axis=1, keepdims=True)
    copies[1].wait()
    angles = upper * table_ref[0:1, :] + lower * table_ref[1:2, :]
    low = lax.broadcasted_iota(jnp.int32, angles.shape, 1) < HD // 2
    mixed = jnp.cos(jnp.where(low, angles, angles - 0.5 * math.pi))
    turned = pltpu.roll(mixed, HD // 2, 1)
    cosine = jnp.where(low, mixed, turned)
    sine = jnp.where(low, -turned, mixed)
    trig_ref[0:slots, :] = cosine
    trig_ref[slots : 2 * slots, :] = sine
    for copy in copies[2:]:
        copy.wait()
    for number in range(KVH):
        wide = key_ref[:, head(number)].astype(jnp.float32)
        pair_ref[rows_of(number, slots), :] = turn(wide, cosine, sine).astype(jnp.bfloat16)
        pair_ref[rows_of(KVH + number, slots), :] = value_ref[:, head(number)]
    for number in range(HQ):
        wide = query_ref[:, head(number)].astype(jnp.float32)
        query_out[rows_of(number, slots), :] = turn(wide, cosine, sine).astype(jnp.bfloat16)
        query_out[rows_of(HQ + number, slots), :] = upstream_ref[:, head(number)]


def gate_kernel(weight_hbm, input_hbm, gate_ref, input_ref, weight_ref, semaphores):
    copies = [
        pltpu.make_async_copy(weight_hbm, weight_ref, semaphores.at[0]),
        pltpu.make_async_copy(input_hbm, input_ref, semaphores.at[1]),
    ]
    for copy in copies:
        copy.start()
    for copy in copies:
        copy.wait()
    slots = input_ref.shape[0]
    blocks = weight_ref.shape[0]
    total = jnp.zeros((slots, HD), jnp.float32)
    for number in range(blocks):
        total += input_ref[:, head(number)].astype(jnp.float32) * weight_ref[number : number + 1, :]
    gate = jax.nn.sigmoid(jnp.sum(total, axis=1, keepdims=True))
    same = diagonal(slots, gate_ref.shape[1])
    gate_ref[...] = jnp.broadcast_to(
        jnp.sum(jnp.where(same, gate, 0.0), axis=0, keepdims=True), gate_ref.shape
    )


def tiles(pair_refs, query_refs, number, slots):
    rows = GROUP * slots
    key_tile = jnp.concatenate([ref[rows_of(number, slots), :] for ref in pair_refs], axis=0)
    value_tile = jnp.concatenate(
        [ref[rows_of(KVH + number, slots), :] for ref in pair_refs], axis=0
    )
    query_tile = jnp.concatenate([ref[rows_of(number, rows), :] for ref in query_refs], axis=0)
    upstream_tile = jnp.concatenate(
        [ref[rows_of(KVH + number, rows), :] for ref in query_refs], axis=0
    )
    return key_tile, value_tile, query_tile, upstream_tile


def scores_kernel(slots, *refs):
    gate_ref, own_ref, other_ref = refs[:3]
    pair_refs = refs[3:-3]
    grown_out, grad_out, stats_out = refs[-3:]
    rows = GROUP * slots
    keys_total = len(pair_refs) * slots
    own = lax.axis_index("ctx")
    other = own + 1 - 2 * lax.rem(own, 2)
    row = lax.broadcasted_iota(jnp.int32, (keys_total, 2 * rows), 0)
    lane = lax.broadcasted_iota(jnp.int32, (keys_total, 2 * rows), 1)
    owner = 2 * jnp.bitwise_xor(own // 2, row // slots) + lax.rem(own, 2)
    key_at = owner * slots + lax.rem(row, slots)
    query_at = lax.rem(lane, slots) + jnp.where(lane < rows, own, other) * slots
    bias = jnp.where(key_at <= query_at, 0.0, NEG_LARGE)
    across = (((1,), (1,)), ((), ()))
    for number in range(KVH):
        key_tile, value_tile, query_tile, upstream_tile = tiles(
            pair_refs, (own_ref, other_ref), number, slots
        )
        scores = lax.dot_general(
            key_tile, query_tile, across, preferred_element_type=jnp.float32
        )
        scores = scores * (1.0 / math.sqrt(HD)) + bias
        top = jnp.max(scores, axis=0, keepdims=True)
        grown = jnp.exp(scores - top)
        prob_grad = lax.dot_general(
            value_tile, upstream_tile, across, preferred_element_type=jnp.float32
        )
        grown_out[number] = grown
        grad_out[number] = prob_grad
        stats_out[number : number + 1, :] = top
        stats_out[KVH + number : KVH + number + 1, :] = jnp.sum(grown, axis=0, keepdims=True)
        stats_out[2 * KVH + number : 2 * KVH + number + 1, :] = jnp.sum(
            grown * prob_grad, axis=0, keepdims=True
        )
    stats_out[3 * KVH :, :] = jnp.concatenate(
        [gate_ref[0:KVH, :], jnp.zeros((KVH, rows), jnp.float32)], axis=1
    )


def combine_kernel(own_ref, other_ref, input_ref, input_other_ref, coef_out, router_out):
    slots = input_ref.shape[0]
    rows = GROUP * slots
    mine = own_ref[...]
    swapped = other_ref[...]
    theirs = jnp.concatenate([swapped[:, rows:], swapped[:, :rows]], axis=1)
    top = jnp.maximum(mine[0:KVH], theirs[0:KVH])
    mine_part = jnp.exp(mine[0:KVH] - top)
    their_part = jnp.exp(theirs[0:KVH] - top)
    mass = mine[KVH : 2 * KVH] * mine_part + theirs[KVH : 2 * KVH] * their_part
    inverse = 1.0 / mass
    inner = (
        mine[2 * KVH : 3 * KVH] * mine_part + theirs[2 * KVH : 3 * KVH] * their_part
    ) * inverse
    gate = mine[3 * KVH :] + theirs[3 * KVH :]
    coef_out[0:KVH, :] = mine_part * inverse * gate
    coef_out[KVH : 2 * KVH, :] = inner
    slope = gate[0:1] * (1.0 - gate[0:1]) * jnp.sum(inner, axis=0, keepdims=True)
    same = diagonal(slots, rows)
    own_slope = jnp.sum(jnp.where(same, slope[:, :rows], 0.0), axis=1, keepdims=True)
    other_slope = jnp.sum(jnp.where(same, slope[:, rows:], 0.0), axis=1, keepdims=True)
    for number in range(router_out.shape[0]):
        router_out[number : number + 1, :] = jnp.sum(
            own_slope * input_ref[:, head(number)].astype(jnp.float32)
            + other_slope * input_other_ref[:, head(number)].astype(jnp.float32),
            axis=0,
            keepdims=True,
        )


def terms_kernel(slots, half, *refs):
    coef_ref, grown_ref, grad_ref, own_ref, other_ref = refs[:5]
    pair_refs = refs[5 : 5 + half]
    query_out, query_send, term_own = refs[5 + half : 8 + half]
    term_refs = refs[8 + half :]
    rows = GROUP * slots
    scale = 1.0 / math.sqrt(HD)
    for number in range(KVH):
        key_tile, _, query_tile, upstream_tile = tiles(
            pair_refs, (own_ref, other_ref), number, slots
        )
        gated = grown_ref[number] * coef_ref[number : number + 1, :]
        inner = coef_ref[KVH + number : KVH + number + 1, :]
        score_grad = (gated * (grad_ref[number] - inner) * scale).astype(jnp.bfloat16)
        key_term = jnp.dot(score_grad, query_tile, preferred_element_type=jnp.float32)
        value_term = jnp.dot(
            gated.astype(jnp.bfloat16), upstream_tile, preferred_element_type=jnp.float32
        )
        key_rows, value_rows = rows_of(number, slots), rows_of(KVH + number, slots)
        term_own[key_rows, :] = key_term[0:slots]
        term_own[value_rows, :] = value_term[0:slots]
        for at, ref in enumerate(term_refs, 1):
            ref[key_rows, :] = key_term[rows_of(at, slots)].astype(jnp.bfloat16)
            ref[value_rows, :] = value_term[rows_of(at, slots)].astype(jnp.bfloat16)
        query_term = lax.dot_general(
            score_grad, key_tile, (((0,), (0,)), ((), ())), preferred_element_type=jnp.float32
        )
        query_out[rows_of(number, rows), :] = query_term[0:rows]
        query_send[rows_of(number, rows), :] = query_term[rows:].astype(jnp.bfloat16)


def ride_kernel(groups, *refs):
    count = (len(refs) - groups - 2) // 2
    term_refs = refs[groups : groups + count]
    router_out, send_out = refs[groups + count : groups + count + 2]
    router = refs[0][...]
    for ref in refs[1:groups]:
        router += ref[...]
    router_out[...] = router
    narrow = router.astype(jnp.bfloat16)
    send_out[...] = narrow
    for term, out in zip(term_refs, refs[groups + count + 2 :]):
        out[0 : term.shape[0], :] = term[...]
        out[term.shape[0] :, :] = narrow


def query_kernel(trig_ref, own_ref, other_ref, far_ref, term_ref, query_out, trig_out, term_out):
    slots = query_out.shape[0]
    cosine = trig_ref[0:slots, :]
    sine = trig_ref[slots : 2 * slots, :]
    trig_out[...] = trig_ref[...]
    term_out[...] = term_ref[...] + far_ref[...].astype(jnp.float32)
    for number in range(HQ):
        part = rows_of(number, slots)
        total = own_ref[part, :] + other_ref[part, :].astype(jnp.float32)
        query_out[:, head(number)] = turn(total, cosine, -sine).astype(jnp.bfloat16)


def final_kernel(router_scale, *refs):
    trig_ref, own_ref, router_ref, alone_ref = refs[:4]
    term_refs = refs[4:-3]
    key_out, value_out, router_out = refs[-3:]
    slots = key_out.shape[0]
    cosine = trig_ref[0:slots, :]
    sine = trig_ref[slots : 2 * slots, :]
    for number in range(2 * KVH):
        part = rows_of(number, slots)
        total = own_ref[part, :]
        for ref in term_refs:
            total += ref[part, :].astype(jnp.float32)
        if number < KVH:
            key_out[:, head(number)] = turn(total, cosine, -sine).astype(jnp.bfloat16)
        else:
            value_out[:, head(number - KVH)] = total.astype(jnp.bfloat16)
    router = router_ref[...] + alone_ref[...].astype(jnp.float32)
    for ref in term_refs:
        router += ref[2 * KVH * slots :, :].astype(jnp.float32)
    router_out[...] = router * router_scale


def call(kernel, outs, args, fetched=(), scratch=(), cost=None):
    local = pl.BlockSpec(memory_space=pltpu.VMEM)
    distant = pl.BlockSpec(memory_space=pl.ANY)
    scratch = list(scratch) + [pltpu.SemaphoreType.DMA((len(fetched),))] * bool(fetched)
    return pl.pallas_call(
        kernel,
        out_shape=outs,
        in_specs=[local] * len(args) + [distant] * len(fetched),
        out_specs=[local] * len(outs),
        scratch_shapes=scratch,
        compiler_params=pltpu.CompilerParams(vmem_limit_bytes=VMEM_LIMIT),
        cost_estimate=cost and pl.CostEstimate(cost, 0, 0),
    )(*args, *[pltpu.with_memory_space_constraint(array, pltpu.HBM) for array in fetched])


def exchange(array, axis, step, size):
    return lax.ppermute(array, axis, [(at, at ^ step) for at in range(size)])


def shards(queries, keys, values, out_grad, routed_inputs, router_weight, positions):
    slots = queries.shape[1]
    width = routed_inputs.shape[2]
    count = lax.axis_size("ctx")
    groups = lax.axis_size("dp")
    half = count // 2
    rows = GROUP * slots
    lines = width // HD
    bf16, f32 = jnp.bfloat16, jnp.float32

    def swap(array):
        return exchange(array, "ctx", 1, count)

    near = pltpu.VMEM
    fetched = [positions, jnp.asarray(rope_table()), keys[0], values[0], queries[0], out_grad[0]]
    pair, query, trig = call(
        prepare_kernel,
        [
            near((2 * KVH * slots, HD), bf16),
            near((2 * HQ * slots, HD), bf16),
            near((2 * slots, HD), f32),
        ],
        [],
        fetched,
        [near(array.shape, array.dtype) for array in fetched],
    )
    query_other = swap(query)
    pairs = [pair] + [
        exchange(pair, "ctx", 2 * step, count) for step in range(1, half)
    ]
    gate, inputs = call(
        gate_kernel,
        [near((8, rows), f32), near((slots, width), bf16)],
        [],
        [router_weight.reshape(lines, HD), routed_inputs[0]],
        [near((lines, HD), f32)],
    )
    inputs_other = swap(routed_inputs[0])
    grown, grad, stats = call(
        functools.partial(scores_kernel, slots),
        [
            near((KVH, half * slots, 2 * rows), f32),
            near((KVH, half * slots, 2 * rows), f32),
            near((4 * KVH, 2 * rows), f32),
        ],
        [gate, query, query_other, *pairs],
        cost=SCORES_COST,
    )
    coef, router = call(
        combine_kernel,
        [near((2 * KVH, 2 * rows), f32), near((lines, HD), f32)],
        [stats, swap(stats), inputs, inputs_other],
    )
    routers = [router] + [
        exchange(router, "dp", step, groups) for step in range(1, groups)
    ]
    query_own, query_send, term_own, *terms = call(
        functools.partial(terms_kernel, slots, half),
        [
            near((HQ * slots, HD), f32),
            near((HQ * slots, HD), bf16),
            near((2 * KVH * slots, HD), f32),
        ]
        + [near((2 * KVH * slots, HD), bf16)] * (half - 1),
        [coef, grown, grad, query, query_other, *pairs],
        cost=TERMS_COST,
    )
    query_back = swap(query_send)
    far = exchange(terms[-1], "ctx", 2 * (half - 1), count)
    router, router_send, *terms = call(
        functools.partial(ride_kernel, groups),
        [near((lines, HD), f32), near((lines, HD), bf16)]
        + [near((2 * KVH * slots + lines, HD), bf16)] * (half - 2),
        [*routers, *terms[:-1]],
        cost=RIDE_COST,
    )
    terms = [
        exchange(terms[step - 1], "ctx", 2 * step, count) for step in reversed(range(1, half - 1))
    ]
    alone = exchange(router_send, "ctx", 2 * (half - 1), count)
    shape = jax.ShapeDtypeStruct
    query_grad, trig, term_own = call(
        query_kernel,
        [
            shape((slots, HQ * HD), bf16),
            near((2 * slots, HD), f32),
            near((2 * KVH * slots, HD), f32),
        ],
        [trig, query_own, query_back, far, term_own],
        cost=QUERY_COST,
    )
    key_grad, value_grad, router_grad = call(
        functools.partial(final_kernel, 1.0 / math.sqrt(groups * count * slots)),
        [shape((slots, KVH * HD), bf16), shape((slots, KVH * HD), bf16), shape((lines, HD), f32)],
        [trig, term_own, router, alone, *terms],
    )
    return (query_grad[None], key_grad[None], value_grad[None], router_grad.reshape(width))


def solution(mesh):
    in_specs = (
        P("dp", "ctx", None),
        P("dp", "ctx", None),
        P("dp", "ctx", None),
        P("dp", "ctx", None),
        P("dp", "ctx", None),
        P(),
        P("dp", "ctx"),
    )
    out_specs = (P("dp", "ctx", None), P("dp", "ctx", None), P("dp", "ctx", None), P())
    return jax.shard_map(shards, mesh=mesh, in_specs=in_specs, out_specs=out_specs, check_vma=False)
```

```python
import functools
import math

import jax
import jax.numpy as jnp
import numpy as np
from jax import lax
from jax.experimental import pallas as pl
from jax.experimental.pallas import tpu as pltpu
from jax.sharding import PartitionSpec as P

HQ = 16
KVH = 4
HD = 128
GROUP = HQ // KVH
ROPE_BASE = 500000.0
NEG_LARGE = -1e30
VMEM_LIMIT = 32 * 1024 * 1024
SCORES_COST = 20 * 10**9
TERMS_COST = 20 * 10**9
RIDE_COST = 20 * 10**9
QUERY_COST = 5 * 10**8


def rope_table():
    half = HD // 2
    frequency = [ROPE_BASE ** (-number / half) for number in range(half)]
    coarse = [256.0 * factor % (2.0 * math.pi) for factor in frequency]
    return np.asarray([coarse + coarse, frequency + frequency], np.float32)


def turn(vectors, cosine, sine):
    return vectors * cosine + pltpu.roll(vectors, HD // 2, 1) * sine


def head(number):
    return slice(number * HD, (number + 1) * HD)


def rows_of(number, depth):
    return slice(number * depth, (number + 1) * depth)


def diagonal(slots, lanes):
    row = lax.broadcasted_iota(jnp.int32, (slots, lanes), 0)
    lane = lax.broadcasted_iota(jnp.int32, (slots, lanes), 1)
    return lax.rem(lane, slots) == row


def prepare_kernel(*refs):
    place_hbm, table_hbm, key_hbm, value_hbm, query_hbm, upstream_hbm = refs[:6]
    pair_ref, query_out, trig_ref = refs[6:9]
    place_ref, table_ref, key_ref, value_ref, query_ref, upstream_ref, semaphores = refs[9:]
    slots = key_ref.shape[0]
    copies = [
        pltpu.make_async_copy(source, target, semaphores.at[at])
        for at, (source, target) in enumerate(
            [
                (place_hbm, place_ref),
                (table_hbm, table_ref),
                (key_hbm, key_ref),
                (value_hbm, value_ref),
                (query_hbm, query_ref),
                (upstream_hbm, upstream_ref),
            ]
        )
    ]
    for copy in copies:
        copy.start()
    copies[0].wait()
    place = place_ref[...]
    upper = (place >> 8).astype(jnp.float32)
    lower = (place & 255).astype(jnp.float32)
    same = diagonal(slots, slots)
    upper = jnp.sum(jnp.where(same, upper, 0.0), axis=1, keepdims=True)
    lower = jnp.sum(jnp.where(same, lower, 0.0), axis=1, keepdims=True)
    copies[1].wait()
    angles = upper * table_ref[0:1, :] + lower * table_ref[1:2, :]
    low = lax.broadcasted_iota(jnp.int32, angles.shape, 1) < HD // 2
    mixed = jnp.cos(jnp.where(low, angles, angles - 0.5 * math.pi))
    turned = pltpu.roll(mixed, HD // 2, 1)
    cosine = jnp.where(low, mixed, turned)
    sine = jnp.where(low, -turned, mixed)
    trig_ref[0:slots, :] = cosine
    trig_ref[slots : 2 * slots, :] = sine
    for copy in copies[2:]:
        copy.wait()
    for number in range(KVH):
        wide = key_ref[:, head(number)].astype(jnp.float32)
        pair_ref[rows_of(number, slots), :] = turn(wide, cosine, sine).astype(jnp.bfloat16)
        pair_ref[rows_of(KVH + number, slots), :] = value_ref[:, head(number)]
    for number in range(HQ):
        wide = query_ref[:, head(number)].astype(jnp.float32)
        query_out[rows_of(number, slots), :] = turn(wide, cosine, sine).astype(jnp.bfloat16)
        query_out[rows_of(HQ + number, slots), :] = upstream_ref[:, head(number)]


def gate_kernel(weight_hbm, input_hbm, gate_ref, input_ref, weight_ref, semaphores):
    copies = [
        pltpu.make_async_copy(weight_hbm, weight_ref, semaphores.at[0]),
        pltpu.make_async_copy(input_hbm, input_ref, semaphores.at[1]),
    ]
    for copy in copies:
        copy.start()
    for copy in copies:
        copy.wait()
    slots = input_ref.shape[0]
    blocks = weight_ref.shape[0]
    total = jnp.zeros((slots, HD), jnp.float32)
    for number in range(blocks):
        total += input_ref[:, head(number)].astype(jnp.float32) * weight_ref[number : number + 1, :]
    gate = jax.nn.sigmoid(jnp.sum(total, axis=1, keepdims=True))
    same = diagonal(slots, gate_ref.shape[1])
    gate_ref[...] = jnp.broadcast_to(
        jnp.sum(jnp.where(same, gate, 0.0), axis=0, keepdims=True), gate_ref.shape
    )


def tiles(pair_refs, query_refs, number, slots):
    rows = GROUP * slots
    key_tile = jnp.concatenate([ref[rows_of(number, slots), :] for ref in pair_refs], axis=0)
    value_tile = jnp.concatenate(
        [ref[rows_of(KVH + number, slots), :] for ref in pair_refs], axis=0
    )
    query_tile = jnp.concatenate([ref[rows_of(number, rows), :] for ref in query_refs], axis=0)
    upstream_tile = jnp.concatenate(
        [ref[rows_of(KVH + number, rows), :] for ref in query_refs], axis=0
    )
    return key_tile, value_tile, query_tile, upstream_tile


def scores_kernel(slots, *refs):
    gate_ref, own_ref, other_ref = refs[:3]
    pair_refs = refs[3:-3]
    grown_out, grad_out, stats_out = refs[-3:]
    rows = GROUP * slots
    keys_total = len(pair_refs) * slots
    own = lax.axis_index("ctx")
    other = own + 1 - 2 * lax.rem(own, 2)
    row = lax.broadcasted_iota(jnp.int32, (keys_total, 2 * rows), 0)
    lane = lax.broadcasted_iota(jnp.int32, (keys_total, 2 * rows), 1)
    owner = 2 * jnp.bitwise_xor(own // 2, row // slots) + lax.rem(own, 2)
    key_at = owner * slots + lax.rem(row, slots)
    query_at = lax.rem(lane, slots) + jnp.where(lane < rows, own, other) * slots
    bias = jnp.where(key_at <= query_at, 0.0, NEG_LARGE)
    across = (((1,), (1,)), ((), ()))
    for number in range(KVH):
        key_tile, value_tile, query_tile, upstream_tile = tiles(
            pair_refs, (own_ref, other_ref), number, slots
        )
        scores = lax.dot_general(
            key_tile, query_tile, across, preferred_element_type=jnp.float32
        )
        scores = scores * (1.0 / math.sqrt(HD)) + bias
        top = jnp.max(scores, axis=0, keepdims=True)
        grown = jnp.exp(scores - top)
        prob_grad = lax.dot_general(
            value_tile, upstream_tile, across, preferred_element_type=jnp.float32
        )
        grown_out[number] = grown
        grad_out[number] = prob_grad
        stats_out[number : number + 1, :] = top
        stats_out[KVH + number : KVH + number + 1, :] = jnp.sum(grown, axis=0, keepdims=True)
        stats_out[2 * KVH + number : 2 * KVH + number + 1, :] = jnp.sum(
            grown * prob_grad, axis=0, keepdims=True
        )
    stats_out[3 * KVH :, :] = jnp.concatenate(
        [gate_ref[0:KVH, :], jnp.zeros((KVH, rows), jnp.float32)], axis=1
    )


def combine_kernel(own_ref, other_ref, input_ref, input_other_ref, coef_out, router_out):
    slots = input_ref.shape[0]
    rows = GROUP * slots
    mine = own_ref[...]
    swapped = other_ref[...]
    theirs = jnp.concatenate([swapped[:, rows:], swapped[:, :rows]], axis=1)
    top = jnp.maximum(mine[0:KVH], theirs[0:KVH])
    mine_part = jnp.exp(mine[0:KVH] - top)
    their_part = jnp.exp(theirs[0:KVH] - top)
    mass = mine[KVH : 2 * KVH] * mine_part + theirs[KVH : 2 * KVH] * their_part
    inverse = 1.0 / mass
    inner = (
        mine[2 * KVH : 3 * KVH] * mine_part + theirs[2 * KVH : 3 * KVH] * their_part
    ) * inverse
    gate = mine[3 * KVH :] + theirs[3 * KVH :]
    coef_out[0:KVH, :] = mine_part * inverse * gate
    coef_out[KVH : 2 * KVH, :] = inner
    slope = gate[0:1] * (1.0 - gate[0:1]) * jnp.sum(inner, axis=0, keepdims=True)
    same = diagonal(slots, rows)
    own_slope = jnp.sum(jnp.where(same, slope[:, :rows], 0.0), axis=1, keepdims=True)
    other_slope = jnp.sum(jnp.where(same, slope[:, rows:], 0.0), axis=1, keepdims=True)
    for number in range(router_out.shape[0]):
        router_out[number : number + 1, :] = jnp.sum(
            own_slope * input_ref[:, head(number)].astype(jnp.float32)
            + other_slope * input_other_ref[:, head(number)].astype(jnp.float32),
            axis=0,
            keepdims=True,
        )


def terms_kernel(slots, half, *refs):
    coef_ref, grown_ref, grad_ref, own_ref, other_ref = refs[:5]
    pair_refs = refs[5 : 5 + half]
    query_out, query_send, term_own = refs[5 + half : 8 + half]
    term_refs = refs[8 + half :]
    rows = GROUP * slots
    scale = 1.0 / math.sqrt(HD)
    for number in range(KVH):
        key_tile, _, query_tile, upstream_tile = tiles(
            pair_refs, (own_ref, other_ref), number, slots
        )
        gated = grown_ref[number] * coef_ref[number : number + 1, :]
        inner = coef_ref[KVH + number : KVH + number + 1, :]
        score_grad = (gated * (grad_ref[number] - inner) * scale).astype(jnp.bfloat16)
        key_term = jnp.dot(score_grad, query_tile, preferred_element_type=jnp.float32)
        value_term = jnp.dot(
            gated.astype(jnp.bfloat16), upstream_tile, preferred_element_type=jnp.float32
        )
        key_rows, value_rows = rows_of(number, slots), rows_of(KVH + number, slots)
        term_own[key_rows, :] = key_term[0:slots]
        term_own[value_rows, :] = value_term[0:slots]
        for at, ref in enumerate(term_refs, 1):
            ref[key_rows, :] = key_term[rows_of(at, slots)].astype(jnp.bfloat16)
            ref[value_rows, :] = value_term[rows_of(at, slots)].astype(jnp.bfloat16)
        query_term = lax.dot_general(
            score_grad, key_tile, (((0,), (0,)), ((), ())), preferred_element_type=jnp.float32
        )
        query_out[rows_of(number, rows), :] = query_term[0:rows]
        query_send[rows_of(number, rows), :] = query_term[rows:].astype(jnp.bfloat16)


def ride_kernel(groups, *refs):
    count = (len(refs) - groups - 2) // 2
    term_refs = refs[groups : groups + count]
    router_out, send_out = refs[groups + count : groups + count + 2]
    router = refs[0][...]
    for ref in refs[1:groups]:
        router += ref[...]
    router_out[...] = router
    narrow = router.astype(jnp.bfloat16)
    send_out[...] = narrow
    for term, out in zip(term_refs, refs[groups + count + 2 :]):
        out[0 : term.shape[0], :] = term[...]
        out[term.shape[0] :, :] = narrow


def query_kernel(trig_ref, own_ref, other_ref, far_ref, term_ref, query_out, trig_out, term_out):
    slots = query_out.shape[0]
    cosine = trig_ref[0:slots, :]
    sine = trig_ref[slots : 2 * slots, :]
    trig_out[...] = trig_ref[...]
    term_out[...] = term_ref[...] + far_ref[...].astype(jnp.float32)
    for number in range(HQ):
        part = rows_of(number, slots)
        total = own_ref[part, :] + other_ref[part, :].astype(jnp.float32)
        query_out[:, head(number)] = turn(total, cosine, -sine).astype(jnp.bfloat16)


def final_kernel(router_scale, *refs):
    trig_ref, own_ref, router_ref, alone_ref = refs[:4]
    term_refs = refs[4:-3]
    key_out, value_out, router_out = refs[-3:]
    slots = key_out.shape[0]
    cosine = trig_ref[0:slots, :]
    sine = trig_ref[slots : 2 * slots, :]
    for number in range(2 * KVH):
        part = rows_of(number, slots)
        total = own_ref[part, :]
        for ref in term_refs:
            total += ref[part, :].astype(jnp.float32)
        if number < KVH:
            key_out[:, head(number)] = turn(total, cosine, -sine).astype(jnp.bfloat16)
        else:
            value_out[:, head(number - KVH)] = total.astype(jnp.bfloat16)
    router = router_ref[...] + alone_ref[...].astype(jnp.float32)
    for ref in term_refs:
        router += ref[2 * KVH * slots :, :].astype(jnp.float32)
    router_out[...] = router * router_scale


def call(kernel, outs, args, fetched=(), scratch=(), cost=None):
    local = pl.BlockSpec(memory_space=pltpu.VMEM)
    distant = pl.BlockSpec(memory_space=pl.ANY)
    scratch = list(scratch) + [pltpu.SemaphoreType.DMA((len(fetched),))] * bool(fetched)
    return pl.pallas_call(
        kernel,
        out_shape=outs,
        in_specs=[local] * len(args) + [distant] * len(fetched),
        out_specs=[local] * len(outs),
        scratch_shapes=scratch,
        compiler_params=pltpu.CompilerParams(vmem_limit_bytes=VMEM_LIMIT),
        cost_estimate=cost and pl.CostEstimate(cost, 0, 0),
    )(*args, *[pltpu.with_memory_space_constraint(array, pltpu.HBM) for array in fetched])


def exchange(array, axis, step, size):
    return lax.ppermute(array, axis, [(at, at ^ step) for at in range(size)])


def shards(queries, keys, values, out_grad, routed_inputs, router_weight, positions):
    slots = queries.shape[1]
    width = routed_inputs.shape[2]
    count = lax.axis_size("ctx")
    groups = lax.axis_size("dp")
    half = count // 2
    rows = GROUP * slots
    lines = width // HD
    bf16, f32 = jnp.bfloat16, jnp.float32

    def swap(array):
        return exchange(array, "ctx", 1, count)

    near = pltpu.VMEM
    fetched = [positions, jnp.asarray(rope_table()), keys[0], values[0], queries[0], out_grad[0]]
    pair, query, trig = call(
        prepare_kernel,
        [
            near((2 * KVH * slots, HD), bf16),
            near((2 * HQ * slots, HD), bf16),
            near((2 * slots, HD), f32),
        ],
        [],
        fetched,
        [near(array.shape, array.dtype) for array in fetched],
    )
    query_other = swap(query)
    pairs = [pair] + [
        exchange(pair, "ctx", 2 * step, count) for step in range(1, half)
    ]
    gate, inputs = call(
        gate_kernel,
        [near((8, rows), f32), near((slots, width), bf16)],
        [],
        [router_weight.reshape(lines, HD), routed_inputs[0]],
        [near((lines, HD), f32)],
    )
    inputs_other = swap(routed_inputs[0])
    grown, grad, stats = call(
        functools.partial(scores_kernel, slots),
        [
            near((KVH, half * slots, 2 * rows), f32),
            near((KVH, half * slots, 2 * rows), f32),
            near((4 * KVH, 2 * rows), f32),
        ],
        [gate, query, query_other, *pairs],
        cost=SCORES_COST,
    )
    coef, router = call(
        combine_kernel,
        [near((2 * KVH, 2 * rows), f32), near((lines, HD), f32)],
        [stats, swap(stats), inputs, inputs_other],
    )
    routers = [router] + [
        exchange(router, "dp", step, groups) for step in range(1, groups)
    ]
    query_own, query_send, term_own, *terms = call(
        functools.partial(terms_kernel, slots, half),
        [
            near((HQ * slots, HD), f32),
            near((HQ * slots, HD), bf16),
            near((2 * KVH * slots, HD), f32),
        ]
        + [near((2 * KVH * slots, HD), bf16)] * (half - 1),
        [coef, grown, grad, query, query_other, *pairs],
        cost=TERMS_COST,
    )
    query_back = swap(query_send)
    early = half // 2
    far = exchange(terms[early - 1], "ctx", 2 * early, count)
    others = [step for step in reversed(range(1, half)) if step != early]
    router, router_send, *terms = call(
        functools.partial(ride_kernel, groups),
        [near((lines, HD), f32), near((lines, HD), bf16)]
        + [near((2 * KVH * slots + lines, HD), bf16)] * len(others),
        [*routers, *[terms[step - 1] for step in others]],
        cost=RIDE_COST,
    )
    terms = [exchange(term, "ctx", 2 * step, count) for step, term in zip(others, terms)]
    alone = exchange(router_send, "ctx", 2 * early, count)
    shape = jax.ShapeDtypeStruct
    query_grad, trig, term_own = call(
        query_kernel,
        [
            shape((slots, HQ * HD), bf16),
            near((2 * slots, HD), f32),
            near((2 * KVH * slots, HD), f32),
        ],
        [trig, query_own, query_back, far, term_own],
        cost=QUERY_COST,
    )
    key_grad, value_grad, router_grad = call(
        functools.partial(final_kernel, 1.0 / math.sqrt(groups * count * slots)),
        [shape((slots, KVH * HD), bf16), shape((slots, KVH * HD), bf16), shape((lines, HD), f32)],
        [trig, term_own, router, alone, *terms],
    )
    return (query_grad[None], key_grad[None], value_grad[None], router_grad.reshape(width))


def solution(mesh):
    in_specs = (
        P("dp", "ctx", None),
        P("dp", "ctx", None),
        P("dp", "ctx", None),
        P("dp", "ctx", None),
        P("dp", "ctx", None),
        P(),
        P("dp", "ctx"),
    )
    out_specs = (P("dp", "ctx", None), P("dp", "ctx", None), P("dp", "ctx", None), P())
    return jax.shard_map(shards, mesh=mesh, in_specs=in_specs, out_specs=out_specs, check_vma=False)
```

```python
import functools
import math

import jax
import jax.numpy as jnp
import numpy as np
from jax import lax
from jax.experimental import pallas as pl
from jax.experimental.pallas import tpu as pltpu
from jax.sharding import PartitionSpec as P

HQ = 16
KVH = 4
HD = 128
GROUP = HQ // KVH
ROPE_BASE = 500000.0
NEG_LARGE = -1e30
VMEM_LIMIT = 32 * 1024 * 1024
SCORES_COST = 20 * 10**9
TERMS_COST = 20 * 10**9
RIDE_COST = 20 * 10**9
QUERY_COST = 5 * 10**8


def rope_table():
    half = HD // 2
    frequency = [ROPE_BASE ** (-number / half) for number in range(half)]
    coarse = [256.0 * factor % (2.0 * math.pi) for factor in frequency]
    return np.asarray([coarse + coarse, frequency + frequency], np.float32)


def turn(vectors, cosine, sine):
    return vectors * cosine + pltpu.roll(vectors, HD // 2, 1) * sine


def head(number):
    return slice(number * HD, (number + 1) * HD)


def rows_of(number, depth):
    return slice(number * depth, (number + 1) * depth)


def diagonal(slots, lanes):
    row = lax.broadcasted_iota(jnp.int32, (slots, lanes), 0)
    lane = lax.broadcasted_iota(jnp.int32, (slots, lanes), 1)
    return lax.rem(lane, slots) == row


def prepare_kernel(*refs):
    place_hbm, table_hbm, key_hbm, value_hbm, query_hbm = refs[:5]
    pair_ref, query_out, trig_ref = refs[5:8]
    place_ref, table_ref, key_ref, value_ref, query_ref, semaphores = refs[8:]
    slots = key_ref.shape[0]
    copies = [
        pltpu.make_async_copy(source, target, semaphores.at[at])
        for at, (source, target) in enumerate(
            [
                (place_hbm, place_ref),
                (table_hbm, table_ref),
                (key_hbm, key_ref),
                (value_hbm, value_ref),
                (query_hbm, query_ref),
            ]
        )
    ]
    for copy in copies:
        copy.start()
    copies[0].wait()
    place = place_ref[...]
    upper = (place >> 8).astype(jnp.float32)
    lower = (place & 255).astype(jnp.float32)
    same = diagonal(slots, slots)
    upper = jnp.sum(jnp.where(same, upper, 0.0), axis=1, keepdims=True)
    lower = jnp.sum(jnp.where(same, lower, 0.0), axis=1, keepdims=True)
    copies[1].wait()
    angles = upper * table_ref[0:1, :] + lower * table_ref[1:2, :]
    low = lax.broadcasted_iota(jnp.int32, angles.shape, 1) < HD // 2
    mixed = jnp.cos(jnp.where(low, angles, angles - 0.5 * math.pi))
    turned = pltpu.roll(mixed, HD // 2, 1)
    cosine = jnp.where(low, mixed, turned)
    sine = jnp.where(low, -turned, mixed)
    trig_ref[0:slots, :] = cosine
    trig_ref[slots : 2 * slots, :] = sine
    for copy in copies[2:]:
        copy.wait()
    for number in range(KVH):
        wide = key_ref[:, head(number)].astype(jnp.float32)
        pair_ref[rows_of(number, slots), :] = turn(wide, cosine, sine).astype(jnp.bfloat16)
        pair_ref[rows_of(KVH + number, slots), :] = value_ref[:, head(number)]
    for number in range(HQ):
        wide = query_ref[:, head(number)].astype(jnp.float32)
        query_out[rows_of(number, slots), :] = turn(wide, cosine, sine).astype(jnp.bfloat16)


def gate_kernel(arrived_ref, *refs):
    weight_hbm, input_hbm, upstream_hbm, gate_ref, input_ref, upstream_ref = refs[:6]
    weight_ref, semaphores = refs[6:]
    copies = [
        pltpu.make_async_copy(weight_hbm, weight_ref, semaphores.at[0]),
        pltpu.make_async_copy(input_hbm, input_ref, semaphores.at[1]),
        pltpu.make_async_copy(upstream_hbm, upstream_ref, semaphores.at[2]),
    ]
    for copy in copies:
        copy.start()
    for copy in copies:
        copy.wait()
    slots = input_ref.shape[0]
    blocks = weight_ref.shape[0]
    total = jnp.zeros((slots, HD), jnp.float32)
    for number in range(blocks):
        total += input_ref[:, head(number)].astype(jnp.float32) * weight_ref[number : number + 1, :]
    gate = jax.nn.sigmoid(jnp.sum(total, axis=1, keepdims=True))
    same = diagonal(slots, gate_ref.shape[1])
    gate_ref[...] = jnp.broadcast_to(
        jnp.sum(jnp.where(same, gate, 0.0), axis=0, keepdims=True), gate_ref.shape
    )


def tiles(pair_refs, query_refs, upstream_refs, number, slots):
    rows = GROUP * slots
    key_tile = jnp.concatenate([ref[rows_of(number, slots), :] for ref in pair_refs], axis=0)
    value_tile = jnp.concatenate(
        [ref[rows_of(KVH + number, slots), :] for ref in pair_refs], axis=0
    )
    query_tile = jnp.concatenate([ref[rows_of(number, rows), :] for ref in query_refs], axis=0)
    members = range(number * GROUP, (number + 1) * GROUP)
    upstream_tile = jnp.concatenate(
        [ref[:, head(at)] for ref in upstream_refs for at in members], axis=0
    )
    return key_tile, value_tile, query_tile, upstream_tile


def scores_kernel(slots, *refs):
    gate_ref = refs[0]
    query_refs, upstream_refs = refs[1:3], refs[3:5]
    pair_refs = refs[5:-3]
    grown_out, grad_out, stats_out = refs[-3:]
    rows = GROUP * slots
    keys_total = len(pair_refs) * slots
    own = lax.axis_index("ctx")
    other = own + 1 - 2 * lax.rem(own, 2)
    row = lax.broadcasted_iota(jnp.int32, (keys_total, 2 * rows), 0)
    lane = lax.broadcasted_iota(jnp.int32, (keys_total, 2 * rows), 1)
    owner = 2 * jnp.bitwise_xor(own // 2, row // slots) + lax.rem(own, 2)
    key_at = owner * slots + lax.rem(row, slots)
    query_at = lax.rem(lane, slots) + jnp.where(lane < rows, own, other) * slots
    bias = jnp.where(key_at <= query_at, 0.0, NEG_LARGE)
    across = (((1,), (1,)), ((), ()))
    for number in range(KVH):
        key_tile, value_tile, query_tile, upstream_tile = tiles(
            pair_refs, query_refs, upstream_refs, number, slots
        )
        scores = lax.dot_general(
            key_tile, query_tile, across, preferred_element_type=jnp.float32
        )
        scores = scores * (1.0 / math.sqrt(HD)) + bias
        top = jnp.max(scores, axis=0, keepdims=True)
        grown = jnp.exp(scores - top)
        prob_grad = lax.dot_general(
            value_tile, upstream_tile, across, preferred_element_type=jnp.float32
        )
        grown_out[number] = grown
        grad_out[number] = prob_grad
        stats_out[number : number + 1, :] = top
        stats_out[KVH + number : KVH + number + 1, :] = jnp.sum(grown, axis=0, keepdims=True)
        stats_out[2 * KVH + number : 2 * KVH + number + 1, :] = jnp.sum(
            grown * prob_grad, axis=0, keepdims=True
        )
    stats_out[3 * KVH :, :] = jnp.concatenate(
        [gate_ref[0:KVH, :], jnp.zeros((KVH, rows), jnp.float32)], axis=1
    )


def combine_kernel(own_ref, other_ref, input_ref, input_other_ref, coef_out, router_out):
    slots = input_ref.shape[0]
    rows = GROUP * slots
    mine = own_ref[...]
    swapped = other_ref[...]
    theirs = jnp.concatenate([swapped[:, rows:], swapped[:, :rows]], axis=1)
    top = jnp.maximum(mine[0:KVH], theirs[0:KVH])
    mine_part = jnp.exp(mine[0:KVH] - top)
    their_part = jnp.exp(theirs[0:KVH] - top)
    mass = mine[KVH : 2 * KVH] * mine_part + theirs[KVH : 2 * KVH] * their_part
    inverse = 1.0 / mass
    inner = (
        mine[2 * KVH : 3 * KVH] * mine_part + theirs[2 * KVH : 3 * KVH] * their_part
    ) * inverse
    gate = mine[3 * KVH :] + theirs[3 * KVH :]
    coef_out[0:KVH, :] = mine_part * inverse * gate
    coef_out[KVH : 2 * KVH, :] = inner
    slope = gate[0:1] * (1.0 - gate[0:1]) * jnp.sum(inner, axis=0, keepdims=True)
    same = diagonal(slots, rows)
    own_slope = jnp.sum(jnp.where(same, slope[:, :rows], 0.0), axis=1, keepdims=True)
    other_slope = jnp.sum(jnp.where(same, slope[:, rows:], 0.0), axis=1, keepdims=True)
    for number in range(router_out.shape[0]):
        router_out[number : number + 1, :] = jnp.sum(
            own_slope * input_ref[:, head(number)].astype(jnp.float32)
            + other_slope * input_other_ref[:, head(number)].astype(jnp.float32),
            axis=0,
            keepdims=True,
        )


def terms_kernel(slots, half, *refs):
    coef_ref, grown_ref, grad_ref = refs[:3]
    query_refs, upstream_refs = refs[3:5], refs[5:7]
    pair_refs = refs[7 : 7 + half]
    query_out, query_send, term_own = refs[7 + half : 10 + half]
    term_refs = refs[10 + half :]
    rows = GROUP * slots
    scale = 1.0 / math.sqrt(HD)
    for number in range(KVH):
        key_tile, _, query_tile, upstream_tile = tiles(
            pair_refs, query_refs, upstream_refs, number, slots
        )
        gated = grown_ref[number] * coef_ref[number : number + 1, :]
        inner = coef_ref[KVH + number : KVH + number + 1, :]
        score_grad = (gated * (grad_ref[number] - inner) * scale).astype(jnp.bfloat16)
        key_term = jnp.dot(score_grad, query_tile, preferred_element_type=jnp.float32)
        value_term = jnp.dot(
            gated.astype(jnp.bfloat16), upstream_tile, preferred_element_type=jnp.float32
        )
        key_rows, value_rows = rows_of(number, slots), rows_of(KVH + number, slots)
        term_own[key_rows, :] = key_term[0:slots]
        term_own[value_rows, :] = value_term[0:slots]
        for at, ref in enumerate(term_refs, 1):
            ref[key_rows, :] = key_term[rows_of(at, slots)].astype(jnp.bfloat16)
            ref[value_rows, :] = value_term[rows_of(at, slots)].astype(jnp.bfloat16)
        query_term = lax.dot_general(
            score_grad, key_tile, (((0,), (0,)), ((), ())), preferred_element_type=jnp.float32
        )
        query_out[rows_of(number, rows), :] = query_term[0:rows]
        query_send[rows_of(number, rows), :] = query_term[rows:].astype(jnp.bfloat16)


def ride_kernel(groups, *refs):
    count = (len(refs) - groups - 2) // 2
    term_refs = refs[groups : groups + count]
    router_out, send_out = refs[groups + count : groups + count + 2]
    router = refs[0][...]
    for ref in refs[1:groups]:
        router += ref[...]
    router_out[...] = router
    narrow = router.astype(jnp.bfloat16)
    send_out[...] = narrow
    for term, out in zip(term_refs, refs[groups + count + 2 :]):
        out[0 : term.shape[0], :] = term[...]
        out[term.shape[0] :, :] = narrow


def query_kernel(trig_ref, own_ref, other_ref, far_ref, term_ref, query_out, trig_out, term_out):
    slots = query_out.shape[0]
    cosine = trig_ref[0:slots, :]
    sine = trig_ref[slots : 2 * slots, :]
    trig_out[...] = trig_ref[...]
    term_out[...] = term_ref[...] + far_ref[...].astype(jnp.float32)
    for number in range(HQ):
        part = rows_of(number, slots)
        total = own_ref[part, :] + other_ref[part, :].astype(jnp.float32)
        query_out[:, head(number)] = turn(total, cosine, -sine).astype(jnp.bfloat16)


def final_kernel(router_scale, *refs):
    trig_ref, own_ref, router_ref, alone_ref = refs[:4]
    term_refs = refs[4:-3]
    key_out, value_out, router_out = refs[-3:]
    slots = key_out.shape[0]
    cosine = trig_ref[0:slots, :]
    sine = trig_ref[slots : 2 * slots, :]
    for number in range(2 * KVH):
        part = rows_of(number, slots)
        total = own_ref[part, :]
        for ref in term_refs:
            total += ref[part, :].astype(jnp.float32)
        if number < KVH:
            key_out[:, head(number)] = turn(total, cosine, -sine).astype(jnp.bfloat16)
        else:
            value_out[:, head(number - KVH)] = total.astype(jnp.bfloat16)
    router = router_ref[...] + alone_ref[...].astype(jnp.float32)
    for ref in term_refs:
        router += ref[2 * KVH * slots :, :].astype(jnp.float32)
    router_out[...] = router * router_scale


def call(kernel, outs, args, fetched=(), scratch=(), cost=None):
    local = pl.BlockSpec(memory_space=pltpu.VMEM)
    distant = pl.BlockSpec(memory_space=pl.ANY)
    scratch = list(scratch) + [pltpu.SemaphoreType.DMA((len(fetched),))] * bool(fetched)
    return pl.pallas_call(
        kernel,
        out_shape=outs,
        in_specs=[local] * len(args) + [distant] * len(fetched),
        out_specs=[local] * len(outs),
        scratch_shapes=scratch,
        compiler_params=pltpu.CompilerParams(vmem_limit_bytes=VMEM_LIMIT),
        cost_estimate=cost and pl.CostEstimate(cost, 0, 0),
    )(*args, *[pltpu.with_memory_space_constraint(array, pltpu.HBM) for array in fetched])


def exchange(array, axis, step, size):
    return lax.ppermute(array, axis, [(at, at ^ step) for at in range(size)])


def shards(queries, keys, values, out_grad, routed_inputs, router_weight, positions):
    slots = queries.shape[1]
    width = routed_inputs.shape[2]
    count = lax.axis_size("ctx")
    groups = lax.axis_size("dp")
    half = count // 2
    rows = GROUP * slots
    lines = width // HD
    bf16, f32 = jnp.bfloat16, jnp.float32

    def swap(array):
        return exchange(array, "ctx", 1, count)

    near = pltpu.VMEM
    upstream_other = swap(out_grad[0])
    fetched = [positions, jnp.asarray(rope_table()), keys[0], values[0], queries[0]]
    pair, query, trig = call(
        prepare_kernel,
        [
            near((2 * KVH * slots, HD), bf16),
            near((HQ * slots, HD), bf16),
            near((2 * slots, HD), f32),
        ],
        [],
        fetched,
        [near(array.shape, array.dtype) for array in fetched],
    )
    query_other = swap(query)
    pairs = [pair] + [
        exchange(pair, "ctx", 2 * step, count) for step in range(1, half)
    ]
    gate, inputs, upstream = call(
        gate_kernel,
        [near((8, rows), f32), near((slots, width), bf16), near((slots, HQ * HD), bf16)],
        [upstream_other],
        [router_weight.reshape(lines, HD), routed_inputs[0], out_grad[0]],
        [near((lines, HD), f32)],
    )
    inputs_other = swap(routed_inputs[0])
    grown, grad, stats = call(
        functools.partial(scores_kernel, slots),
        [
            near((KVH, half * slots, 2 * rows), f32),
            near((KVH, half * slots, 2 * rows), f32),
            near((4 * KVH, 2 * rows), f32),
        ],
        [gate, query, query_other, upstream, upstream_other, *pairs],
        cost=SCORES_COST,
    )
    coef, router = call(
        combine_kernel,
        [near((2 * KVH, 2 * rows), f32), near((lines, HD), f32)],
        [stats, swap(stats), inputs, inputs_other],
    )
    routers = [router] + [
        exchange(router, "dp", step, groups) for step in range(1, groups)
    ]
    query_own, query_send, term_own, *terms = call(
        functools.partial(terms_kernel, slots, half),
        [
            near((HQ * slots, HD), f32),
            near((HQ * slots, HD), bf16),
            near((2 * KVH * slots, HD), f32),
        ]
        + [near((2 * KVH * slots, HD), bf16)] * (half - 1),
        [coef, grown, grad, query, query_other, upstream, upstream_other, *pairs],
        cost=TERMS_COST,
    )
    query_back = swap(query_send)
    early = half // 2
    far = exchange(terms[early - 1], "ctx", 2 * early, count)
    others = [step for step in reversed(range(1, half)) if step != early]
    router, router_send, *terms = call(
        functools.partial(ride_kernel, groups),
        [near((lines, HD), f32), near((lines, HD), bf16)]
        + [near((2 * KVH * slots + lines, HD), bf16)] * len(others),
        [*routers, *[terms[step - 1] for step in others]],
        cost=RIDE_COST,
    )
    terms = [exchange(term, "ctx", 2 * step, count) for step, term in zip(others, terms)]
    alone = exchange(router_send, "ctx", 2 * early, count)
    shape = jax.ShapeDtypeStruct
    query_grad, trig, term_own = call(
        query_kernel,
        [
            shape((slots, HQ * HD), bf16),
            near((2 * slots, HD), f32),
            near((2 * KVH * slots, HD), f32),
        ],
        [trig, query_own, query_back, far, term_own],
        cost=QUERY_COST,
    )
    key_grad, value_grad, router_grad = call(
        functools.partial(final_kernel, 1.0 / math.sqrt(groups * count * slots)),
        [shape((slots, KVH * HD), bf16), shape((slots, KVH * HD), bf16), shape((lines, HD), f32)],
        [trig, term_own, router, alone, *terms],
    )
    return (query_grad[None], key_grad[None], value_grad[None], router_grad.reshape(width))


def solution(mesh):
    in_specs = (
        P("dp", "ctx", None),
        P("dp", "ctx", None),
        P("dp", "ctx", None),
        P("dp", "ctx", None),
        P("dp", "ctx", None),
        P(),
        P("dp", "ctx"),
    )
    out_specs = (P("dp", "ctx", None), P("dp", "ctx", None), P("dp", "ctx", None), P())
    return jax.shard_map(shards, mesh=mesh, in_specs=in_specs, out_specs=out_specs, check_vma=False)
```

```python
import functools
import math

import jax
import jax.numpy as jnp
import numpy as np
from jax import lax
from jax.experimental import pallas as pl
from jax.experimental.pallas import tpu as pltpu
from jax.sharding import PartitionSpec as P

HQ = 16
KVH = 4
HD = 128
GROUP = HQ // KVH
ROPE_BASE = 500000.0
NEG_LARGE = -1e30
VMEM_LIMIT = 32 * 1024 * 1024
SCORES_COST = 20 * 10**9
TERMS_COST = 20 * 10**9
RIDE_COST = 20 * 10**9
QUERY_COST = 5 * 10**8


def rope_table():
    half = HD // 2
    frequency = [ROPE_BASE ** (-number / half) for number in range(half)]
    coarse = [256.0 * factor % (2.0 * math.pi) for factor in frequency]
    return np.asarray([coarse + coarse, frequency + frequency], np.float32)


def turn(vectors, cosine, sine):
    return vectors * cosine + pltpu.roll(vectors, HD // 2, 1) * sine


def head(number):
    return slice(number * HD, (number + 1) * HD)


def rows_of(number, depth):
    return slice(number * depth, (number + 1) * depth)


def diagonal(slots, lanes):
    row = lax.broadcasted_iota(jnp.int32, (slots, lanes), 0)
    lane = lax.broadcasted_iota(jnp.int32, (slots, lanes), 1)
    return lax.rem(lane, slots) == row


def prepare_kernel(*refs):
    place_hbm, table_hbm, key_hbm, value_hbm, query_hbm, upstream_hbm = refs[:6]
    pair_ref, query_out, trig_ref = refs[6:9]
    place_ref, table_ref, key_ref, value_ref, query_ref, upstream_ref, semaphores = refs[9:]
    slots = key_ref.shape[0]
    copies = [
        pltpu.make_async_copy(source, target, semaphores.at[at])
        for at, (source, target) in enumerate(
            [
                (place_hbm, place_ref),
                (table_hbm, table_ref),
                (key_hbm, key_ref),
                (value_hbm, value_ref),
                (query_hbm, query_ref),
                (upstream_hbm, upstream_ref),
            ]
        )
    ]
    for copy in copies:
        copy.start()
    copies[0].wait()
    place = place_ref[...]
    upper = (place >> 8).astype(jnp.float32)
    lower = (place & 255).astype(jnp.float32)
    same = diagonal(slots, slots)
    upper = jnp.sum(jnp.where(same, upper, 0.0), axis=1, keepdims=True)
    lower = jnp.sum(jnp.where(same, lower, 0.0), axis=1, keepdims=True)
    copies[1].wait()
    angles = upper * table_ref[0:1, :] + lower * table_ref[1:2, :]
    low = lax.broadcasted_iota(jnp.int32, angles.shape, 1) < HD // 2
    mixed = jnp.cos(jnp.where(low, angles, angles - 0.5 * math.pi))
    turned = pltpu.roll(mixed, HD // 2, 1)
    cosine = jnp.where(low, mixed, turned)
    sine = jnp.where(low, -turned, mixed)
    trig_ref[0:slots, :] = cosine
    trig_ref[slots : 2 * slots, :] = sine
    for copy in copies[2:]:
        copy.wait()
    for number in range(KVH):
        wide = key_ref[:, head(number)].astype(jnp.float32)
        pair_ref[rows_of(number, slots), :] = turn(wide, cosine, sine).astype(jnp.bfloat16)
        pair_ref[rows_of(KVH + number, slots), :] = value_ref[:, head(number)]
    for number in range(HQ):
        wide = query_ref[:, head(number)].astype(jnp.float32)
        query_out[rows_of(number, slots), :] = turn(wide, cosine, sine).astype(jnp.bfloat16)
        query_out[rows_of(HQ + number, slots), :] = upstream_ref[:, head(number)]


def gate_kernel(weight_hbm, input_hbm, gate_ref, input_ref, weight_ref, semaphores):
    copies = [
        pltpu.make_async_copy(weight_hbm, weight_ref, semaphores.at[0]),
        pltpu.make_async_copy(input_hbm, input_ref, semaphores.at[1]),
    ]
    for copy in copies:
        copy.start()
    for copy in copies:
        copy.wait()
    slots = input_ref.shape[0]
    blocks = weight_ref.shape[0]
    total = jnp.zeros((slots, HD), jnp.float32)
    for number in range(blocks):
        total += input_ref[:, head(number)].astype(jnp.float32) * weight_ref[number : number + 1, :]
    gate = jax.nn.sigmoid(jnp.sum(total, axis=1, keepdims=True))
    same = diagonal(slots, gate_ref.shape[1])
    gate_ref[...] = jnp.broadcast_to(
        jnp.sum(jnp.where(same, gate, 0.0), axis=0, keepdims=True), gate_ref.shape
    )


def tiles(pair_refs, query_refs, number, slots):
    rows = GROUP * slots
    key_tile = jnp.concatenate([ref[rows_of(number, slots), :] for ref in pair_refs], axis=0)
    value_tile = jnp.concatenate(
        [ref[rows_of(KVH + number, slots), :] for ref in pair_refs], axis=0
    )
    query_tile = jnp.concatenate([ref[rows_of(number, rows), :] for ref in query_refs], axis=0)
    upstream_tile = jnp.concatenate(
        [ref[rows_of(KVH + number, rows), :] for ref in query_refs], axis=0
    )
    return key_tile, value_tile, query_tile, upstream_tile


def scores_kernel(slots, *refs):
    gate_ref, own_ref, other_ref = refs[:3]
    pair_refs = refs[3:-3]
    grown_out, grad_out, stats_out = refs[-3:]
    rows = GROUP * slots
    keys_total = len(pair_refs) * slots
    own = lax.axis_index("ctx")
    other = own + 1 - 2 * lax.rem(own, 2)
    row = lax.broadcasted_iota(jnp.int32, (keys_total, 2 * rows), 0)
    lane = lax.broadcasted_iota(jnp.int32, (keys_total, 2 * rows), 1)
    owner = 2 * jnp.bitwise_xor(own // 2, row // slots) + lax.rem(own, 2)
    key_at = owner * slots + lax.rem(row, slots)
    query_at = lax.rem(lane, slots) + jnp.where(lane < rows, own, other) * slots
    bias = jnp.where(key_at <= query_at, 0.0, NEG_LARGE)
    across = (((1,), (1,)), ((), ()))
    for number in range(KVH):
        key_tile, value_tile, query_tile, upstream_tile = tiles(
            pair_refs, (own_ref, other_ref), number, slots
        )
        scores = lax.dot_general(
            key_tile, query_tile, across, preferred_element_type=jnp.float32
        )
        scores = scores * (1.0 / math.sqrt(HD)) + bias
        top = jnp.max(scores, axis=0, keepdims=True)
        grown = jnp.exp(scores - top)
        prob_grad = lax.dot_general(
            value_tile, upstream_tile, across, preferred_element_type=jnp.float32
        )
        grown_out[number] = grown
        grad_out[number] = prob_grad
        stats_out[number : number + 1, :] = top
        stats_out[KVH + number : KVH + number + 1, :] = jnp.sum(grown, axis=0, keepdims=True)
        stats_out[2 * KVH + number : 2 * KVH + number + 1, :] = jnp.sum(
            grown * prob_grad, axis=0, keepdims=True
        )
    stats_out[3 * KVH :, :] = jnp.concatenate(
        [gate_ref[0:KVH, :], jnp.zeros((KVH, rows), jnp.float32)], axis=1
    )


def combine_kernel(own_ref, other_ref, input_ref, input_other_ref, coef_out, router_out):
    slots = input_ref.shape[0]
    rows = GROUP * slots
    mine = own_ref[...]
    swapped = other_ref[...]
    theirs = jnp.concatenate([swapped[:, rows:], swapped[:, :rows]], axis=1)
    top = jnp.maximum(mine[0:KVH], theirs[0:KVH])
    mine_part = jnp.exp(mine[0:KVH] - top)
    their_part = jnp.exp(theirs[0:KVH] - top)
    mass = mine[KVH : 2 * KVH] * mine_part + theirs[KVH : 2 * KVH] * their_part
    inverse = 1.0 / mass
    inner = (
        mine[2 * KVH : 3 * KVH] * mine_part + theirs[2 * KVH : 3 * KVH] * their_part
    ) * inverse
    gate = mine[3 * KVH :] + theirs[3 * KVH :]
    coef_out[0:KVH, :] = mine_part * inverse * gate
    coef_out[KVH : 2 * KVH, :] = inner
    slope = gate[0:1] * (1.0 - gate[0:1]) * jnp.sum(inner, axis=0, keepdims=True)
    same = diagonal(slots, rows)
    own_slope = jnp.sum(jnp.where(same, slope[:, :rows], 0.0), axis=1, keepdims=True)
    other_slope = jnp.sum(jnp.where(same, slope[:, rows:], 0.0), axis=1, keepdims=True)
    for number in range(router_out.shape[0]):
        router_out[number : number + 1, :] = jnp.sum(
            own_slope * input_ref[:, head(number)].astype(jnp.float32)
            + other_slope * input_other_ref[:, head(number)].astype(jnp.float32),
            axis=0,
            keepdims=True,
        )


def terms_kernel(slots, half, *refs):
    coef_ref, grown_ref, grad_ref, own_ref, other_ref = refs[:5]
    pair_refs = refs[5 : 5 + half]
    query_out, query_send, term_own = refs[5 + half : 8 + half]
    term_refs = refs[8 + half :]
    rows = GROUP * slots
    scale = 1.0 / math.sqrt(HD)
    for number in range(KVH):
        key_tile, _, query_tile, upstream_tile = tiles(
            pair_refs, (own_ref, other_ref), number, slots
        )
        gated = grown_ref[number] * coef_ref[number : number + 1, :]
        inner = coef_ref[KVH + number : KVH + number + 1, :]
        score_grad = (gated * (grad_ref[number] - inner) * scale).astype(jnp.bfloat16)
        key_term = jnp.dot(score_grad, query_tile, preferred_element_type=jnp.float32)
        value_term = jnp.dot(
            gated.astype(jnp.bfloat16), upstream_tile, preferred_element_type=jnp.float32
        )
        key_rows, value_rows = rows_of(number, slots), rows_of(KVH + number, slots)
        term_own[key_rows, :] = key_term[0:slots]
        term_own[value_rows, :] = value_term[0:slots]
        for at, ref in enumerate(term_refs, 1):
            ref[key_rows, :] = key_term[rows_of(at, slots)].astype(jnp.bfloat16)
            ref[value_rows, :] = value_term[rows_of(at, slots)].astype(jnp.bfloat16)
        query_term = lax.dot_general(
            score_grad, key_tile, (((0,), (0,)), ((), ())), preferred_element_type=jnp.float32
        )
        query_out[rows_of(number, rows), :] = query_term[0:rows]
        query_send[rows_of(number, rows), :] = query_term[rows:].astype(jnp.bfloat16)


def ride_kernel(groups, *refs):
    count = (len(refs) - groups - 2) // 2
    term_refs = refs[groups : groups + count]
    router_out, send_out = refs[groups + count : groups + count + 2]
    router = refs[0][...]
    for ref in refs[1:groups]:
        router += ref[...]
    router_out[...] = router
    narrow = router.astype(jnp.bfloat16)
    send_out[...] = narrow
    for term, out in zip(term_refs, refs[groups + count + 2 :]):
        out[0 : term.shape[0], :] = term[...]
        out[term.shape[0] :, :] = narrow


def query_kernel(trig_ref, own_ref, other_ref, far_ref, term_ref, query_out, trig_out, term_out):
    slots = query_out.shape[0]
    cosine = trig_ref[0:slots, :]
    sine = trig_ref[slots : 2 * slots, :]
    trig_out[...] = trig_ref[...]
    term_out[...] = term_ref[...] + far_ref[...].astype(jnp.float32)
    for number in range(HQ):
        part = rows_of(number, slots)
        total = own_ref[part, :] + other_ref[part, :].astype(jnp.float32)
        query_out[:, head(number)] = turn(total, cosine, -sine).astype(jnp.bfloat16)


def final_kernel(router_scale, *refs):
    trig_ref, own_ref, router_ref, alone_ref = refs[:4]
    term_refs = refs[4:-3]
    key_out, value_out, router_out = refs[-3:]
    slots = key_out.shape[0]
    cosine = trig_ref[0:slots, :]
    sine = trig_ref[slots : 2 * slots, :]
    for number in range(2 * KVH):
        part = rows_of(number, slots)
        total = own_ref[part, :]
        for ref in term_refs:
            total += ref[part, :].astype(jnp.float32)
        if number < KVH:
            key_out[:, head(number)] = turn(total, cosine, -sine).astype(jnp.bfloat16)
        else:
            value_out[:, head(number - KVH)] = total.astype(jnp.bfloat16)
    router = router_ref[...] + alone_ref[...].astype(jnp.float32)
    for ref in term_refs:
        router += ref[2 * KVH * slots :, :].astype(jnp.float32)
    router_out[...] = router * router_scale


def call(kernel, outs, args, fetched=(), scratch=(), cost=None):
    local = pl.BlockSpec(memory_space=pltpu.VMEM)
    distant = pl.BlockSpec(memory_space=pl.ANY)
    scratch = list(scratch) + [pltpu.SemaphoreType.DMA((len(fetched),))] * bool(fetched)
    return pl.pallas_call(
        kernel,
        out_shape=outs,
        in_specs=[local] * len(args) + [distant] * len(fetched),
        out_specs=[local] * len(outs),
        scratch_shapes=scratch,
        compiler_params=pltpu.CompilerParams(vmem_limit_bytes=VMEM_LIMIT),
        cost_estimate=cost and pl.CostEstimate(cost, 0, 0),
    )(*args, *[pltpu.with_memory_space_constraint(array, pltpu.HBM) for array in fetched])


def exchange(array, axis, step, size):
    return lax.ppermute(array, axis, [(at, at ^ step) for at in range(size)])


def shards(queries, keys, values, out_grad, routed_inputs, router_weight, positions):
    slots = queries.shape[1]
    width = routed_inputs.shape[2]
    count = lax.axis_size("ctx")
    groups = lax.axis_size("dp")
    half = count // 2
    rows = GROUP * slots
    lines = width // HD
    bf16, f32 = jnp.bfloat16, jnp.float32

    def swap(array):
        return exchange(array, "ctx", 1, count)

    near = pltpu.VMEM
    fetched = [positions, jnp.asarray(rope_table()), keys[0], values[0], queries[0], out_grad[0]]
    pair, query, trig = call(
        prepare_kernel,
        [
            near((2 * KVH * slots, HD), bf16),
            near((2 * HQ * slots, HD), bf16),
            near((2 * slots, HD), f32),
        ],
        [],
        fetched,
        [near(array.shape, array.dtype) for array in fetched],
    )
    query_other = swap(query)
    pairs = [pair] + [
        exchange(pair, "ctx", 2 * step, count) for step in range(1, half)
    ]
    gate, inputs = call(
        gate_kernel,
        [near((8, rows), f32), near((slots, width), bf16)],
        [],
        [router_weight.reshape(lines, HD), routed_inputs[0]],
        [near((lines, HD), f32)],
    )
    inputs_other = swap(routed_inputs[0])
    grown, grad, stats = call(
        functools.partial(scores_kernel, slots),
        [
            near((KVH, half * slots, 2 * rows), f32),
            near((KVH, half * slots, 2 * rows), f32),
            near((4 * KVH, 2 * rows), f32),
        ],
        [gate, query, query_other, *pairs],
        cost=SCORES_COST,
    )
    coef, router = call(
        combine_kernel,
        [near((2 * KVH, 2 * rows), f32), near((lines, HD), f32)],
        [stats, swap(stats), inputs, inputs_other],
    )
    routers = [router] + [
        exchange(router, "dp", step, groups) for step in range(1, groups)
    ]
    query_own, query_send, term_own, *terms = call(
        functools.partial(terms_kernel, slots, half),
        [
            near((HQ * slots, HD), f32),
            near((HQ * slots, HD), bf16),
            near((2 * KVH * slots, HD), f32),
        ]
        + [near((2 * KVH * slots, HD), bf16)] * (half - 1),
        [coef, grown, grad, query, query_other, *pairs],
        cost=TERMS_COST,
    )
    query_back = swap(query_send)
    early = half // 2
    far = exchange(terms[early - 1], "ctx", 2 * early, count)
    others = [step for step in range(1, half) if step != early]
    router, router_send, *terms = call(
        functools.partial(ride_kernel, groups),
        [near((lines, HD), f32), near((lines, HD), bf16)]
        + [near((2 * KVH * slots + lines, HD), bf16)] * len(others),
        [*routers, *[terms[step - 1] for step in others]],
        cost=RIDE_COST,
    )
    terms = [exchange(term, "ctx", 2 * step, count) for step, term in zip(others, terms)]
    alone = exchange(router_send, "ctx", 2 * early, count)
    shape = jax.ShapeDtypeStruct
    query_grad, trig, term_own = call(
        query_kernel,
        [
            shape((slots, HQ * HD), bf16),
            near((2 * slots, HD), f32),
            near((2 * KVH * slots, HD), f32),
        ],
        [trig, query_own, query_back, far, term_own],
        cost=QUERY_COST,
    )
    key_grad, value_grad, router_grad = call(
        functools.partial(final_kernel, 1.0 / math.sqrt(groups * count * slots)),
        [shape((slots, KVH * HD), bf16), shape((slots, KVH * HD), bf16), shape((lines, HD), f32)],
        [trig, term_own, router, alone, *terms],
    )
    return (query_grad[None], key_grad[None], value_grad[None], router_grad.reshape(width))


def solution(mesh):
    in_specs = (
        P("dp", "ctx", None),
        P("dp", "ctx", None),
        P("dp", "ctx", None),
        P("dp", "ctx", None),
        P("dp", "ctx", None),
        P(),
        P("dp", "ctx"),
    )
    out_specs = (P("dp", "ctx", None), P("dp", "ctx", None), P("dp", "ctx", None), P())
    return jax.shard_map(shards, mesh=mesh, in_specs=in_specs, out_specs=out_specs, check_vma=False)
```

```python
import functools
import math

import jax
import jax.numpy as jnp
import numpy as np
from jax import lax
from jax.experimental import pallas as pl
from jax.experimental.pallas import tpu as pltpu
from jax.sharding import PartitionSpec as P

HQ = 16
KVH = 4
HD = 128
GROUP = HQ // KVH
ROPE_BASE = 500000.0
NEG_LARGE = -1e30
VMEM_LIMIT = 32 * 1024 * 1024
SCORES_COST = 20 * 10**9
TERMS_COST = 20 * 10**9
RIDE_COST = 20 * 10**9
QUERY_COST = 5 * 10**8


def rope_table():
    half = HD // 2
    frequency = [ROPE_BASE ** (-number / half) for number in range(half)]
    coarse = [256.0 * factor % (2.0 * math.pi) for factor in frequency]
    return np.asarray([coarse + coarse, frequency + frequency], np.float32)


def turn(vectors, cosine, sine):
    return vectors * cosine + pltpu.roll(vectors, HD // 2, 1) * sine


def head(number):
    return slice(number * HD, (number + 1) * HD)


def rows_of(number, depth):
    return slice(number * depth, (number + 1) * depth)


def diagonal(slots, lanes):
    row = lax.broadcasted_iota(jnp.int32, (slots, lanes), 0)
    lane = lax.broadcasted_iota(jnp.int32, (slots, lanes), 1)
    return lax.rem(lane, slots) == row


def prepare_kernel(*refs):
    place_hbm, table_hbm, key_hbm, value_hbm, query_hbm, upstream_hbm = refs[:6]
    pair_ref, query_out, trig_ref = refs[6:9]
    place_ref, table_ref, key_ref, value_ref, query_ref, upstream_ref, semaphores = refs[9:]
    slots = key_ref.shape[0]
    copies = [
        pltpu.make_async_copy(source, target, semaphores.at[at])
        for at, (source, target) in enumerate(
            [
                (place_hbm, place_ref),
                (table_hbm, table_ref),
                (key_hbm, key_ref),
                (value_hbm, value_ref),
                (query_hbm, query_ref),
                (upstream_hbm, upstream_ref),
            ]
        )
    ]
    for copy in copies:
        copy.start()
    copies[0].wait()
    place = place_ref[...]
    upper = (place >> 8).astype(jnp.float32)
    lower = (place & 255).astype(jnp.float32)
    same = diagonal(slots, slots)
    upper = jnp.sum(jnp.where(same, upper, 0.0), axis=1, keepdims=True)
    lower = jnp.sum(jnp.where(same, lower, 0.0), axis=1, keepdims=True)
    copies[1].wait()
    angles = upper * table_ref[0:1, :] + lower * table_ref[1:2, :]
    low = lax.broadcasted_iota(jnp.int32, angles.shape, 1) < HD // 2
    mixed = jnp.cos(jnp.where(low, angles, angles - 0.5 * math.pi))
    turned = pltpu.roll(mixed, HD // 2, 1)
    cosine = jnp.where(low, mixed, turned)
    sine = jnp.where(low, -turned, mixed)
    trig_ref[0:slots, :] = cosine
    trig_ref[slots : 2 * slots, :] = sine
    for copy in copies[2:]:
        copy.wait()
    for number in range(KVH):
        wide = key_ref[:, head(number)].astype(jnp.float32)
        pair_ref[rows_of(number, slots), :] = turn(wide, cosine, sine).astype(jnp.bfloat16)
        pair_ref[rows_of(KVH + number, slots), :] = value_ref[:, head(number)]
    for number in range(HQ):
        wide = query_ref[:, head(number)].astype(jnp.float32)
        query_out[rows_of(number, slots), :] = turn(wide, cosine, sine).astype(jnp.bfloat16)
        query_out[rows_of(HQ + number, slots), :] = upstream_ref[:, head(number)]


def gate_kernel(weight_hbm, input_hbm, gate_ref, input_ref, bias_ref, weight_ref, semaphores):
    copies = [
        pltpu.make_async_copy(weight_hbm, weight_ref, semaphores.at[0]),
        pltpu.make_async_copy(input_hbm, input_ref, semaphores.at[1]),
    ]
    for copy in copies:
        copy.start()
    slots = input_ref.shape[0]
    rows = GROUP * slots
    keys_total = bias_ref.shape[0]
    own = lax.axis_index("ctx")
    other = own + 1 - 2 * lax.rem(own, 2)
    row = lax.broadcasted_iota(jnp.int32, (keys_total, 2 * rows), 0)
    lane = lax.broadcasted_iota(jnp.int32, (keys_total, 2 * rows), 1)
    owner = 2 * jnp.bitwise_xor(own // 2, row // slots) + lax.rem(own, 2)
    key_at = owner * slots + lax.rem(row, slots)
    query_at = lax.rem(lane, slots) + jnp.where(lane < rows, own, other) * slots
    bias_ref[...] = jnp.where(key_at <= query_at, 0.0, NEG_LARGE)
    for copy in copies:
        copy.wait()
    blocks = weight_ref.shape[0]
    total = jnp.zeros((slots, HD), jnp.float32)
    for number in range(blocks):
        total += input_ref[:, head(number)].astype(jnp.float32) * weight_ref[number : number + 1, :]
    gate = jax.nn.sigmoid(jnp.sum(total, axis=1, keepdims=True))
    same = diagonal(slots, gate_ref.shape[1])
    gate_ref[...] = jnp.broadcast_to(
        jnp.sum(jnp.where(same, gate, 0.0), axis=0, keepdims=True), gate_ref.shape
    )


def tiles(pair_refs, query_refs, number, slots):
    rows = GROUP * slots
    key_tile = jnp.concatenate([ref[rows_of(number, slots), :] for ref in pair_refs], axis=0)
    value_tile = jnp.concatenate(
        [ref[rows_of(KVH + number, slots), :] for ref in pair_refs], axis=0
    )
    query_tile = jnp.concatenate([ref[rows_of(number, rows), :] for ref in query_refs], axis=0)
    upstream_tile = jnp.concatenate(
        [ref[rows_of(KVH + number, rows), :] for ref in query_refs], axis=0
    )
    return key_tile, value_tile, query_tile, upstream_tile


def scores_kernel(slots, *refs):
    gate_ref, bias_ref, own_ref, other_ref = refs[:4]
    pair_refs = refs[4:-2]
    grown_out, stats_out = refs[-2:]
    rows = GROUP * slots
    across = (((1,), (1,)), ((), ()))
    for number in range(KVH):
        key_tile, value_tile, query_tile, upstream_tile = tiles(
            pair_refs, (own_ref, other_ref), number, slots
        )
        scores = lax.dot_general(
            key_tile, query_tile, across, preferred_element_type=jnp.float32
        )
        scores = scores * (1.0 / math.sqrt(HD)) + bias_ref[...]
        top = jnp.max(scores, axis=0, keepdims=True)
        grown = jnp.exp(scores - top)
        prob_grad = lax.dot_general(
            value_tile, upstream_tile, across, preferred_element_type=jnp.float32
        )
        grown_out[number] = grown
        stats_out[number : number + 1, :] = top
        stats_out[KVH + number : KVH + number + 1, :] = jnp.sum(grown, axis=0, keepdims=True)
        stats_out[2 * KVH + number : 2 * KVH + number + 1, :] = jnp.sum(
            grown * prob_grad, axis=0, keepdims=True
        )
    stats_out[3 * KVH :, :] = jnp.concatenate(
        [gate_ref[0:KVH, :], jnp.zeros((KVH, rows), jnp.float32)], axis=1
    )


def combine_kernel(
    own_ref, other_ref, input_ref, input_other_ref, coef_out, router_out, send_out
):
    slots = input_ref.shape[0]
    rows = GROUP * slots
    mine = own_ref[...]
    swapped = other_ref[...]
    theirs = jnp.concatenate([swapped[:, rows:], swapped[:, :rows]], axis=1)
    top = jnp.maximum(mine[0:KVH], theirs[0:KVH])
    mine_part = jnp.exp(mine[0:KVH] - top)
    their_part = jnp.exp(theirs[0:KVH] - top)
    mass = mine[KVH : 2 * KVH] * mine_part + theirs[KVH : 2 * KVH] * their_part
    inverse = 1.0 / mass
    inner = (
        mine[2 * KVH : 3 * KVH] * mine_part + theirs[2 * KVH : 3 * KVH] * their_part
    ) * inverse
    gate = mine[3 * KVH :] + theirs[3 * KVH :]
    coef_out[0:KVH, :] = mine_part * inverse * gate
    coef_out[KVH : 2 * KVH, :] = inner
    slope = gate[0:1] * (1.0 - gate[0:1]) * jnp.sum(inner, axis=0, keepdims=True)
    same = diagonal(slots, rows)
    own_slope = jnp.sum(jnp.where(same, slope[:, :rows], 0.0), axis=1, keepdims=True)
    other_slope = jnp.sum(jnp.where(same, slope[:, rows:], 0.0), axis=1, keepdims=True)
    for number in range(router_out.shape[0]):
        router_out[number : number + 1, :] = jnp.sum(
            own_slope * input_ref[:, head(number)].astype(jnp.float32)
            + other_slope * input_other_ref[:, head(number)].astype(jnp.float32),
            axis=0,
            keepdims=True,
        )
    send_out[...] = router_out[...].astype(jnp.bfloat16)


def terms_kernel(slots, half, *refs):
    coef_ref, grown_ref, own_ref, other_ref = refs[:4]
    pair_refs = refs[4 : 4 + half]
    query_out, query_send, term_own = refs[4 + half : 7 + half]
    term_refs = refs[7 + half :]
    rows = GROUP * slots
    scale = 1.0 / math.sqrt(HD)
    for number in range(KVH):
        key_tile, value_tile, query_tile, upstream_tile = tiles(
            pair_refs, (own_ref, other_ref), number, slots
        )
        prob_grad = lax.dot_general(
            value_tile,
            upstream_tile,
            (((1,), (1,)), ((), ())),
            preferred_element_type=jnp.float32,
        )
        gated = grown_ref[number] * coef_ref[number : number + 1, :]
        inner = coef_ref[KVH + number : KVH + number + 1, :]
        score_grad = (gated * (prob_grad - inner) * scale).astype(jnp.bfloat16)
        key_term = jnp.dot(score_grad, query_tile, preferred_element_type=jnp.float32)
        value_term = jnp.dot(
            gated.astype(jnp.bfloat16), upstream_tile, preferred_element_type=jnp.float32
        )
        key_rows, value_rows = rows_of(number, slots), rows_of(KVH + number, slots)
        term_own[key_rows, :] = key_term[0:slots]
        term_own[value_rows, :] = value_term[0:slots]
        for at, ref in enumerate(term_refs, 1):
            ref[key_rows, :] = key_term[rows_of(at, slots)].astype(jnp.bfloat16)
            ref[value_rows, :] = value_term[rows_of(at, slots)].astype(jnp.bfloat16)
        query_term = lax.dot_general(
            score_grad, key_tile, (((0,), (0,)), ((), ())), preferred_element_type=jnp.float32
        )
        query_out[rows_of(number, rows), :] = query_term[0:rows]
        query_send[rows_of(number, rows), :] = query_term[rows:].astype(jnp.bfloat16)


def ride_kernel(groups, *refs):
    count = (len(refs) - groups - 2) // 2
    term_refs = refs[groups : groups + count]
    router_out, send_out = refs[groups + count : groups + count + 2]
    router = refs[0][...]
    for ref in refs[1:groups]:
        router += ref[...].astype(jnp.float32)
    router_out[...] = router
    narrow = router.astype(jnp.bfloat16)
    send_out[...] = narrow
    for term, out in zip(term_refs, refs[groups + count + 2 :]):
        out[0 : term.shape[0], :] = term[...]
        out[term.shape[0] :, :] = narrow


def query_kernel(trig_ref, own_ref, other_ref, far_ref, term_ref, query_out, trig_out, term_out):
    slots = query_out.shape[0]
    cosine = trig_ref[0:slots, :]
    sine = trig_ref[slots : 2 * slots, :]
    trig_out[...] = trig_ref[...]
    term_out[...] = term_ref[...] + far_ref[...].astype(jnp.float32)
    for number in range(HQ):
        part = rows_of(number, slots)
        total = own_ref[part, :] + other_ref[part, :].astype(jnp.float32)
        query_out[:, head(number)] = turn(total, cosine, -sine).astype(jnp.bfloat16)


def final_kernel(router_scale, *refs):
    trig_ref, own_ref, router_ref, alone_ref = refs[:4]
    term_refs = refs[4:-3]
    key_out, value_out, router_out = refs[-3:]
    slots = key_out.shape[0]
    cosine = trig_ref[0:slots, :]
    sine = trig_ref[slots : 2 * slots, :]
    for number in range(2 * KVH):
        part = rows_of(number, slots)
        total = own_ref[part, :]
        for ref in term_refs:
            total += ref[part, :].astype(jnp.float32)
        if number < KVH:
            key_out[:, head(number)] = turn(total, cosine, -sine).astype(jnp.bfloat16)
        else:
            value_out[:, head(number - KVH)] = total.astype(jnp.bfloat16)
    router = router_ref[...] + alone_ref[...].astype(jnp.float32)
    for ref in term_refs:
        router += ref[2 * KVH * slots :, :].astype(jnp.float32)
    router_out[...] = router * router_scale


def call(kernel, outs, args, fetched=(), scratch=(), cost=None):
    local = pl.BlockSpec(memory_space=pltpu.VMEM)
    distant = pl.BlockSpec(memory_space=pl.ANY)
    scratch = list(scratch) + [pltpu.SemaphoreType.DMA((len(fetched),))] * bool(fetched)
    return pl.pallas_call(
        kernel,
        out_shape=outs,
        in_specs=[local] * len(args) + [distant] * len(fetched),
        out_specs=[local] * len(outs),
        scratch_shapes=scratch,
        compiler_params=pltpu.CompilerParams(vmem_limit_bytes=VMEM_LIMIT),
        cost_estimate=cost and pl.CostEstimate(cost, 0, 0),
    )(*args, *[pltpu.with_memory_space_constraint(array, pltpu.HBM) for array in fetched])


def exchange(array, axis, step, size):
    return lax.ppermute(array, axis, [(at, at ^ step) for at in range(size)])


def shards(queries, keys, values, out_grad, routed_inputs, router_weight, positions):
    slots = queries.shape[1]
    width = routed_inputs.shape[2]
    count = lax.axis_size("ctx")
    groups = lax.axis_size("dp")
    half = count // 2
    rows = GROUP * slots
    lines = width // HD
    bf16, f32 = jnp.bfloat16, jnp.float32

    def swap(array):
        return exchange(array, "ctx", 1, count)

    near = pltpu.VMEM
    fetched = [positions, jnp.asarray(rope_table()), keys[0], values[0], queries[0], out_grad[0]]
    pair, query, trig = call(
        prepare_kernel,
        [
            near((2 * KVH * slots, HD), bf16),
            near((2 * HQ * slots, HD), bf16),
            near((2 * slots, HD), f32),
        ],
        [],
        fetched,
        [near(array.shape, array.dtype) for array in fetched],
    )
    query_other = swap(query)
    pairs = [pair] + [
        exchange(pair, "ctx", 2 * step, count) for step in range(1, half)
    ]
    gate, inputs, bias = call(
        gate_kernel,
        [
            near((8, rows), f32),
            near((slots, width), bf16),
            near((half * slots, 2 * rows), f32),
        ],
        [],
        [router_weight.reshape(lines, HD), routed_inputs[0]],
        [near((lines, HD), f32)],
    )
    inputs_other = swap(routed_inputs[0])
    grown, stats = call(
        functools.partial(scores_kernel, slots),
        [
            near((KVH, half * slots, 2 * rows), f32),
            near((4 * KVH, 2 * rows), f32),
        ],
        [gate, bias, query, query_other, *pairs],
        cost=SCORES_COST,
    )
    coef, router, router_send = call(
        combine_kernel,
        [near((2 * KVH, 2 * rows), f32), near((lines, HD), f32), near((lines, HD), bf16)],
        [stats, swap(stats), inputs, inputs_other],
    )
    routers = [router] + [exchange(router_send, "dp", step, groups) for step in range(1, groups)]
    query_own, query_send, term_own, *terms = call(
        functools.partial(terms_kernel, slots, half),
        [
            near((HQ * slots, HD), f32),
            near((HQ * slots, HD), bf16),
            near((2 * KVH * slots, HD), f32),
        ]
        + [near((2 * KVH * slots, HD), bf16)] * (half - 1),
        [coef, grown, query, query_other, *pairs],
        cost=TERMS_COST,
    )
    query_back = swap(query_send)
    early = half // 2
    far = exchange(terms[early - 1], "ctx", 2 * early, count)
    others = [step for step in reversed(range(1, half)) if step != early]
    router, router_send, *terms = call(
        functools.partial(ride_kernel, groups),
        [near((lines, HD), f32), near((lines, HD), bf16)]
        + [near((2 * KVH * slots + lines, HD), bf16)] * len(others),
        [*routers, *[terms[step - 1] for step in others]],
        cost=RIDE_COST,
    )
    terms = [exchange(term, "ctx", 2 * step, count) for step, term in zip(others, terms)]
    alone = exchange(router_send, "ctx", 2 * early, count)
    shape = jax.ShapeDtypeStruct
    query_grad, trig, term_own = call(
        query_kernel,
        [
            shape((slots, HQ * HD), bf16),
            near((2 * slots, HD), f32),
            near((2 * KVH * slots, HD), f32),
        ],
        [trig, query_own, query_back, far, term_own],
        cost=QUERY_COST,
    )
    key_grad, value_grad, router_grad = call(
        functools.partial(final_kernel, 1.0 / math.sqrt(groups * count * slots)),
        [shape((slots, KVH * HD), bf16), shape((slots, KVH * HD), bf16), shape((lines, HD), f32)],
        [trig, term_own, router, alone, *terms],
    )
    return (query_grad[None], key_grad[None], value_grad[None], router_grad.reshape(width))


def solution(mesh):
    in_specs = (
        P("dp", "ctx", None),
        P("dp", "ctx", None),
        P("dp", "ctx", None),
        P("dp", "ctx", None),
        P("dp", "ctx", None),
        P(),
        P("dp", "ctx"),
    )
    out_specs = (P("dp", "ctx", None), P("dp", "ctx", None), P("dp", "ctx", None), P())
    return jax.shard_map(shards, mesh=mesh, in_specs=in_specs, out_specs=out_specs, check_vma=False)
```

```python
import functools
import math

import jax
import jax.numpy as jnp
import numpy as np
from jax import lax
from jax.experimental import pallas as pl
from jax.experimental.pallas import tpu as pltpu
from jax.sharding import PartitionSpec as P

HQ = 16
KVH = 4
HD = 128
GROUP = HQ // KVH
ROPE_BASE = 500000.0
NEG_LARGE = -1e30
VMEM_LIMIT = 32 * 1024 * 1024
SCORES_COST = 20 * 10**9
TERMS_COST = 20 * 10**9
RIDE_COST = 20 * 10**9
QUERY_COST = 5 * 10**8
QUERY_TERMS_COST = 1


def rope_table():
    half = HD // 2
    frequency = [ROPE_BASE ** (-number / half) for number in range(half)]
    coarse = [256.0 * factor % (2.0 * math.pi) for factor in frequency]
    return np.asarray([coarse + coarse, frequency + frequency], np.float32)


def turn(vectors, cosine, sine):
    return vectors * cosine + pltpu.roll(vectors, HD // 2, 1) * sine


def head(number):
    return slice(number * HD, (number + 1) * HD)


def rows_of(number, depth):
    return slice(number * depth, (number + 1) * depth)


def diagonal(slots, lanes):
    row = lax.broadcasted_iota(jnp.int32, (slots, lanes), 0)
    lane = lax.broadcasted_iota(jnp.int32, (slots, lanes), 1)
    return lax.rem(lane, slots) == row


def prepare_kernel(*refs):
    place_hbm, table_hbm, key_hbm, value_hbm, query_hbm, upstream_hbm = refs[:6]
    pair_ref, query_out, trig_ref = refs[6:9]
    place_ref, table_ref, key_ref, value_ref, query_ref, upstream_ref, semaphores = refs[9:]
    slots = key_ref.shape[0]
    copies = [
        pltpu.make_async_copy(source, target, semaphores.at[at])
        for at, (source, target) in enumerate(
            [
                (place_hbm, place_ref),
                (table_hbm, table_ref),
                (key_hbm, key_ref),
                (value_hbm, value_ref),
                (query_hbm, query_ref),
                (upstream_hbm, upstream_ref),
            ]
        )
    ]
    for copy in copies:
        copy.start()
    copies[0].wait()
    place = place_ref[...]
    upper = (place >> 8).astype(jnp.float32)
    lower = (place & 255).astype(jnp.float32)
    same = diagonal(slots, slots)
    upper = jnp.sum(jnp.where(same, upper, 0.0), axis=1, keepdims=True)
    lower = jnp.sum(jnp.where(same, lower, 0.0), axis=1, keepdims=True)
    copies[1].wait()
    angles = upper * table_ref[0:1, :] + lower * table_ref[1:2, :]
    low = lax.broadcasted_iota(jnp.int32, angles.shape, 1) < HD // 2
    mixed = jnp.cos(jnp.where(low, angles, angles - 0.5 * math.pi))
    turned = pltpu.roll(mixed, HD // 2, 1)
    cosine = jnp.where(low, mixed, turned)
    sine = jnp.where(low, -turned, mixed)
    trig_ref[0:slots, :] = cosine
    trig_ref[slots : 2 * slots, :] = sine
    for copy in copies[2:]:
        copy.wait()
    for number in range(KVH):
        wide = key_ref[:, head(number)].astype(jnp.float32)
        pair_ref[rows_of(number, slots), :] = turn(wide, cosine, sine).astype(jnp.bfloat16)
        pair_ref[rows_of(KVH + number, slots), :] = value_ref[:, head(number)]
    for number in range(HQ):
        wide = query_ref[:, head(number)].astype(jnp.float32)
        query_out[rows_of(number, slots), :] = turn(wide, cosine, sine).astype(jnp.bfloat16)
        query_out[rows_of(HQ + number, slots), :] = upstream_ref[:, head(number)]


def gate_kernel(weight_hbm, input_hbm, gate_ref, input_ref, weight_ref, semaphores):
    copies = [
        pltpu.make_async_copy(weight_hbm, weight_ref, semaphores.at[0]),
        pltpu.make_async_copy(input_hbm, input_ref, semaphores.at[1]),
    ]
    for copy in copies:
        copy.start()
    for copy in copies:
        copy.wait()
    slots = input_ref.shape[0]
    blocks = weight_ref.shape[0]
    total = jnp.zeros((slots, HD), jnp.float32)
    for number in range(blocks):
        total += input_ref[:, head(number)].astype(jnp.float32) * weight_ref[number : number + 1, :]
    gate = jax.nn.sigmoid(jnp.sum(total, axis=1, keepdims=True))
    same = diagonal(slots, gate_ref.shape[1])
    gate_ref[...] = jnp.broadcast_to(
        jnp.sum(jnp.where(same, gate, 0.0), axis=0, keepdims=True), gate_ref.shape
    )


def tiles(pair_refs, query_refs, number, slots):
    rows = GROUP * slots
    key_tile = jnp.concatenate([ref[rows_of(number, slots), :] for ref in pair_refs], axis=0)
    value_tile = jnp.concatenate(
        [ref[rows_of(KVH + number, slots), :] for ref in pair_refs], axis=0
    )
    query_tile = jnp.concatenate([ref[rows_of(number, rows), :] for ref in query_refs], axis=0)
    upstream_tile = jnp.concatenate(
        [ref[rows_of(KVH + number, rows), :] for ref in query_refs], axis=0
    )
    return key_tile, value_tile, query_tile, upstream_tile


def scores_kernel(slots, *refs):
    gate_ref, own_ref, other_ref = refs[:3]
    pair_refs = refs[3:-3]
    grown_out, grad_out, stats_out = refs[-3:]
    rows = GROUP * slots
    keys_total = len(pair_refs) * slots
    own = lax.axis_index("ctx")
    other = own + 1 - 2 * lax.rem(own, 2)
    row = lax.broadcasted_iota(jnp.int32, (keys_total, 2 * rows), 0)
    lane = lax.broadcasted_iota(jnp.int32, (keys_total, 2 * rows), 1)
    owner = 2 * jnp.bitwise_xor(own // 2, row // slots) + lax.rem(own, 2)
    key_at = owner * slots + lax.rem(row, slots)
    query_at = lax.rem(lane, slots) + jnp.where(lane < rows, own, other) * slots
    bias = jnp.where(key_at <= query_at, 0.0, NEG_LARGE)
    across = (((1,), (1,)), ((), ()))
    for number in range(KVH):
        key_tile, value_tile, query_tile, upstream_tile = tiles(
            pair_refs, (own_ref, other_ref), number, slots
        )
        scores = lax.dot_general(
            key_tile, query_tile, across, preferred_element_type=jnp.float32
        )
        scores = scores * (1.0 / math.sqrt(HD)) + bias
        top = jnp.max(scores, axis=0, keepdims=True)
        grown = jnp.exp(scores - top)
        prob_grad = lax.dot_general(
            value_tile, upstream_tile, across, preferred_element_type=jnp.float32
        )
        grown_out[number] = grown
        grad_out[number] = prob_grad
        stats_out[number : number + 1, :] = top
        stats_out[KVH + number : KVH + number + 1, :] = jnp.sum(grown, axis=0, keepdims=True)
        stats_out[2 * KVH + number : 2 * KVH + number + 1, :] = jnp.sum(
            grown * prob_grad, axis=0, keepdims=True
        )
    stats_out[3 * KVH :, :] = jnp.concatenate(
        [gate_ref[0:KVH, :], jnp.zeros((KVH, rows), jnp.float32)], axis=1
    )


def combine_kernel(own_ref, other_ref, input_ref, input_other_ref, coef_out, router_out):
    slots = input_ref.shape[0]
    rows = GROUP * slots
    mine = own_ref[...]
    swapped = other_ref[...]
    theirs = jnp.concatenate([swapped[:, rows:], swapped[:, :rows]], axis=1)
    top = jnp.maximum(mine[0:KVH], theirs[0:KVH])
    mine_part = jnp.exp(mine[0:KVH] - top)
    their_part = jnp.exp(theirs[0:KVH] - top)
    mass = mine[KVH : 2 * KVH] * mine_part + theirs[KVH : 2 * KVH] * their_part
    inverse = 1.0 / mass
    inner = (
        mine[2 * KVH : 3 * KVH] * mine_part + theirs[2 * KVH : 3 * KVH] * their_part
    ) * inverse
    gate = mine[3 * KVH :] + theirs[3 * KVH :]
    coef_out[0:KVH, :] = mine_part * inverse * gate
    coef_out[KVH : 2 * KVH, :] = inner
    slope = gate[0:1] * (1.0 - gate[0:1]) * jnp.sum(inner, axis=0, keepdims=True)
    same = diagonal(slots, rows)
    own_slope = jnp.sum(jnp.where(same, slope[:, :rows], 0.0), axis=1, keepdims=True)
    other_slope = jnp.sum(jnp.where(same, slope[:, rows:], 0.0), axis=1, keepdims=True)
    for number in range(router_out.shape[0]):
        router_out[number : number + 1, :] = jnp.sum(
            own_slope * input_ref[:, head(number)].astype(jnp.float32)
            + other_slope * input_other_ref[:, head(number)].astype(jnp.float32),
            axis=0,
            keepdims=True,
        )


def terms_kernel(slots, half, *refs):
    coef_ref, grown_ref, grad_ref, own_ref, other_ref = refs[:5]
    pair_refs = refs[5 : 5 + half]
    score_out, term_own = refs[5 + half : 7 + half]
    term_refs = refs[7 + half :]
    rows = GROUP * slots
    scale = 1.0 / math.sqrt(HD)
    for number in range(KVH):
        key_tile, _, query_tile, upstream_tile = tiles(
            pair_refs, (own_ref, other_ref), number, slots
        )
        gated = grown_ref[number] * coef_ref[number : number + 1, :]
        inner = coef_ref[KVH + number : KVH + number + 1, :]
        score_grad = (gated * (grad_ref[number] - inner) * scale).astype(jnp.bfloat16)
        score_out[number] = score_grad
        key_term = jnp.dot(score_grad, query_tile, preferred_element_type=jnp.float32)
        value_term = jnp.dot(
            gated.astype(jnp.bfloat16), upstream_tile, preferred_element_type=jnp.float32
        )
        key_rows, value_rows = rows_of(number, slots), rows_of(KVH + number, slots)
        term_own[key_rows, :] = key_term[0:slots]
        term_own[value_rows, :] = value_term[0:slots]
        for at, ref in enumerate(term_refs, 1):
            ref[key_rows, :] = key_term[rows_of(at, slots)].astype(jnp.bfloat16)
            ref[value_rows, :] = value_term[rows_of(at, slots)].astype(jnp.bfloat16)


def query_terms_kernel(score_ref, *refs):
    pair_refs = refs[:-2]
    query_out, query_send = refs[-2:]
    slots = pair_refs[0].shape[0] // (2 * KVH)
    rows = GROUP * slots
    for number in range(KVH):
        key_tile = jnp.concatenate([ref[rows_of(number, slots), :] for ref in pair_refs], axis=0)
        query_term = lax.dot_general(
            score_ref[number],
            key_tile,
            (((0,), (0,)), ((), ())),
            preferred_element_type=jnp.float32,
        )
        query_out[rows_of(number, rows), :] = query_term[0:rows]
        query_send[rows_of(number, rows), :] = query_term[rows:].astype(jnp.bfloat16)


def ride_kernel(groups, *refs):
    count = (len(refs) - groups - 2) // 2
    term_refs = refs[groups : groups + count]
    router_out, send_out = refs[groups + count : groups + count + 2]
    router = refs[0][...]
    for ref in refs[1:groups]:
        router += ref[...]
    router_out[...] = router
    narrow = router.astype(jnp.bfloat16)
    send_out[...] = narrow
    for term, out in zip(term_refs, refs[groups + count + 2 :]):
        out[0 : term.shape[0], :] = term[...]
        out[term.shape[0] :, :] = narrow


def query_kernel(trig_ref, own_ref, other_ref, far_ref, term_ref, query_out, trig_out, term_out):
    slots = query_out.shape[0]
    cosine = trig_ref[0:slots, :]
    sine = trig_ref[slots : 2 * slots, :]
    trig_out[...] = trig_ref[...]
    term_out[...] = term_ref[...] + far_ref[...].astype(jnp.float32)
    for number in range(HQ):
        part = rows_of(number, slots)
        total = own_ref[part, :] + other_ref[part, :].astype(jnp.float32)
        query_out[:, head(number)] = turn(total, cosine, -sine).astype(jnp.bfloat16)


def final_kernel(router_scale, *refs):
    trig_ref, own_ref, router_ref, alone_ref = refs[:4]
    term_refs = refs[4:-3]
    key_out, value_out, router_out = refs[-3:]
    slots = key_out.shape[0]
    cosine = trig_ref[0:slots, :]
    sine = trig_ref[slots : 2 * slots, :]
    for number in range(2 * KVH):
        part = rows_of(number, slots)
        total = own_ref[part, :]
        for ref in term_refs:
            total += ref[part, :].astype(jnp.float32)
        if number < KVH:
            key_out[:, head(number)] = turn(total, cosine, -sine).astype(jnp.bfloat16)
        else:
            value_out[:, head(number - KVH)] = total.astype(jnp.bfloat16)
    router = router_ref[...] + alone_ref[...].astype(jnp.float32)
    for ref in term_refs:
        router += ref[2 * KVH * slots :, :].astype(jnp.float32)
    router_out[...] = router * router_scale


def call(kernel, outs, args, fetched=(), scratch=(), cost=None):
    local = pl.BlockSpec(memory_space=pltpu.VMEM)
    distant = pl.BlockSpec(memory_space=pl.ANY)
    scratch = list(scratch) + [pltpu.SemaphoreType.DMA((len(fetched),))] * bool(fetched)
    return pl.pallas_call(
        kernel,
        out_shape=outs,
        in_specs=[local] * len(args) + [distant] * len(fetched),
        out_specs=[local] * len(outs),
        scratch_shapes=scratch,
        compiler_params=pltpu.CompilerParams(vmem_limit_bytes=VMEM_LIMIT),
        cost_estimate=cost and pl.CostEstimate(cost, 0, 0),
    )(*args, *[pltpu.with_memory_space_constraint(array, pltpu.HBM) for array in fetched])


def exchange(array, axis, step, size):
    return lax.ppermute(array, axis, [(at, at ^ step) for at in range(size)])


def shards(queries, keys, values, out_grad, routed_inputs, router_weight, positions):
    slots = queries.shape[1]
    width = routed_inputs.shape[2]
    count = lax.axis_size("ctx")
    groups = lax.axis_size("dp")
    half = count // 2
    rows = GROUP * slots
    lines = width // HD
    bf16, f32 = jnp.bfloat16, jnp.float32

    def swap(array):
        return exchange(array, "ctx", 1, count)

    near = pltpu.VMEM
    fetched = [positions, jnp.asarray(rope_table()), keys[0], values[0], queries[0], out_grad[0]]
    pair, query, trig = call(
        prepare_kernel,
        [
            near((2 * KVH * slots, HD), bf16),
            near((2 * HQ * slots, HD), bf16),
            near((2 * slots, HD), f32),
        ],
        [],
        fetched,
        [near(array.shape, array.dtype) for array in fetched],
    )
    query_other = swap(query)
    pairs = [pair] + [
        exchange(pair, "ctx", 2 * step, count) for step in range(1, half)
    ]
    gate, inputs = call(
        gate_kernel,
        [near((8, rows), f32), near((slots, width), bf16)],
        [],
        [router_weight.reshape(lines, HD), routed_inputs[0]],
        [near((lines, HD), f32)],
    )
    inputs_other = swap(routed_inputs[0])
    grown, grad, stats = call(
        functools.partial(scores_kernel, slots),
        [
            near((KVH, half * slots, 2 * rows), f32),
            near((KVH, half * slots, 2 * rows), f32),
            near((4 * KVH, 2 * rows), f32),
        ],
        [gate, query, query_other, *pairs],
        cost=SCORES_COST,
    )
    coef, router = call(
        combine_kernel,
        [near((2 * KVH, 2 * rows), f32), near((lines, HD), f32)],
        [stats, swap(stats), inputs, inputs_other],
    )
    routers = [router] + [
        exchange(router, "dp", step, groups) for step in range(1, groups)
    ]
    score_grad, term_own, *terms = call(
        functools.partial(terms_kernel, slots, half),
        [near((KVH, half * slots, 2 * rows), bf16), near((2 * KVH * slots, HD), f32)]
        + [near((2 * KVH * slots, HD), bf16)] * (half - 1),
        [coef, grown, grad, query, query_other, *pairs],
        cost=TERMS_COST,
    )
    query_own, query_send = call(
        query_terms_kernel,
        [near((HQ * slots, HD), f32), near((HQ * slots, HD), bf16)],
        [score_grad, *pairs],
        cost=QUERY_TERMS_COST,
    )
    query_back = swap(query_send)
    early = half // 2
    far = exchange(terms[early - 1], "ctx", 2 * early, count)
    others = [step for step in reversed(range(1, half)) if step != early]
    router, router_send, *terms = call(
        functools.partial(ride_kernel, groups),
        [near((lines, HD), f32), near((lines, HD), bf16)]
        + [near((2 * KVH * slots + lines, HD), bf16)] * len(others),
        [*routers, *[terms[step - 1] for step in others]],
        cost=RIDE_COST,
    )
    terms = [exchange(term, "ctx", 2 * step, count) for step, term in zip(others, terms)]
    alone = exchange(router_send, "ctx", 2 * early, count)
    shape = jax.ShapeDtypeStruct
    query_grad, trig, term_own = call(
        query_kernel,
        [
            shape((slots, HQ * HD), bf16),
            near((2 * slots, HD), f32),
            near((2 * KVH * slots, HD), f32),
        ],
        [trig, query_own, query_back, far, term_own],
        cost=QUERY_COST,
    )
    key_grad, value_grad, router_grad = call(
        functools.partial(final_kernel, 1.0 / math.sqrt(groups * count * slots)),
        [shape((slots, KVH * HD), bf16), shape((slots, KVH * HD), bf16), shape((lines, HD), f32)],
        [trig, term_own, router, alone, *terms],
    )
    return (query_grad[None], key_grad[None], value_grad[None], router_grad.reshape(width))


def solution(mesh):
    in_specs = (
        P("dp", "ctx", None),
        P("dp", "ctx", None),
        P("dp", "ctx", None),
        P("dp", "ctx", None),
        P("dp", "ctx", None),
        P(),
        P("dp", "ctx"),
    )
    out_specs = (P("dp", "ctx", None), P("dp", "ctx", None), P("dp", "ctx", None), P())
    return jax.shard_map(shards, mesh=mesh, in_specs=in_specs, out_specs=out_specs, check_vma=False)
```

```python
import functools
import math

import jax
import jax.numpy as jnp
import numpy as np
from jax import lax
from jax.experimental import pallas as pl
from jax.experimental.pallas import tpu as pltpu
from jax.sharding import PartitionSpec as P

HQ = 16
KVH = 4
HD = 128
GROUP = HQ // KVH
ROPE_BASE = 500000.0
NEG_LARGE = -1e30
VMEM_LIMIT = 32 * 1024 * 1024
SCORES_COST = 20 * 10**9
TERMS_COST = 20 * 10**9
RIDE_COST = 20 * 10**9
QUERY_COST = 5 * 10**8
QUERY_TERMS_COST = 1


def rope_table():
    half = HD // 2
    frequency = [ROPE_BASE ** (-number / half) for number in range(half)]
    coarse = [256.0 * factor % (2.0 * math.pi) for factor in frequency]
    return np.asarray([coarse + coarse, frequency + frequency], np.float32)


def turn(vectors, cosine, sine):
    return vectors * cosine + pltpu.roll(vectors, HD // 2, 1) * sine


def head(number):
    return slice(number * HD, (number + 1) * HD)


def rows_of(number, depth):
    return slice(number * depth, (number + 1) * depth)


def diagonal(slots, lanes):
    row = lax.broadcasted_iota(jnp.int32, (slots, lanes), 0)
    lane = lax.broadcasted_iota(jnp.int32, (slots, lanes), 1)
    return lax.rem(lane, slots) == row


def prepare_kernel(*refs):
    place_hbm, table_hbm, key_hbm, value_hbm, query_hbm, upstream_hbm = refs[:6]
    pair_ref, query_out, trig_ref = refs[6:9]
    place_ref, table_ref, key_ref, value_ref, query_ref, upstream_ref, semaphores = refs[9:]
    slots = key_ref.shape[0]
    copies = [
        pltpu.make_async_copy(source, target, semaphores.at[at])
        for at, (source, target) in enumerate(
            [
                (place_hbm, place_ref),
                (table_hbm, table_ref),
                (key_hbm, key_ref),
                (value_hbm, value_ref),
                (query_hbm, query_ref),
                (upstream_hbm, upstream_ref),
            ]
        )
    ]
    for copy in copies:
        copy.start()
    copies[0].wait()
    place = place_ref[...]
    upper = (place >> 8).astype(jnp.float32)
    lower = (place & 255).astype(jnp.float32)
    same = diagonal(slots, slots)
    upper = jnp.sum(jnp.where(same, upper, 0.0), axis=1, keepdims=True)
    lower = jnp.sum(jnp.where(same, lower, 0.0), axis=1, keepdims=True)
    copies[1].wait()
    angles = upper * table_ref[0:1, :] + lower * table_ref[1:2, :]
    low = lax.broadcasted_iota(jnp.int32, angles.shape, 1) < HD // 2
    mixed = jnp.cos(jnp.where(low, angles, angles - 0.5 * math.pi))
    turned = pltpu.roll(mixed, HD // 2, 1)
    cosine = jnp.where(low, mixed, turned)
    sine = jnp.where(low, -turned, mixed)
    trig_ref[0:slots, :] = cosine
    trig_ref[slots : 2 * slots, :] = sine
    for copy in copies[2:]:
        copy.wait()
    for number in range(KVH):
        wide = key_ref[:, head(number)].astype(jnp.float32)
        pair_ref[rows_of(number, slots), :] = turn(wide, cosine, sine).astype(jnp.bfloat16)
        pair_ref[rows_of(KVH + number, slots), :] = value_ref[:, head(number)]
    for number in range(HQ):
        wide = query_ref[:, head(number)].astype(jnp.float32)
        query_out[rows_of(number, slots), :] = turn(wide, cosine, sine).astype(jnp.bfloat16)
        query_out[rows_of(HQ + number, slots), :] = upstream_ref[:, head(number)]


def gate_kernel(weight_hbm, input_hbm, gate_ref, input_ref, weight_ref, semaphores):
    copies = [
        pltpu.make_async_copy(weight_hbm, weight_ref, semaphores.at[0]),
        pltpu.make_async_copy(input_hbm, input_ref, semaphores.at[1]),
    ]
    for copy in copies:
        copy.start()
    for copy in copies:
        copy.wait()
    slots = input_ref.shape[0]
    blocks = weight_ref.shape[0]
    total = jnp.zeros((slots, HD), jnp.float32)
    for number in range(blocks):
        total += input_ref[:, head(number)].astype(jnp.float32) * weight_ref[number : number + 1, :]
    gate = jax.nn.sigmoid(jnp.sum(total, axis=1, keepdims=True))
    same = diagonal(slots, gate_ref.shape[1])
    gate_ref[...] = jnp.broadcast_to(
        jnp.sum(jnp.where(same, gate, 0.0), axis=0, keepdims=True), gate_ref.shape
    )


def tiles(pair_refs, query_refs, number, slots):
    rows = GROUP * slots
    key_tile = jnp.concatenate([ref[rows_of(number, slots), :] for ref in pair_refs], axis=0)
    value_tile = jnp.concatenate(
        [ref[rows_of(KVH + number, slots), :] for ref in pair_refs], axis=0
    )
    query_tile = jnp.concatenate([ref[rows_of(number, rows), :] for ref in query_refs], axis=0)
    upstream_tile = jnp.concatenate(
        [ref[rows_of(KVH + number, rows), :] for ref in query_refs], axis=0
    )
    return key_tile, value_tile, query_tile, upstream_tile


def scores_kernel(slots, *refs):
    gate_ref, own_ref, other_ref = refs[:3]
    pair_refs = refs[3:-3]
    grown_out, grad_out, stats_out = refs[-3:]
    rows = GROUP * slots
    keys_total = len(pair_refs) * slots
    own = lax.axis_index("ctx")
    other = own + 1 - 2 * lax.rem(own, 2)
    row = lax.broadcasted_iota(jnp.int32, (keys_total, 2 * rows), 0)
    lane = lax.broadcasted_iota(jnp.int32, (keys_total, 2 * rows), 1)
    owner = 2 * jnp.bitwise_xor(own // 2, row // slots) + lax.rem(own, 2)
    key_at = owner * slots + lax.rem(row, slots)
    query_at = lax.rem(lane, slots) + jnp.where(lane < rows, own, other) * slots
    bias = jnp.where(key_at <= query_at, 0.0, NEG_LARGE)
    across = (((1,), (1,)), ((), ()))
    for number in range(KVH):
        key_tile, value_tile, query_tile, upstream_tile = tiles(
            pair_refs, (own_ref, other_ref), number, slots
        )
        scores = lax.dot_general(
            key_tile, query_tile, across, preferred_element_type=jnp.float32
        )
        scores = scores * (1.0 / math.sqrt(HD)) + bias
        top = jnp.max(scores, axis=0, keepdims=True)
        grown = jnp.exp(scores - top)
        prob_grad = lax.dot_general(
            value_tile, upstream_tile, across, preferred_element_type=jnp.float32
        )
        grown_out[number] = grown
        grad_out[number] = prob_grad
        stats_out[number : number + 1, :] = top
        stats_out[KVH + number : KVH + number + 1, :] = jnp.sum(grown, axis=0, keepdims=True)
        stats_out[2 * KVH + number : 2 * KVH + number + 1, :] = jnp.sum(
            grown * prob_grad, axis=0, keepdims=True
        )
    stats_out[3 * KVH :, :] = jnp.concatenate(
        [gate_ref[0:KVH, :], jnp.zeros((KVH, rows), jnp.float32)], axis=1
    )


def combine_kernel(
    own_ref, other_ref, input_ref, input_other_ref, coef_out, router_out, send_out
):
    slots = input_ref.shape[0]
    rows = GROUP * slots
    mine = own_ref[...]
    swapped = other_ref[...]
    theirs = jnp.concatenate([swapped[:, rows:], swapped[:, :rows]], axis=1)
    top = jnp.maximum(mine[0:KVH], theirs[0:KVH])
    mine_part = jnp.exp(mine[0:KVH] - top)
    their_part = jnp.exp(theirs[0:KVH] - top)
    mass = mine[KVH : 2 * KVH] * mine_part + theirs[KVH : 2 * KVH] * their_part
    inverse = 1.0 / mass
    inner = (
        mine[2 * KVH : 3 * KVH] * mine_part + theirs[2 * KVH : 3 * KVH] * their_part
    ) * inverse
    gate = mine[3 * KVH :] + theirs[3 * KVH :]
    coef_out[0:KVH, :] = mine_part * inverse * gate
    coef_out[KVH : 2 * KVH, :] = inner
    slope = gate[0:1] * (1.0 - gate[0:1]) * jnp.sum(inner, axis=0, keepdims=True)
    same = diagonal(slots, rows)
    own_slope = jnp.sum(jnp.where(same, slope[:, :rows], 0.0), axis=1, keepdims=True)
    other_slope = jnp.sum(jnp.where(same, slope[:, rows:], 0.0), axis=1, keepdims=True)
    for number in range(router_out.shape[0]):
        router_out[number : number + 1, :] = jnp.sum(
            own_slope * input_ref[:, head(number)].astype(jnp.float32)
            + other_slope * input_other_ref[:, head(number)].astype(jnp.float32),
            axis=0,
            keepdims=True,
        )
    send_out[...] = router_out[...].astype(jnp.bfloat16)


def terms_kernel(slots, half, *refs):
    coef_ref, grown_ref, grad_ref, own_ref, other_ref = refs[:5]
    pair_refs = refs[5 : 5 + half]
    score_out, term_own = refs[5 + half : 7 + half]
    term_refs = refs[7 + half :]
    rows = GROUP * slots
    scale = 1.0 / math.sqrt(HD)
    for number in range(KVH):
        key_tile, _, query_tile, upstream_tile = tiles(
            pair_refs, (own_ref, other_ref), number, slots
        )
        gated = grown_ref[number] * coef_ref[number : number + 1, :]
        inner = coef_ref[KVH + number : KVH + number + 1, :]
        score_grad = (gated * (grad_ref[number] - inner) * scale).astype(jnp.bfloat16)
        score_out[number] = score_grad
        key_term = jnp.dot(score_grad, query_tile, preferred_element_type=jnp.float32)
        value_term = jnp.dot(
            gated.astype(jnp.bfloat16), upstream_tile, preferred_element_type=jnp.float32
        )
        key_rows, value_rows = rows_of(number, slots), rows_of(KVH + number, slots)
        term_own[key_rows, :] = key_term[0:slots]
        term_own[value_rows, :] = value_term[0:slots]
        for at, ref in enumerate(term_refs, 1):
            ref[key_rows, :] = key_term[rows_of(at, slots)].astype(jnp.bfloat16)
            ref[value_rows, :] = value_term[rows_of(at, slots)].astype(jnp.bfloat16)


def query_terms_kernel(score_ref, *refs):
    pair_refs = refs[:-2]
    query_out, query_send = refs[-2:]
    slots = pair_refs[0].shape[0] // (2 * KVH)
    rows = GROUP * slots
    for number in range(KVH):
        key_tile = jnp.concatenate([ref[rows_of(number, slots), :] for ref in pair_refs], axis=0)
        query_term = lax.dot_general(
            score_ref[number],
            key_tile,
            (((0,), (0,)), ((), ())),
            preferred_element_type=jnp.float32,
        )
        query_out[rows_of(number, rows), :] = query_term[0:rows]
        query_send[rows_of(number, rows), :] = query_term[rows:].astype(jnp.bfloat16)


def ride_kernel(groups, *refs):
    count = (len(refs) - groups - 2) // 2
    term_refs = refs[groups : groups + count]
    router_out, send_out = refs[groups + count : groups + count + 2]
    router = refs[0][...]
    for ref in refs[1:groups]:
        router += ref[...].astype(jnp.float32)
    router_out[...] = router
    narrow = router.astype(jnp.bfloat16)
    send_out[...] = narrow
    for term, out in zip(term_refs, refs[groups + count + 2 :]):
        out[0 : term.shape[0], :] = term[...]
        out[term.shape[0] :, :] = narrow


def query_kernel(trig_ref, own_ref, other_ref, far_ref, term_ref, query_out, trig_out, term_out):
    slots = query_out.shape[0]
    cosine = trig_ref[0:slots, :]
    sine = trig_ref[slots : 2 * slots, :]
    trig_out[...] = trig_ref[...]
    term_out[...] = term_ref[...] + far_ref[...].astype(jnp.float32)
    for number in range(HQ):
        part = rows_of(number, slots)
        total = own_ref[part, :] + other_ref[part, :].astype(jnp.float32)
        query_out[:, head(number)] = turn(total, cosine, -sine).astype(jnp.bfloat16)


def final_kernel(router_scale, *refs):
    trig_ref, own_ref, router_ref, alone_ref = refs[:4]
    term_refs = refs[4:-3]
    key_out, value_out, router_out = refs[-3:]
    slots = key_out.shape[0]
    cosine = trig_ref[0:slots, :]
    sine = trig_ref[slots : 2 * slots, :]
    for number in range(2 * KVH):
        part = rows_of(number, slots)
        total = own_ref[part, :]
        for ref in term_refs:
            total += ref[part, :].astype(jnp.float32)
        if number < KVH:
            key_out[:, head(number)] = turn(total, cosine, -sine).astype(jnp.bfloat16)
        else:
            value_out[:, head(number - KVH)] = total.astype(jnp.bfloat16)
    router = router_ref[...] + alone_ref[...].astype(jnp.float32)
    for ref in term_refs:
        router += ref[2 * KVH * slots :, :].astype(jnp.float32)
    router_out[...] = router * router_scale


def call(kernel, outs, args, fetched=(), scratch=(), cost=None):
    local = pl.BlockSpec(memory_space=pltpu.VMEM)
    distant = pl.BlockSpec(memory_space=pl.ANY)
    scratch = list(scratch) + [pltpu.SemaphoreType.DMA((len(fetched),))] * bool(fetched)
    return pl.pallas_call(
        kernel,
        out_shape=outs,
        in_specs=[local] * len(args) + [distant] * len(fetched),
        out_specs=[local] * len(outs),
        scratch_shapes=scratch,
        compiler_params=pltpu.CompilerParams(vmem_limit_bytes=VMEM_LIMIT),
        cost_estimate=cost and pl.CostEstimate(cost, 0, 0),
    )(*args, *[pltpu.with_memory_space_constraint(array, pltpu.HBM) for array in fetched])


def exchange(array, axis, step, size):
    return lax.ppermute(array, axis, [(at, at ^ step) for at in range(size)])


def shards(queries, keys, values, out_grad, routed_inputs, router_weight, positions):
    slots = queries.shape[1]
    width = routed_inputs.shape[2]
    count = lax.axis_size("ctx")
    groups = lax.axis_size("dp")
    half = count // 2
    rows = GROUP * slots
    lines = width // HD
    bf16, f32 = jnp.bfloat16, jnp.float32

    def swap(array):
        return exchange(array, "ctx", 1, count)

    near = pltpu.VMEM
    fetched = [positions, jnp.asarray(rope_table()), keys[0], values[0], queries[0], out_grad[0]]
    pair, query, trig = call(
        prepare_kernel,
        [
            near((2 * KVH * slots, HD), bf16),
            near((2 * HQ * slots, HD), bf16),
            near((2 * slots, HD), f32),
        ],
        [],
        fetched,
        [near(array.shape, array.dtype) for array in fetched],
    )
    query_other = swap(query)
    pairs = [pair] + [
        exchange(pair, "ctx", 2 * step, count) for step in range(1, half)
    ]
    gate, inputs = call(
        gate_kernel,
        [near((8, rows), f32), near((slots, width), bf16)],
        [],
        [router_weight.reshape(lines, HD), routed_inputs[0]],
        [near((lines, HD), f32)],
    )
    inputs_other = swap(routed_inputs[0])
    grown, grad, stats = call(
        functools.partial(scores_kernel, slots),
        [
            near((KVH, half * slots, 2 * rows), f32),
            near((KVH, half * slots, 2 * rows), f32),
            near((4 * KVH, 2 * rows), f32),
        ],
        [gate, query, query_other, *pairs],
        cost=SCORES_COST,
    )
    coef, router, router_send = call(
        combine_kernel,
        [near((2 * KVH, 2 * rows), f32), near((lines, HD), f32), near((lines, HD), bf16)],
        [stats, swap(stats), inputs, inputs_other],
    )
    routers = [router] + [exchange(router_send, "dp", step, groups) for step in range(1, groups)]
    score_grad, term_own, *terms = call(
        functools.partial(terms_kernel, slots, half),
        [near((KVH, half * slots, 2 * rows), bf16), near((2 * KVH * slots, HD), f32)]
        + [near((2 * KVH * slots, HD), bf16)] * (half - 1),
        [coef, grown, grad, query, query_other, *pairs],
        cost=TERMS_COST,
    )
    query_own, query_send = call(
        query_terms_kernel,
        [near((HQ * slots, HD), f32), near((HQ * slots, HD), bf16)],
        [score_grad, *pairs],
        cost=QUERY_TERMS_COST,
    )
    query_back = swap(query_send)
    early = half // 2
    far = exchange(terms[early - 1], "ctx", 2 * early, count)
    others = [step for step in reversed(range(1, half)) if step != early]
    router, router_send, *terms = call(
        functools.partial(ride_kernel, groups),
        [near((lines, HD), f32), near((lines, HD), bf16)]
        + [near((2 * KVH * slots + lines, HD), bf16)] * len(others),
        [*routers, *[terms[step - 1] for step in others]],
        cost=RIDE_COST,
    )
    terms = [exchange(term, "ctx", 2 * step, count) for step, term in zip(others, terms)]
    alone = exchange(router_send, "ctx", 2 * early, count)
    shape = jax.ShapeDtypeStruct
    query_grad, trig, term_own = call(
        query_kernel,
        [
            shape((slots, HQ * HD), bf16),
            near((2 * slots, HD), f32),
            near((2 * KVH * slots, HD), f32),
        ],
        [trig, query_own, query_back, far, term_own],
        cost=QUERY_COST,
    )
    key_grad, value_grad, router_grad = call(
        functools.partial(final_kernel, 1.0 / math.sqrt(groups * count * slots)),
        [shape((slots, KVH * HD), bf16), shape((slots, KVH * HD), bf16), shape((lines, HD), f32)],
        [trig, term_own, router, alone, *terms],
    )
    return (query_grad[None], key_grad[None], value_grad[None], router_grad.reshape(width))


def solution(mesh):
    in_specs = (
        P("dp", "ctx", None),
        P("dp", "ctx", None),
        P("dp", "ctx", None),
        P("dp", "ctx", None),
        P("dp", "ctx", None),
        P(),
        P("dp", "ctx"),
    )
    out_specs = (P("dp", "ctx", None), P("dp", "ctx", None), P("dp", "ctx", None), P())
    return jax.shard_map(shards, mesh=mesh, in_specs=in_specs, out_specs=out_specs, check_vma=False)
```
